1024 devices in a mesh: gx: 16 (over x, y), gy: 64 (over z, core).
Axes of the slice: x: 4, y: 4, z: 32, core: 2. Of those that a mesh axis runs over, the one named last changes fastest.
Arguments:
- a_tiles: bfloat16 [32, 256, 5, 128, 128], P('gx', 'gy'), may hold values from -0.5 to 0.5
- a_links: int32 [32, 256, 4], P('gx', 'gy'), may hold values 0 or 1
- p_own: bfloat16 [32, 256, 128, 128], P('gx', 'gy'), may hold values from -0.75 to 0.75
- p_side: bfloat16 [32, 64, 2, 128, 128], P('gx', 'gy'), may hold values from -0.75 to 0.75
- p_links: int32 [32, 64, 2], P('gx', 'gy'), may hold values 0 or 1
- coarse_pick: int32 [32, 64], P('gx', 'gy'), may hold values from 0 to 3, as said below
Outputs:
- coarse: float32 [32, 64, 3, 3, 128, 128], P('gx', 'gy')
The draws below stay inside these ranges and needn't reach their ends.
Inputs may be any that keep to these rules, and one draw needn't show every extreme that they name: `coarse_pick`: within each aligned run of 4 entries along the second dimension, the entries are a permutation of 0 to 3.
All inputs are finite; a program needn't handle non-finite values. No bound on the sum of `a_links` or of `p_links` on one device may be relied on, other than what follows from the above.
Results may differ from the reference program's by a relative error of at most 0.0029.
Values may be sent and summed in bfloat16 or wider, within the bound.
No kernel may reach another device: no remote copies, remote signals or barrier semaphores. Data moves between devices by JAX's collectives and lax.ppermute only.
A program may use at most 32 MiB of HBM per device.

```python
import jax
import jax.numpy as jnp
from jax import lax

BLOCK = 128
RATIO = 4
GROUP = 4
NBX = 32
NFY = 256
NCY = 64


def draw_coarse_pick(key, part):
    key = jax.random.fold_in(key, 11)
    sub_keys = jax.random.split(key, NBX * NCY // GROUP)
    orders = jax.vmap(lambda sub_key: jax.random.permutation(sub_key, GROUP))(sub_keys)
    return orders.reshape(NBX, NCY).astype(jnp.int32)


def with_ends(values, own_key, least, high):
    place = [jax.random.randint(jax.random.fold_in(own_key, axis), (), 0, length) for axis, length in enumerate(values.shape)]
    main_axis = values.shape.index(max(values.shape))
    next_to = place[:main_axis] + [(place[main_axis] + 1) % values.shape[main_axis]] + place[main_axis + 1:]
    return values.at[tuple(place)].set(least).at[tuple(next_to)].set(high)


def level_of(key, dims, pieces, smallest, largest):
    def one(dim, parts):
        heights = jax.random.uniform(jax.random.fold_in(jax.random.fold_in(key, 6), dim), (parts,), jnp.float32, smallest / len(pieces), largest / len(pieces))
        return jnp.repeat(jnp.exp(heights), dims[dim] // parts).reshape((-1,) + (1,) * (len(dims) - dim - 1))

    loudness = one(*pieces[0])
    for cut in pieces[1:]:
        loudness = loudness * one(*cut)
    return loudness


def centred(own_key, shape, deviation, most, cuts=(), kind=jnp.bfloat16):
    level = level_of(own_key, shape, cuts, -0.22, 0.18) if cuts else 1.0
    values = jax.random.normal(own_key, shape, jnp.float32) * deviation * level
    return jnp.minimum(jnp.maximum(values, -most), most).astype(kind)


def setup_inputs(seed: int = 0) -> dict:
    streams_of = jax.random.split(jax.random.key(seed), 7)
    return {
        "a_tiles": centred(streams_of[0], (NBX, NFY, 5, BLOCK, BLOCK), BLOCK ** -0.5, 0.5, ((0, 16), (1, 64))),
        "a_links": with_ends((jax.random.randint(streams_of[1], (NBX, NFY, 4), 0, 4) < 3).astype(jnp.int32), jax.random.fold_in(streams_of[1], 1), 0, 1),
        "p_own": centred(streams_of[2], (NBX, NFY, BLOCK, BLOCK), (BLOCK // 2) ** -0.5, 0.75, ((0, 16), (1, 64))),
        "p_side": centred(streams_of[3], (NBX, NCY, 2, BLOCK, BLOCK), (BLOCK // 2) ** -0.5, 0.75, ((0, 16), (1, 64))),
        "p_links": with_ends((jax.random.randint(streams_of[4], (NBX, NCY, 2), 0, 4) < 3).astype(jnp.int32), jax.random.fold_in(streams_of[4], 1), 0, 1),
        "coarse_pick": draw_coarse_pick(jax.random.fold_in(streams_of[6], 71), 0),
    }


def slide_down(blocks, slot_axis):
    head = lax.slice_in_dim(blocks, 1, 3, axis=slot_axis)
    empty = jnp.zeros_like(lax.slice_in_dim(blocks, 0, 1, axis=slot_axis))
    return jnp.concatenate([head, empty], axis=slot_axis)


def slide_up(blocks, slot_axis):
    tail = lax.slice_in_dim(blocks, 0, 2, axis=slot_axis)
    empty = jnp.zeros_like(lax.slice_in_dim(blocks, 0, 1, axis=slot_axis))
    return jnp.concatenate([empty, tail], axis=slot_axis)


def apply_tiles(blocks, panels):
    return jnp.einsum('nab,nsbe->nsae', blocks.astype(jnp.float32), panels.astype(jnp.float32))


def column_interp(p_own, p_side, p_links, column_index):
    column_count = p_own.shape[0]
    inside = (column_index >= 0) & (column_index < column_count)
    clamped = jnp.clip(column_index, 0, column_count - 1).astype(jnp.int32)
    own_tiles = lax.dynamic_index_in_dim(p_own, clamped, 0, keepdims=False)
    side_tiles = lax.dynamic_index_in_dim(p_side, clamped, 0, keepdims=False)
    link_mask = lax.dynamic_index_in_dim(p_links, clamped, 0, keepdims=False)
    coarse_rows = side_tiles.shape[0]
    coarse_index = jnp.arange(coarse_rows)
    keep_low = jnp.where(inside & (coarse_index > 0), link_mask[:, 0], 0).astype(own_tiles.dtype)
    keep_high = jnp.where(inside & (coarse_index < coarse_rows - 1), link_mask[:, 1], 0).astype(own_tiles.dtype)
    own_tiles = own_tiles * inside.astype(own_tiles.dtype)
    own_tiles = own_tiles.reshape(coarse_rows, RATIO, BLOCK, BLOCK)
    low_side = side_tiles[:, 0] * keep_low[:, None, None]
    high_side = side_tiles[:, 1] * keep_high[:, None, None]
    filler = jnp.zeros((coarse_rows, RATIO - 1, BLOCK, BLOCK), own_tiles.dtype)
    low_slot = jnp.concatenate([low_side[:, None], filler], axis=1)
    high_slot = jnp.concatenate([filler, high_side[:, None]], axis=1)
    interp = jnp.stack([low_slot, own_tiles, high_slot], axis=2)
    return interp.reshape(coarse_rows * RATIO, 3, BLOCK, BLOCK)


def reference(a_tiles, a_links, p_own, p_side, p_links, coarse_pick):
    fine_rows = p_own.shape[1]
    coarse_rows = p_side.shape[1]
    fine_index = jnp.arange(fine_rows)

    def column(column_index):
        middle = column_interp(p_own, p_side, p_links, column_index)
        west_panel = column_interp(p_own, p_side, p_links, column_index - 1)
        east_panel = column_interp(p_own, p_side, p_links, column_index + 1)
        operator_tiles = lax.dynamic_index_in_dim(a_tiles, column_index, 0, keepdims=False)
        link_float = lax.dynamic_index_in_dim(a_links, column_index, 0, keepdims=False).astype(jnp.float32)
        link_float = link_float[:, :, None, None, None]
        empty_row = jnp.zeros_like(middle[:1])
        lower_panel = jnp.concatenate([empty_row, middle[:-1]], axis=0)
        lower_panel = jnp.where((fine_index % RATIO == 0)[:, None, None, None], slide_down(lower_panel, 1), lower_panel)
        upper_panel = jnp.concatenate([middle[1:], empty_row], axis=0)
        upper_panel = jnp.where((fine_index % RATIO == RATIO - 1)[:, None, None, None], slide_up(upper_panel, 1), upper_panel)
        centre = apply_tiles(operator_tiles[:, 0], middle)
        centre = centre + link_float[:, 2] * apply_tiles(operator_tiles[:, 3], lower_panel)
        centre = centre + link_float[:, 3] * apply_tiles(operator_tiles[:, 4], upper_panel)
        western = link_float[:, 0] * apply_tiles(operator_tiles[:, 1], west_panel)
        eastern = link_float[:, 1] * apply_tiles(operator_tiles[:, 2], east_panel)
        product = jnp.stack([western, centre, eastern], axis=1).astype(jnp.bfloat16)
        local_terms = jnp.einsum('njrab,njdsae->nrdsbe',
                                 middle.reshape(coarse_rows, RATIO, 3, BLOCK, BLOCK).astype(jnp.float32),
                                 product.reshape(coarse_rows, RATIO, 3, 3, BLOCK, BLOCK).astype(jnp.float32))
        empty_slot = jnp.zeros_like(local_terms[:, 0, :, :1])
        from_upper = jnp.concatenate([empty_slot, local_terms[:, 0, :, :2]], axis=2)
        from_upper = jnp.concatenate([from_upper[1:], jnp.zeros_like(from_upper[:1])], axis=0)
        from_lower = jnp.concatenate([local_terms[:, 2, :, 1:], empty_slot], axis=2)
        from_lower = jnp.concatenate([jnp.zeros_like(from_lower[:1]), from_lower[:-1]], axis=0)
        galerkin = local_terms[:, 1] + from_upper + from_lower
        picks = lax.dynamic_index_in_dim(coarse_pick, column_index, 0, keepdims=False)
        source = ((jnp.arange(coarse_rows, dtype=jnp.int32) // GROUP) * GROUP + picks).astype(jnp.int32)
        return jnp.take(galerkin, source, axis=0)

    return lax.map(column, jnp.arange(p_own.shape[0], dtype=jnp.int32))
```

```python
import jax
import jax.numpy as jnp
from jax import lax
from jax.experimental import pallas as pl
from jax.experimental.pallas import tpu as pltpu
from jax.sharding import PartitionSpec as P

B = 128
PAD = 16
F32 = jnp.float32
BF16 = jnp.bfloat16
SMEM = pl.BlockSpec(memory_space=pltpu.SMEM)
VMEM = pl.BlockSpec(memory_space=pltpu.VMEM)


def call(kernel, in_specs, shapes, *args, vmem=None):
    return pl.pallas_call(
        kernel,
        in_specs=in_specs,
        out_specs=[VMEM] * len(shapes),
        out_shape=[jax.ShapeDtypeStruct(shape, dtype) for shape, dtype in shapes],
        compiler_params=pltpu.CompilerParams(vmem_limit_bytes=32 * 2**20),
    )(*args)


def tile(index):
    return pl.ds(index * B, B)


def pick_rows(first, second):
    rows = lax.broadcasted_iota(jnp.int32, (PAD, B), 0)
    return jnp.where(rows < PAD // 2, first, second)


def pack_kernel(me, links, picks, own, side, east, west, sides, msg_e, msg_o):
    c = me[0]
    core = lax.rem(c, 2)
    keep = [c > 0, c < me[1] - 1]
    for u in range(2):
        for k in range(2):
            factor = jnp.where(keep[k], links[u, 0, k], 0).astype(F32).astype(BF16)
            sides[u, k] = side[u, 0, k] * factor
    for u, message in ((1, east), (0, west)):
        for j in range(4):
            message[j] = own[u, j]
        for k in range(2):
            message[4 + k] = sides[u, k]
    mine = pick_rows(picks[0, 0], picks[1, 0]).astype(F32).astype(BF16)

    def fill(message, up):
        for u in range(2):
            message[tile(2 * u)] = own[u, 3 if up else 0]
            message[tile(2 * u + 1)] = sides[u, 1 if up else 0]
        message[pl.ds(4 * B, PAD)] = mine

    @pl.when(core == 0)
    def _():
        fill(msg_e, True)
        fill(msg_o, False)

    @pl.when(core == 1)
    def _():
        fill(msg_e, False)
        fill(msg_o, True)


def dot(a, b):
    return lax.dot_general(a, b, (((1,), (0,)), ((), ())), preferred_element_type=F32)


def dot_t(a, b):
    return lax.dot_general(a, b, (((0,), (0,)), ((), ())), preferred_element_type=F32)


def cat(parts, axis):
    return jnp.concatenate(parts, axis=axis)


def compute_kernel(me, links, a, own, sides, xw, xe, halo_e, halo_o, row, for_e, for_o):
    core = lax.rem(me[0], 2)
    zero = jnp.zeros((B, B), BF16)
    even = core == 0
    for u in range(2):
        def edge(k):
            from_e, from_o = halo_e[1 - core, tile(2 * u + k)], halo_o[tile(2 * u + k)]
            return jnp.where(even, from_o, from_e), jnp.where(even, from_e, from_o)

        own_down, own_up = edge(0)
        high_down, low_up = edge(1)
        low, high = sides[u, 0], sides[u, 1]
        o = [own[u, j] for j in range(4)]
        west = xw if u == 0 else None
        east = xe if u == 1 else None

        def neighbour(message, other, j, k):
            if message is not None:
                return message[j] if k is None else message[4 + k]
            return own[other, j] if k is None else sides[other, k]

        def weight(j, k, link):
            return a[u, j, k] * links[u, j, link].astype(F32).astype(BF16)

        right = [
            [[low, o[0]], [own_down, high_down], [zero, o[1]]],
            [[zero, o[1]], [low, o[0]], [zero, o[2]]],
            [[o[2], zero], [o[1], zero], [o[3], high]],
            [[o[3], high], [o[2], zero], [low_up, own_up]],
        ]
        centre, western, eastern = [], [], []
        for j in range(4):
            left = cat([a[u, j, 0], weight(j, 3, 2), weight(j, 4, 3)], 1)
            centre.append(dot(left, cat([cat(r, 1) for r in right[j]], 0)).astype(BF16))
            for out, k, link, message in ((western, 1, 0, west), (eastern, 2, 1, east)):
                panel = neighbour(message, 1 - u, j, None)
                if j == 0:
                    panel = cat([neighbour(message, 1 - u, j, 0), panel], 1)
                if j == 3:
                    panel = cat([panel, neighbour(message, 1 - u, j, 1)], 1)
                out.append(dot(weight(j, k, link), panel).astype(BF16))

        def slot(values, j, second):
            return values[j][:, B:] if second else values[j][:, :B]

        middle = [
            cat([western[0][:, B:], slot(centre, 0, True), eastern[0][:, B:]], 1),
            cat([western[1], slot(centre, 1, True), eastern[1]], 1),
            cat([western[2], slot(centre, 2, False), eastern[2]], 1),
            cat([western[3][:, :B], slot(centre, 3, False), eastern[3][:, :B]], 1),
        ]
        first = cat([western[0][:, :B], slot(centre, 0, False), eastern[0][:, :B]], 1)
        last = cat([western[3][:, B:], slot(centre, 3, True), eastern[3][:, B:]], 1)
        result1 = dot_t(cat(o, 0), cat(middle, 0))
        result0 = dot_t(o[0], first)
        result2 = dot_t(o[3], last)
        extra0 = dot_t(o[1], slot(centre, 1, False))
        extra2 = dot_t(o[2], slot(centre, 2, True))
        for d in range(3):
            at = slice(d * B, (d + 1) * B)
            row[u, d, 0] = result0[:, at] + extra0 if d == 1 else result0[:, at]
            row[u, d, 1] = result1[:, at]
            row[u, d, 2] = result2[:, at] + extra2 if d == 1 else result2[:, at]
        down = dot_t(low, cat([first, middle[0]], 1))
        up = dot_t(high, cat([middle[3], last], 1))
        for d in range(3):
            for s in range(2):
                at = slice((s * 3 + d) * B, (s * 3 + d + 1) * B)
                for_e[u, d, s] = jnp.where(even, up[:, at], down[:, at])
                for_o[6 * u + 2 * d + s] = jnp.where(even, down[:, at], up[:, at]).astype(BF16)


def merge_kernel(me, row, for_e, from_o, halo_o, row_out, message):
    core = lax.rem(me[0], 2)
    for u in range(2):
        for d in range(3):
            for t in range(3):
                row_out[u, d, t] = row[u, d, t]
            for s in range(2):
                row_out[u, d, core + s] += from_o[6 * u + 2 * d + s].astype(F32)
            for t in range(3):
                message[tile(15 * u + 3 * d + t)] = row_out[u, d, t].astype(BF16)
            for s in range(2):
                message[tile(15 * u + 9 + 2 * d + s)] = for_e[u, d, s].astype(BF16)
    message[pl.ds(30 * B, PAD)] = halo_o[pl.ds(4 * B, PAD)]


def rows_of_chip(core, row, for_e, message, u, d, t):
    mine = row[u, d, t]
    theirs = message[tile(15 * u + 3 * d + t)].astype(F32)
    if t == 1:
        mine = mine + message[tile(15 * u + 9 + 2 * d + core)].astype(F32)
        theirs = theirs + for_e[u, d, 1 - core]
    else:
        gets = (core == 0) == (t == 2)
        s = 1 if t == 2 else 0
        got = message[tile(15 * u + 9 + 2 * d + s)].astype(F32)
        mine = mine + jnp.where(gets, got, 0.0)
        theirs = theirs + jnp.where(gets, 0.0, for_e[u, d, s])
    return mine, theirs


def choose_kernel(me, picks, row, for_e, message, halo_e, halo_o, out):
    c = me[0]
    core = lax.rem(c, 2)
    position = lax.rem(c, 4)
    chip = position // 2
    outer = jnp.logical_or(position == 0, position == 3)
    tail = pl.ds(4 * B, PAD)
    inferred = 6.0 - pick_rows(picks[0, 0], picks[1, 0]).astype(F32)
    inferred = inferred - halo_e[1 - core, tail].astype(F32) - halo_o[tail].astype(F32)
    wanted = jnp.where(outer, message[pl.ds(30 * B, PAD)].astype(F32), inferred)
    own_code = position.astype(F32)
    other_code = (chip * 2 + 1 - core).astype(F32)
    for u in range(2):
        ask = wanted[u * PAD // 2:u * PAD // 2 + 1]
        use_own = jnp.broadcast_to(ask == own_code, (B, B))
        use_other = jnp.broadcast_to(ask == other_code, (B, B))
        for d in range(3):
            for t in range(3):
                mine, theirs = rows_of_chip(core, row, for_e, message, u, d, t)
                out[9 * u + 3 * d + t] = jnp.where(use_own, mine, jnp.where(use_other, theirs, 0.0)).astype(BF16)


def finish_kernel(me, picks, row, for_e, message, arrived, out):
    c = me[0]
    core = lax.rem(c, 2)
    position = lax.rem(c, 4)
    for u in range(2):
        pick = picks[u, 0]

        @pl.when(pick // 2 == position // 2)
        def _():
            for d in range(3):
                for t in range(3):
                    mine, theirs = rows_of_chip(core, row, for_e, message, u, d, t)
                    out[u, 0, d, t] = jnp.where(pick == position, mine, theirs)

        @pl.when(pick // 2 != position // 2)
        def _():
            for d in range(3):
                for t in range(3):
                    out[u, 0, d, t] = arrived[9 * u + 3 * d + t].astype(F32)


def on_device(a_tiles, a_links, p_own, p_side, p_links, coarse_pick):
    count = lax.axis_size("gy")
    columns = lax.axis_size("gx")
    me = jnp.stack([lax.axis_index("gy").astype(jnp.int32), jnp.int32(count)])
    pairs = [(2 * g, 2 * g + 1) for g in range(count // 2)]
    inside = pairs + [(b, a) for a, b in pairs]
    outside = [(i + 1, i + 2) for i in range(0, count - 2, 2)]
    outside = outside + [(b, a) for a, b in outside]
    across = [(i, i ^ 2) for i in range(count)]
    eastward = [(i, i + 1) for i in range(columns - 1)]
    westward = [(b, a) for a, b in eastward]
    tile_shape = (B, B)

    east, west, sides, msg_e, msg_o = call(
        pack_kernel, [SMEM, SMEM, SMEM, VMEM, VMEM],
        [((6,) + tile_shape, BF16), ((6,) + tile_shape, BF16), ((2, 2) + tile_shape, BF16),
         ((4 * B + PAD, B), BF16), ((4 * B + PAD, B), BF16)],
        me, p_links, coarse_pick, p_own, p_side)
    from_west = lax.ppermute(east, "gx", eastward)
    from_east = lax.ppermute(west, "gx", westward)
    halo_o = lax.ppermute(msg_o, "gy", outside)
    halo_e = lax.all_gather(msg_e, "gy", axis_index_groups=[list(p) for p in pairs])
    row, for_e, for_o = call(
        compute_kernel, [SMEM, SMEM] + [VMEM] * 7,
        [((2, 3, 3) + tile_shape, F32), ((2, 3, 2) + tile_shape, F32), ((12,) + tile_shape, BF16)],
        me, a_links, a_tiles, p_own, sides, from_west, from_east, halo_e, halo_o)
    from_o = lax.ppermute(for_o, "gy", outside)
    row, message = call(
        merge_kernel, [SMEM] + [VMEM] * 4,
        [((2, 3, 3) + tile_shape, F32), ((30 * B + PAD, B), BF16)],
        me, row, for_e, from_o, halo_o)
    message = lax.ppermute(message, "gy", inside)
    (chosen,) = call(
        choose_kernel, [SMEM, SMEM] + [VMEM] * 5, [((18,) + tile_shape, BF16)],
        me, coarse_pick, row, for_e, message, halo_e, halo_o)
    arrived = lax.ppermute(chosen, "gy", across)
    (out,) = call(
        finish_kernel, [SMEM, SMEM] + [VMEM] * 4, [((2, 1, 3, 3) + tile_shape, F32)],
        me, coarse_pick, row, for_e, message, arrived)
    return out


def solution(mesh):
    return jax.shard_map(
        on_device,
        mesh=mesh,
        in_specs=(
            P("gx", "gy", None, None, None),
            P("gx", "gy", None),
            P("gx", "gy", None, None),
            P("gx", "gy", None, None, None),
            P("gx", "gy", None),
            P("gx", "gy"),
        ),
        out_specs=P("gx", "gy", None, None, None, None),
        check_vma=False,
    )
```

```python
import jax
import jax.numpy as jnp
from jax import lax
from jax.experimental import pallas as pl
from jax.experimental.pallas import tpu as pltpu
from jax.sharding import PartitionSpec as P

B = 128
PAD = 16
F32 = jnp.float32
BF16 = jnp.bfloat16
VMEM = pl.BlockSpec(memory_space=pltpu.VMEM)
HBM = pl.BlockSpec(memory_space=pltpu.HBM)

NEAR = ((0, 2), (0, 1), (1, 0), (1, 1))
FAR = ((0, 0), (1, 2))
LINK_TILE = {0: 1, 2: 2}


def call(kernel, args, shapes, in_specs=None, out_specs=None, scratch=(), aliases=None, cost=1):
    return pl.pallas_call(
        kernel,
        in_specs=in_specs or [VMEM] * len(args),
        out_specs=out_specs or [VMEM] * len(shapes),
        out_shape=[jax.ShapeDtypeStruct(shape, dtype) for shape, dtype in shapes],
        scratch_shapes=list(scratch),
        input_output_aliases=aliases or {},
        compiler_params=pltpu.CompilerParams(vmem_limit_bytes=32 * 2**20),
        cost_estimate=pl.CostEstimate(flops=cost * 10**9, bytes_accessed=cost * 10**6, transcendentals=0),
    )(*args)


def tile(index):
    return pl.ds(index * B, B)


def dot(a, b):
    return lax.dot_general(a, b, (((1,), (0,)), ((), ())), preferred_element_type=F32)


def dot_t(a, b):
    return lax.dot_general(a, b, (((0,), (0,)), ((), ())), preferred_element_type=F32)


def cat(parts, axis):
    return jnp.concatenate(parts, axis=axis)


def begin_kernel(a_links, p_links, picks, own_in, side_in, a_in,
                 own, a, sides, east, west, msg_o, msg_e, mine,
                 s_links, s_side, s_picks, raw, sems):
    copies = [
        pltpu.make_async_copy(src, dst, sems.at[i])
        for i, (src, dst) in enumerate(((p_links, s_side), (own_in, own), (side_in, raw), (a_links, s_links),
                                        (picks, s_picks), (a_in, a)))
    ]
    for copy in copies:
        copy.start()
    c = lax.axis_index("gy")
    core = lax.rem(c, 2)
    keep = [c > 0, c < lax.axis_size("gy") - 1]
    for copy in copies[:3]:
        copy.wait()
    for u in range(2):
        for k in range(2):
            factor = jnp.where(keep[k], s_side[u, 0, k], 0).astype(F32).astype(BF16)
            sides[u, k] = raw[u, 0, k] * factor
    for u, message in ((1, east), (0, west)):
        for j in range(4):
            message[j] = own[u, j]
        for k in range(2):
            message[4 + k] = sides[u, k]
    for copy in copies[3:5]:
        copy.wait()
    rows = lax.broadcasted_iota(jnp.int32, (PAD, B), 0)
    codes = jnp.where(rows < PAD // 2, s_picks[0, 0], s_picks[0, 1]).astype(F32)
    mine[...] = codes
    msg_o[pl.ds(14 * B, PAD)] = codes.astype(BF16)
    msg_e[pl.ds(4 * B, PAD)] = codes.astype(BF16)
    copies[5].wait()
    for u in range(2):
        for j in range(4):
            for k in range(4):
                a[u, j, k + 1] = a[u, j, k + 1] * s_links[u, j, k].astype(F32).astype(BF16)

    def fill(j_e, k_e, j_o, k_o):
        for u in range(2):
            msg_e[tile(2 * u)] = own[u, j_e]
            msg_e[tile(2 * u + 1)] = sides[u, k_e]
            side, block = sides[u, k_o], own[u, j_o]
            other_side, other_block = sides[1 - u, k_o], own[1 - u, j_o]
            zero = jnp.zeros((B, B), BF16)
            inner = 1 if j_o == 0 else 2
            if j_o == 0:
                right = cat([cat([side, block], 1), cat([zero, own[u, inner]], 1)], 0)
                left = cat([a[u, j_o, 0], a[u, j_o, 4]], 1)
                beyond = a[u, j_o, 3]
                panel = cat([other_side, other_block], 1)
            else:
                right = cat([cat([block, side], 1), cat([own[u, inner], zero], 1)], 0)
                left = cat([a[u, j_o, 0], a[u, j_o, 3]], 1)
                beyond = a[u, j_o, 4]
                panel = cat([other_block, other_side], 1)
            centre = dot(left, right).astype(BF16)
            beside = dot(a[u, j_o, LINK_TILE[NEAR[2 * u][1]]], panel).astype(BF16)
            result = dot_t(side, cat([centre, beyond, beside], 1)).astype(BF16)
            msg_o[tile(7 * u)] = block
            msg_o[tile(7 * u + 1)] = side
            for i in range(5):
                msg_o[tile(7 * u + 2 + i)] = result[:, i * B:(i + 1) * B]

    @pl.when(core == 0)
    def _():
        fill(3, 1, 0, 0)

    @pl.when(core == 1)
    def _():
        fill(0, 0, 3, 1)


def reduce_units(own, u, products, count):
    firsts, middles, lasts = products
    blocks = cat([own[u, j] for j in range(4)], 0)
    slot1 = dot_t(blocks, cat(middles, 0))
    slot0 = dot_t(own[u, 0], firsts)
    slot2 = dot_t(own[u, 3], lasts)
    return [[value[:, i * B:(i + 1) * B] for i in range(count)] for value in (slot0, slot1, slot2)]


def link_products(a, u, d, tiles, side_tiles):
    k = LINK_TILE[d]
    first = dot(a[u, 0, k], cat([side_tiles[0], tiles[0]], 1)).astype(BF16)
    last = dot(a[u, 3, k], cat([tiles[3], side_tiles[1]], 1)).astype(BF16)
    inner = [dot(a[u, j, k], tiles[j]).astype(BF16) for j in (1, 2)]
    return first[:, :B], [first[:, B:], inner[0], inner[1], last[:, :B]], last[:, B:]


def near_kernel(own, a, sides, halo_e, halo_o, from_west, from_east, row, for_e, message):
    del from_west, from_east
    core = lax.rem(lax.axis_index("gy"), 2)
    even = core == 0
    zero = jnp.zeros((B, B), BF16)
    message[pl.ds(20 * B, PAD)] = halo_o[pl.ds(14 * B, PAD)]
    for u in range(2):
        def edge(k):
            from_e, from_o = halo_e[1 - core, tile(2 * u + k)], halo_o[tile(7 * u + k)]
            return jnp.where(even, from_o, from_e), jnp.where(even, from_e, from_o)

        own_down, own_up = edge(0)
        high_down, low_up = edge(1)
        low, high = sides[u, 0], sides[u, 1]
        o = [own[u, j] for j in range(4)]
        right = [
            [[low, o[0]], [own_down, high_down], [zero, o[1]]],
            [[zero, o[1]], [low, o[0]], [zero, o[2]]],
            [[o[2], zero], [o[1], zero], [o[3], high]],
            [[o[3], high], [o[2], zero], [low_up, own_up]],
        ]
        centre = []
        for j in range(4):
            left = cat([a[u, j, 0], a[u, j, 3], a[u, j, 4]], 1)
            centre.append(dot(left, cat([cat(r, 1) for r in right[j]], 0)).astype(BF16))
        left_part = [value[:, :B] for value in centre]
        right_part = [value[:, B:] for value in centre]
        beside = link_products(a, u, NEAR[2 * u][1], [own[1 - u, j] for j in range(4)],
                               [sides[1 - u, k] for k in range(2)])
        first = cat([beside[0], left_part[0]], 1)
        middle = [cat([beside[1][0], right_part[0]], 1), cat([beside[1][1], right_part[1]], 1),
                  cat([beside[1][2], left_part[2]], 1), cat([beside[1][3], left_part[3]], 1)]
        last = cat([beside[2], right_part[3]], 1)
        slots = reduce_units(own, u, (first, middle, last), 2)
        slots[0][1] = slots[0][1] + dot_t(o[1], left_part[1])
        slots[2][1] = slots[2][1] + dot_t(o[2], right_part[2])
        beyond = dot(halo_o[tile(7 * u + 4)], cat([jnp.where(even, low, o[3]), jnp.where(even, o[0], high)], 1))
        given = dot_t(jnp.where(even, high, low),
                      cat([jnp.where(even, middle[3], first), jnp.where(even, last, middle[0])], 1))
        for i in range(2):
            k = 2 * u + i
            for t in range(3):
                row[k, t] = slots[t][i]
            for s in range(2):
                if i == 0:
                    extra = halo_o[tile(7 * u + 5 + s)].astype(F32)
                else:
                    extra = halo_o[tile(7 * u + 2 + s)].astype(F32) + beyond[:, s * B:(s + 1) * B]
                row[k, core + s] += extra
                part = given[:, (2 * s + i) * B:(2 * s + i + 1) * B]
                for_e[k, s] = part
                message[tile(5 * k + 3 + s)] = part.astype(BF16)
            for t in range(3):
                message[tile(5 * k + t)] = row[k, t].astype(BF16)


def far_kernel(own, a, sides, from_west, from_east, row, for_e, for_o):
    even = lax.rem(lax.axis_index("gy"), 2) == 0
    for k, (u, d) in enumerate(FAR):
        arrived = from_west if d == 0 else from_east
        first, middle, last = link_products(a, u, d, [arrived[j] for j in range(4)], [arrived[4], arrived[5]])
        slots = reduce_units(own, u, (first, middle, last), 1)
        for t in range(3):
            row[k, t] = slots[t][0]
        down = dot_t(sides[u, 0], cat([first, middle[0]], 1))
        up = dot_t(sides[u, 1], cat([middle[3], last], 1))
        to_e, to_o = jnp.where(even, up, down), jnp.where(even, down, up)
        for s in range(2):
            for_e[k, s] = to_e[:, s * B:(s + 1) * B]
            for_o[2 * k + s] = to_o[:, s * B:(s + 1) * B].astype(BF16)


def merge_kernel(row, for_e, from_o, row_out, message):
    core = lax.rem(lax.axis_index("gy"), 2)
    for k in range(len(FAR)):
        for t in range(3):
            row_out[k, t] = row[k, t]
        for s in range(2):
            row_out[k, core + s] += from_o[2 * k + s].astype(F32)
            message[tile(5 * k + 3 + s)] = for_e[k, s].astype(BF16)
        for t in range(3):
            message[tile(5 * k + t)] = row_out[k, t].astype(BF16)


def complete(core, row, for_e, message, k, t):
    mine = row[k, t]
    theirs = message(5 * k + t).astype(F32)
    if t == 1:
        mine = mine + message(5 * k + 3 + core).astype(F32)
        theirs = theirs + for_e[k, 1 - core]
    else:
        gets = (core == 0) == (t == 2)
        s = 1 if t == 2 else 0
        mine = mine + jnp.where(gets, message(5 * k + 3 + s).astype(F32), 0.0)
        theirs = theirs + jnp.where(gets, 0.0, for_e[k, s])
    return mine, theirs


def masks(codes, u, position, core):
    code = codes[u * PAD // 2:u * PAD // 2 + 1]
    other = position + 1 - 2 * core
    return (jnp.broadcast_to(code == position.astype(F32), (B, B)),
            jnp.broadcast_to(code == other.astype(F32), (B, B)))


def choose(units, core, position, codes, row, for_e, message, out):
    for k, (u, _) in enumerate(units):
        use_mine, use_theirs = masks(codes, u, position, core)
        for t in range(3):
            mine, theirs = complete(core, row, for_e, message, k, t)
            out[3 * k + t] = jnp.where(use_mine, mine, jnp.where(use_theirs, theirs, 0.0)).astype(BF16)


def choose_near_kernel(mine, row, for_e, message, halo_e, halo_o, out, wanted):
    c = lax.axis_index("gy")
    core, position = lax.rem(c, 2), lax.rem(c, 4)
    outer = jnp.logical_or(position == 0, position == 3)
    inferred = 6.0 - mine[...] - halo_e[1 - core, pl.ds(4 * B, PAD)].astype(F32)
    inferred = inferred - halo_o[pl.ds(14 * B, PAD)].astype(F32)
    codes = jnp.where(outer, message[pl.ds(20 * B, PAD)].astype(F32), inferred)
    wanted[...] = codes
    choose(NEAR, core, position, codes, row, for_e, lambda i: message[tile(i)], out)


def choose_far_kernel(wanted, row, for_e, message, out):
    c = lax.axis_index("gy")
    core, position = lax.rem(c, 2), lax.rem(c, 4)
    choose(FAR, core, position, wanted[...], row, for_e, lambda i: message[1 - core, tile(i)], out)


def finish(units, core, position, codes, row, for_e, message, arrived, out, buffer, sems):
    copies = []
    for k, (u, d) in enumerate(units):
        use_mine, use_theirs = masks(codes, u, position, core)
        for t in range(3):
            mine, theirs = complete(core, row, for_e, message, k, t)
            far = arrived[3 * k + t].astype(F32)
            buffer[k, t] = jnp.where(use_mine, mine, jnp.where(use_theirs, theirs, far))
        copies.append(pltpu.make_async_copy(buffer.at[k], out.at[u, 0, d], sems.at[k]))
        copies[-1].start()
    for copy in copies:
        copy.wait()


def finish_near_kernel(mine, row, for_e, message, arrived, out, buffer, sems):
    c = lax.axis_index("gy")
    core, position = lax.rem(c, 2), lax.rem(c, 4)
    finish(NEAR, core, position, mine[...], row, for_e, lambda i: message[tile(i)], arrived, out, buffer, sems)


def finish_far_kernel(mine, row, for_e, message, arrived, started, out, buffer, sems):
    del started
    c = lax.axis_index("gy")
    core, position = lax.rem(c, 2), lax.rem(c, 4)
    finish(FAR, core, position, mine[...], row, for_e, lambda i: message[1 - core, tile(i)], arrived, out, buffer, sems)


def on_device(a_tiles, a_links, p_own, p_side, p_links, coarse_pick):
    count, columns = lax.axis_size("gy"), lax.axis_size("gx")
    pairs = [(2 * g, 2 * g + 1) for g in range(count // 2)]
    cores = [list(pair) for pair in pairs]
    inside = pairs + [(b, a) for a, b in pairs]
    outside = [(i + 1, i + 2) for i in range(0, count - 2, 2)]
    outside = outside + [(b, a) for a, b in outside]
    across = [(i, i ^ 2) for i in range(count)]
    eastward = [(i, i + 1) for i in range(columns - 1)]
    westward = [(b, a) for a, b in eastward]
    bb = (B, B)
    near, far = len(NEAR), len(FAR)

    own, a, sides, east, west, msg_o, msg_e, mine = call(
        begin_kernel,
        [pltpu.with_memory_space_constraint(x, pltpu.HBM)
         for x in (a_links, p_links, coarse_pick.T, p_own, p_side, a_tiles)],
        [(p_own.shape, BF16), (a_tiles.shape, BF16), ((2, 2) + bb, BF16), ((6,) + bb, BF16), ((6,) + bb, BF16),
         ((14 * B + PAD, B), BF16), ((4 * B + PAD, B), BF16), ((PAD, B), F32)],
        in_specs=[HBM] * 6,
        scratch=[pltpu.SMEM(a_links.shape, jnp.int32), pltpu.SMEM(p_links.shape, jnp.int32),
                 pltpu.SMEM((1, 2), jnp.int32), pltpu.VMEM(p_side.shape, BF16), pltpu.SemaphoreType.DMA((6,))])
    halo_o = lax.ppermute(msg_o, "gy", outside)
    from_west = lax.ppermute(east, "gx", eastward)
    from_east = lax.ppermute(west, "gx", westward)
    halo_e = lax.all_gather(msg_e, "gy", axis_index_groups=cores)
    row_n, for_e_n, message_n = call(
        near_kernel, (own, a, sides, halo_e, halo_o, from_west, from_east),
        [((near, 3) + bb, F32), ((near, 2) + bb, F32), ((5 * near * B + PAD, B), BF16)])
    message_n = lax.ppermute(message_n, "gy", inside)
    row_f, for_e_f, for_o_f = call(
        far_kernel, (own, a, sides, from_west, from_east),
        [((far, 3) + bb, F32), ((far, 2) + bb, F32), ((2 * far,) + bb, BF16)])
    chosen_n, wanted = call(
        choose_near_kernel, (mine, row_n, for_e_n, message_n, halo_e, halo_o),
        [((3 * near,) + bb, BF16), ((PAD, B), F32)])
    for_o_f, chosen_n = lax.optimization_barrier((for_o_f, chosen_n))
    arrived_n = lax.ppermute(chosen_n, "gy", across)
    from_o_f = lax.ppermute(for_o_f, "gy", outside)
    row_f, message_f = call(
        merge_kernel, (row_f, for_e_f, from_o_f), [((far, 3) + bb, F32), ((5 * far * B, B), BF16)])
    message_f = lax.all_gather(message_f, "gy", axis_index_groups=cores)
    (chosen_f,) = call(choose_far_kernel, (wanted, row_f, for_e_f, message_f), [((3 * far,) + bb, BF16)])
    arrived_f = lax.ppermute(chosen_f, "gy", across)
    shape = (2, 1, 3, 3) + bb
    (out,) = call(
        finish_near_kernel, (mine, row_n, for_e_n, message_n, arrived_n), [(shape, F32)], out_specs=[HBM],
        scratch=[pltpu.VMEM((near, 3) + bb, F32), pltpu.SemaphoreType.DMA((near,))])
    (out,) = call(
        finish_far_kernel, (mine, row_f, for_e_f, message_f, arrived_f, out), [(shape, F32)],
        in_specs=[VMEM] * 5 + [HBM], out_specs=[HBM], aliases={5: 0},
        scratch=[pltpu.VMEM((far, 3) + bb, F32), pltpu.SemaphoreType.DMA((far,))])
    return out


def solution(mesh):
    return jax.shard_map(
        on_device,
        mesh=mesh,
        in_specs=(
            P("gx", "gy", None, None, None),
            P("gx", "gy", None),
            P("gx", "gy", None, None),
            P("gx", "gy", None, None, None),
            P("gx", "gy", None),
            P("gx", "gy"),
        ),
        out_specs=P("gx", "gy", None, None, None, None),
        check_vma=False,
    )
```

```python
import jax
import jax.numpy as jnp
from jax import lax
from jax.experimental import pallas as pl
from jax.experimental.pallas import tpu as pltpu
from jax.sharding import PartitionSpec as P

B = 128
PAD = 16
F32 = jnp.float32
BF16 = jnp.bfloat16
VMEM = pl.BlockSpec(memory_space=pltpu.VMEM)
HBM = pl.BlockSpec(memory_space=pltpu.HBM)

NEAR = ((0, 2), (0, 1), (1, 0), (1, 1))
FAR = ((0, 0), (1, 2))
LINK_TILE = {0: 1, 2: 2}


def call(kernel, args, shapes, in_specs=None, out_specs=None, scratch=(), aliases=None, cost=0):
    return pl.pallas_call(
        kernel,
        in_specs=in_specs or [VMEM] * len(args),
        out_specs=out_specs or [VMEM] * len(shapes),
        out_shape=[jax.ShapeDtypeStruct(shape, dtype) for shape, dtype in shapes],
        scratch_shapes=list(scratch),
        input_output_aliases=aliases or {},
        compiler_params=pltpu.CompilerParams(vmem_limit_bytes=32 * 2**20),
        cost_estimate=pl.CostEstimate(flops=cost, bytes_accessed=cost, transcendentals=0),
    )(*args)


def tile(index):
    return pl.ds(index * B, B)


def dot(a, b):
    return lax.dot_general(a, b, (((1,), (0,)), ((), ())), preferred_element_type=F32)


def dot_t(a, b):
    return lax.dot_general(a, b, (((0,), (0,)), ((), ())), preferred_element_type=F32)


def cat(parts, axis):
    return jnp.concatenate(parts, axis=axis)


def begin_kernel(a_links, p_links, picks, own_in, side_in, a_in,
                 own, a, sides, east, west, msg_o, msg_e, mine,
                 s_links, s_side, s_picks, raw, sems):
    copies = [
        pltpu.make_async_copy(src, dst, sems.at[i])
        for i, (src, dst) in enumerate(((p_links, s_side), (own_in, own), (side_in, raw), (a_links, s_links),
                                        (picks, s_picks), (a_in, a)))
    ]
    for copy in copies:
        copy.start()
    c = lax.axis_index("gy")
    core = lax.rem(c, 2)
    keep = [c > 0, c < lax.axis_size("gy") - 1]
    for copy in copies[:3]:
        copy.wait()
    for u in range(2):
        for k in range(2):
            factor = jnp.where(keep[k], s_side[u, 0, k], 0).astype(F32).astype(BF16)
            sides[u, k] = raw[u, 0, k] * factor
    for u, message in ((1, east), (0, west)):
        for j in range(4):
            message[j] = own[u, j]
        for k in range(2):
            message[4 + k] = sides[u, k]
    for copy in copies[3:5]:
        copy.wait()
    rows = lax.broadcasted_iota(jnp.int32, (PAD, B), 0)
    codes = jnp.where(rows < PAD // 2, s_picks[0, 0], s_picks[0, 1]).astype(F32)
    mine[...] = codes
    msg_o[pl.ds(14 * B, PAD)] = codes.astype(BF16)
    msg_e[pl.ds(4 * B, PAD)] = codes.astype(BF16)
    copies[5].wait()
    for u in range(2):
        for j in range(4):
            for k in range(4):
                a[u, j, k + 1] = a[u, j, k + 1] * s_links[u, j, k].astype(F32).astype(BF16)

    def fill(j_e, k_e, j_o, k_o):
        for u in range(2):
            msg_e[tile(2 * u)] = own[u, j_e]
            msg_e[tile(2 * u + 1)] = sides[u, k_e]
            side, block = sides[u, k_o], own[u, j_o]
            other_side, other_block = sides[1 - u, k_o], own[1 - u, j_o]
            zero = jnp.zeros((B, B), BF16)
            inner = 1 if j_o == 0 else 2
            if j_o == 0:
                right = cat([cat([side, block], 1), cat([zero, own[u, inner]], 1)], 0)
                left = cat([a[u, j_o, 0], a[u, j_o, 4]], 1)
                beyond = a[u, j_o, 3]
                panel = cat([other_side, other_block], 1)
            else:
                right = cat([cat([block, side], 1), cat([own[u, inner], zero], 1)], 0)
                left = cat([a[u, j_o, 0], a[u, j_o, 3]], 1)
                beyond = a[u, j_o, 4]
                panel = cat([other_block, other_side], 1)
            centre = dot(left, right).astype(BF16)
            beside = dot(a[u, j_o, LINK_TILE[NEAR[2 * u][1]]], panel).astype(BF16)
            result = dot_t(side, cat([centre, beyond, beside], 1)).astype(BF16)
            msg_o[tile(7 * u)] = block
            msg_o[tile(7 * u + 1)] = side
            for i in range(5):
                msg_o[tile(7 * u + 2 + i)] = result[:, i * B:(i + 1) * B]

    @pl.when(core == 0)
    def _():
        fill(3, 1, 0, 0)

    @pl.when(core == 1)
    def _():
        fill(0, 0, 3, 1)


def reduce_units(own, u, products, count):
    firsts, middles, lasts = products
    blocks = cat([own[u, j] for j in range(4)], 0)
    slot1 = dot_t(blocks, cat(middles, 0))
    slot0 = dot_t(own[u, 0], firsts)
    slot2 = dot_t(own[u, 3], lasts)
    return [[value[:, i * B:(i + 1) * B] for i in range(count)] for value in (slot0, slot1, slot2)]


def link_products(a, u, d, tiles, side_tiles):
    k = LINK_TILE[d]
    first = dot(a[u, 0, k], cat([side_tiles[0], tiles[0]], 1)).astype(BF16)
    last = dot(a[u, 3, k], cat([tiles[3], side_tiles[1]], 1)).astype(BF16)
    inner = [dot(a[u, j, k], tiles[j]).astype(BF16) for j in (1, 2)]
    return first[:, :B], [first[:, B:], inner[0], inner[1], last[:, :B]], last[:, B:]


def near_kernel(own, a, sides, halo_e, halo_o, row, for_e, message):
    core = lax.rem(lax.axis_index("gy"), 2)
    even = core == 0
    zero = jnp.zeros((B, B), BF16)
    message[pl.ds(20 * B, PAD)] = halo_o[pl.ds(14 * B, PAD)]
    for u in range(2):
        def edge(k):
            from_e, from_o = halo_e[1 - core, tile(2 * u + k)], halo_o[tile(7 * u + k)]
            return jnp.where(even, from_o, from_e), jnp.where(even, from_e, from_o)

        own_down, own_up = edge(0)
        high_down, low_up = edge(1)
        low, high = sides[u, 0], sides[u, 1]
        o = [own[u, j] for j in range(4)]
        right = [
            [[low, o[0]], [own_down, high_down], [zero, o[1]]],
            [[zero, o[1]], [low, o[0]], [zero, o[2]]],
            [[o[2], zero], [o[1], zero], [o[3], high]],
            [[o[3], high], [o[2], zero], [low_up, own_up]],
        ]
        centre = []
        for j in range(4):
            left = cat([a[u, j, 0], a[u, j, 3], a[u, j, 4]], 1)
            centre.append(dot(left, cat([cat(r, 1) for r in right[j]], 0)).astype(BF16))
        left_part = [value[:, :B] for value in centre]
        right_part = [value[:, B:] for value in centre]
        beside = link_products(a, u, NEAR[2 * u][1], [own[1 - u, j] for j in range(4)],
                               [sides[1 - u, k] for k in range(2)])
        first = cat([beside[0], left_part[0]], 1)
        middle = [cat([beside[1][0], right_part[0]], 1), cat([beside[1][1], right_part[1]], 1),
                  cat([beside[1][2], left_part[2]], 1), cat([beside[1][3], left_part[3]], 1)]
        last = cat([beside[2], right_part[3]], 1)
        slots = reduce_units(own, u, (first, middle, last), 2)
        slots[0][1] = slots[0][1] + dot_t(o[1], left_part[1])
        slots[2][1] = slots[2][1] + dot_t(o[2], right_part[2])
        beyond = dot(halo_o[tile(7 * u + 4)], cat([jnp.where(even, low, o[3]), jnp.where(even, o[0], high)], 1))
        given = dot_t(jnp.where(even, high, low),
                      cat([jnp.where(even, middle[3], first), jnp.where(even, last, middle[0])], 1))
        for i in range(2):
            k = 2 * u + i
            for t in range(3):
                row[k, t] = slots[t][i]
            for s in range(2):
                if i == 0:
                    extra = halo_o[tile(7 * u + 5 + s)].astype(F32)
                else:
                    extra = halo_o[tile(7 * u + 2 + s)].astype(F32) + beyond[:, s * B:(s + 1) * B]
                row[k, core + s] += extra
                part = given[:, (2 * s + i) * B:(2 * s + i + 1) * B]
                for_e[k, s] = part
                message[tile(5 * k + 3 + s)] = part.astype(BF16)
            for t in range(3):
                message[tile(5 * k + t)] = row[k, t].astype(BF16)


def far_kernel(own, a, sides, from_west, from_east, row, for_e, for_o):
    even = lax.rem(lax.axis_index("gy"), 2) == 0
    for k, (u, d) in enumerate(FAR):
        arrived = from_west if d == 0 else from_east
        first, middle, last = link_products(a, u, d, [arrived[j] for j in range(4)], [arrived[4], arrived[5]])
        slots = reduce_units(own, u, (first, middle, last), 1)
        for t in range(3):
            row[k, t] = slots[t][0]
        down = dot_t(sides[u, 0], cat([first, middle[0]], 1))
        up = dot_t(sides[u, 1], cat([middle[3], last], 1))
        to_e, to_o = jnp.where(even, up, down), jnp.where(even, down, up)
        for s in range(2):
            for_e[k, s] = to_e[:, s * B:(s + 1) * B]
            for_o[2 * k + s] = to_o[:, s * B:(s + 1) * B].astype(BF16)


def merge_kernel(row, for_e, from_o, row_out, message):
    core = lax.rem(lax.axis_index("gy"), 2)
    for k in range(len(FAR)):
        for t in range(3):
            row_out[k, t] = row[k, t]
        for s in range(2):
            row_out[k, core + s] += from_o[2 * k + s].astype(F32)
            message[tile(5 * k + 3 + s)] = for_e[k, s].astype(BF16)
        for t in range(3):
            message[tile(5 * k + t)] = row_out[k, t].astype(BF16)


def complete(core, row, for_e, message, k, t):
    mine = row[k, t]
    theirs = message(5 * k + t).astype(F32)
    if t == 1:
        mine = mine + message(5 * k + 3 + core).astype(F32)
        theirs = theirs + for_e[k, 1 - core]
    else:
        gets = (core == 0) == (t == 2)
        s = 1 if t == 2 else 0
        mine = mine + jnp.where(gets, message(5 * k + 3 + s).astype(F32), 0.0)
        theirs = theirs + jnp.where(gets, 0.0, for_e[k, s])
    return mine, theirs


def masks(codes, u, position, core):
    code = codes[u * PAD // 2:u * PAD // 2 + 1]
    other = position + 1 - 2 * core
    return (jnp.broadcast_to(code == position.astype(F32), (B, B)),
            jnp.broadcast_to(code == other.astype(F32), (B, B)))


def choose(units, core, position, codes, row, for_e, message, out):
    for k, (u, _) in enumerate(units):
        use_mine, use_theirs = masks(codes, u, position, core)
        for t in range(3):
            mine, theirs = complete(core, row, for_e, message, k, t)
            out[3 * k + t] = jnp.where(use_mine, mine, jnp.where(use_theirs, theirs, 0.0)).astype(BF16)


def choose_near_kernel(mine, row, for_e, message, halo_e, halo_o, out, wanted):
    c = lax.axis_index("gy")
    core, position = lax.rem(c, 2), lax.rem(c, 4)
    outer = jnp.logical_or(position == 0, position == 3)
    inferred = 6.0 - mine[...] - halo_e[1 - core, pl.ds(4 * B, PAD)].astype(F32)
    inferred = inferred - halo_o[pl.ds(14 * B, PAD)].astype(F32)
    codes = jnp.where(outer, message[pl.ds(20 * B, PAD)].astype(F32), inferred)
    wanted[...] = codes
    choose(NEAR, core, position, codes, row, for_e, lambda i: message[tile(i)], out)


def choose_far_kernel(wanted, row, for_e, message, out):
    c = lax.axis_index("gy")
    core, position = lax.rem(c, 2), lax.rem(c, 4)
    choose(FAR, core, position, wanted[...], row, for_e, lambda i: message[1 - core, tile(i)], out)


def finish(units, core, position, codes, row, for_e, message, arrived, out, buffer, sems):
    copies = []
    for k, (u, d) in enumerate(units):
        use_mine, use_theirs = masks(codes, u, position, core)
        for t in range(3):
            mine, theirs = complete(core, row, for_e, message, k, t)
            far = arrived[3 * k + t].astype(F32)
            buffer[k, t] = jnp.where(use_mine, mine, jnp.where(use_theirs, theirs, far))
        copies.append(pltpu.make_async_copy(buffer.at[k], out.at[u, 0, d], sems.at[k]))
        copies[-1].start()
    for copy in copies:
        copy.wait()


def finish_near_kernel(mine, row, for_e, message, arrived, out, buffer, sems):
    c = lax.axis_index("gy")
    core, position = lax.rem(c, 2), lax.rem(c, 4)
    finish(NEAR, core, position, mine[...], row, for_e, lambda i: message[tile(i)], arrived, out, buffer, sems)


def finish_far_kernel(mine, row, for_e, message, arrived, started, out, buffer, sems):
    del started
    c = lax.axis_index("gy")
    core, position = lax.rem(c, 2), lax.rem(c, 4)
    finish(FAR, core, position, mine[...], row, for_e, lambda i: message[1 - core, tile(i)], arrived, out, buffer, sems)


def on_device(a_tiles, a_links, p_own, p_side, p_links, coarse_pick):
    count, columns = lax.axis_size("gy"), lax.axis_size("gx")
    pairs = [(2 * g, 2 * g + 1) for g in range(count // 2)]
    cores = [list(pair) for pair in pairs]
    inside = pairs + [(b, a) for a, b in pairs]
    outside = [(i + 1, i + 2) for i in range(0, count - 2, 2)]
    outside = outside + [(b, a) for a, b in outside]
    across = [(i, i ^ 2) for i in range(count)]
    eastward = [(i, i + 1) for i in range(columns - 1)]
    westward = [(b, a) for a, b in eastward]
    bb = (B, B)
    near, far = len(NEAR), len(FAR)

    own, a, sides, east, west, msg_o, msg_e, mine = call(
        begin_kernel,
        [pltpu.with_memory_space_constraint(x, pltpu.HBM)
         for x in (a_links, p_links, coarse_pick.T, p_own, p_side, a_tiles)],
        [(p_own.shape, BF16), (a_tiles.shape, BF16), ((2, 2) + bb, BF16), ((6,) + bb, BF16), ((6,) + bb, BF16),
         ((14 * B + PAD, B), BF16), ((4 * B + PAD, B), BF16), ((PAD, B), F32)],
        in_specs=[HBM] * 6,
        scratch=[pltpu.SMEM(a_links.shape, jnp.int32), pltpu.SMEM(p_links.shape, jnp.int32),
                 pltpu.SMEM((1, 2), jnp.int32), pltpu.VMEM(p_side.shape, BF16), pltpu.SemaphoreType.DMA((6,))])
    halo_o = lax.ppermute(msg_o, "gy", outside)
    from_west = lax.ppermute(east, "gx", eastward)
    from_east = lax.ppermute(west, "gx", westward)
    halo_e = lax.all_gather(msg_e, "gy", axis_index_groups=cores)
    row_n, for_e_n, message_n = call(
        near_kernel, (own, a, sides, halo_e, halo_o),
        [((near, 3) + bb, F32), ((near, 2) + bb, F32), ((5 * near * B + PAD, B), BF16)])
    message_n, from_west, from_east = lax.optimization_barrier((message_n, from_west, from_east))
    message_n = lax.ppermute(message_n, "gy", inside)
    row_f, for_e_f, for_o_f = call(
        far_kernel, (own, a, sides, from_west, from_east),
        [((far, 3) + bb, F32), ((far, 2) + bb, F32), ((2 * far,) + bb, BF16)])
    chosen_n, wanted = call(
        choose_near_kernel, (mine, row_n, for_e_n, message_n, halo_e, halo_o),
        [((3 * near,) + bb, BF16), ((PAD, B), F32)])
    arrived_n = lax.ppermute(chosen_n, "gy", across)
    from_o_f = lax.ppermute(for_o_f, "gy", outside)
    row_f, message_f = call(
        merge_kernel, (row_f, for_e_f, from_o_f), [((far, 3) + bb, F32), ((5 * far * B, B), BF16)])
    message_f = lax.all_gather(message_f, "gy", axis_index_groups=cores)
    (chosen_f,) = call(choose_far_kernel, (wanted, row_f, for_e_f, message_f), [((3 * far,) + bb, BF16)])
    arrived_f = lax.ppermute(chosen_f, "gy", across)
    shape = (2, 1, 3, 3) + bb
    (out,) = call(
        finish_near_kernel, (mine, row_n, for_e_n, message_n, arrived_n), [(shape, F32)], out_specs=[HBM],
        scratch=[pltpu.VMEM((near, 3) + bb, F32), pltpu.SemaphoreType.DMA((near,))])
    (out,) = call(
        finish_far_kernel, (mine, row_f, for_e_f, message_f, arrived_f, out), [(shape, F32)],
        in_specs=[VMEM] * 5 + [HBM], out_specs=[HBM], aliases={5: 0},
        scratch=[pltpu.VMEM((far, 3) + bb, F32), pltpu.SemaphoreType.DMA((far,))])
    return out


def solution(mesh):
    return jax.shard_map(
        on_device,
        mesh=mesh,
        in_specs=(
            P("gx", "gy", None, None, None),
            P("gx", "gy", None),
            P("gx", "gy", None, None),
            P("gx", "gy", None, None, None),
            P("gx", "gy", None),
            P("gx", "gy"),
        ),
        out_specs=P("gx", "gy", None, None, None, None),
        check_vma=False,
    )
```

```python
import jax
import jax.numpy as jnp
from jax import lax
from jax.experimental import pallas as pl
from jax.experimental.pallas import tpu as pltpu
from jax.sharding import PartitionSpec as P

B = 128
PAD = 16
F32 = jnp.float32
BF16 = jnp.bfloat16
VMEM = pl.BlockSpec(memory_space=pltpu.VMEM)
HBM = pl.BlockSpec(memory_space=pltpu.HBM)

NEAR = ((0, 2), (0, 1), (1, 0), (1, 1))
FAR = ((0, 0), (1, 2))
LINK_TILE = {0: 1, 2: 2}


def call(kernel, args, shapes, in_specs=None, out_specs=None, scratch=(), aliases=None, cost=0):
    return pl.pallas_call(
        kernel,
        in_specs=in_specs or [VMEM] * len(args),
        out_specs=out_specs or [VMEM] * len(shapes),
        out_shape=[jax.ShapeDtypeStruct(shape, dtype) for shape, dtype in shapes],
        scratch_shapes=list(scratch),
        input_output_aliases=aliases or {},
        compiler_params=pltpu.CompilerParams(vmem_limit_bytes=32 * 2**20),
        cost_estimate=pl.CostEstimate(flops=cost, bytes_accessed=cost, transcendentals=0),
    )(*args)


def tile(index):
    return pl.ds(index * B, B)


def dot(a, b):
    return lax.dot_general(a, b, (((1,), (0,)), ((), ())), preferred_element_type=F32)


def dot_t(a, b):
    return lax.dot_general(a, b, (((0,), (0,)), ((), ())), preferred_element_type=F32)


def cat(parts, axis):
    return jnp.concatenate(parts, axis=axis)


def begin_kernel(a_links, p_links, picks, own_in, side_in, a_in,
                 own, a, sides, east, west, msg_o, msg_e, mine,
                 s_links, s_side, s_picks, raw, sems):
    copies = [
        pltpu.make_async_copy(src, dst, sems.at[i])
        for i, (src, dst) in enumerate(((p_links, s_side), (own_in, own), (side_in, raw), (a_links, s_links),
                                        (picks, s_picks), (a_in, a)))
    ]
    for copy in copies:
        copy.start()
    c = lax.axis_index("gy")
    core = lax.rem(c, 2)
    keep = [c > 0, c < lax.axis_size("gy") - 1]
    for copy in copies[:3]:
        copy.wait()
    for u in range(2):
        for k in range(2):
            factor = jnp.where(keep[k], s_side[u, 0, k], 0).astype(F32).astype(BF16)
            sides[u, k] = raw[u, 0, k] * factor
    for u, message in ((1, east), (0, west)):
        for j in range(4):
            message[j] = own[u, j]
        for k in range(2):
            message[4 + k] = sides[u, k]
    for copy in copies[3:5]:
        copy.wait()
    rows = lax.broadcasted_iota(jnp.int32, (PAD, B), 0)
    codes = jnp.where(rows < PAD // 2, s_picks[0, 0], s_picks[0, 1]).astype(F32)
    mine[...] = codes
    msg_o[pl.ds(14 * B, PAD)] = codes.astype(BF16)
    msg_e[pl.ds(4 * B, PAD)] = codes.astype(BF16)
    copies[5].wait()
    for u in range(2):
        for j in range(4):
            for k in range(4):
                a[u, j, k + 1] = a[u, j, k + 1] * s_links[u, j, k].astype(F32).astype(BF16)

    def fill_e(j, k):
        for u in range(2):
            msg_e[tile(2 * u)] = own[u, j]
            msg_e[tile(2 * u + 1)] = sides[u, k]

    def fill_o(j_o, k_o):
        for u in range(2):
            side, block = sides[u, k_o], own[u, j_o]
            other_side, other_block = sides[1 - u, k_o], own[1 - u, j_o]
            zero = jnp.zeros((B, B), BF16)
            inner = 1 if j_o == 0 else 2
            if j_o == 0:
                right = cat([cat([side, block], 1), cat([zero, own[u, inner]], 1)], 0)
                left = cat([a[u, j_o, 0], a[u, j_o, 4]], 1)
                beyond = a[u, j_o, 3]
                panel = cat([other_side, other_block], 1)
            else:
                right = cat([cat([block, side], 1), cat([own[u, inner], zero], 1)], 0)
                left = cat([a[u, j_o, 0], a[u, j_o, 3]], 1)
                beyond = a[u, j_o, 4]
                panel = cat([other_block, other_side], 1)
            centre = dot(left, right).astype(BF16)
            beside = dot(a[u, j_o, LINK_TILE[NEAR[2 * u][1]]], panel).astype(BF16)
            result = dot_t(side, cat([centre, beyond, beside], 1)).astype(BF16)
            msg_o[tile(7 * u)] = block
            msg_o[tile(7 * u + 1)] = side
            for i in range(5):
                msg_o[tile(7 * u + 2 + i)] = result[:, i * B:(i + 1) * B]

    pl.when(core == 0)(lambda: fill_e(3, 1))
    pl.when(core == 1)(lambda: fill_e(0, 0))
    pl.when(jnp.logical_and(core == 0, keep[0]))(lambda: fill_o(0, 0))
    pl.when(jnp.logical_and(core == 1, keep[1]))(lambda: fill_o(3, 1))


def reduce_units(own, u, products, count):
    firsts, middles, lasts = products
    blocks = cat([own[u, j] for j in range(4)], 0)
    slot1 = dot_t(blocks, cat(middles, 0))
    slot0 = dot_t(own[u, 0], firsts)
    slot2 = dot_t(own[u, 3], lasts)
    return [[value[:, i * B:(i + 1) * B] for i in range(count)] for value in (slot0, slot1, slot2)]


def link_products(a, u, d, tiles, side_tiles):
    k = LINK_TILE[d]
    first = dot(a[u, 0, k], cat([side_tiles[0], tiles[0]], 1)).astype(BF16)
    last = dot(a[u, 3, k], cat([tiles[3], side_tiles[1]], 1)).astype(BF16)
    inner = [dot(a[u, j, k], tiles[j]).astype(BF16) for j in (1, 2)]
    return first[:, :B], [first[:, B:], inner[0], inner[1], last[:, :B]], last[:, B:]


def near_kernel(own, a, sides, halo_e, halo_o, row, for_e, message):
    core = lax.rem(lax.axis_index("gy"), 2)
    even = core == 0
    zero = jnp.zeros((B, B), BF16)
    message[pl.ds(20 * B, PAD)] = halo_o[pl.ds(14 * B, PAD)]
    for u in range(2):
        def edge(k):
            from_e, from_o = halo_e[1 - core, tile(2 * u + k)], halo_o[tile(7 * u + k)]
            return jnp.where(even, from_o, from_e), jnp.where(even, from_e, from_o)

        own_down, own_up = edge(0)
        high_down, low_up = edge(1)
        low, high = sides[u, 0], sides[u, 1]
        o = [own[u, j] for j in range(4)]
        right = [
            [[low, o[0]], [own_down, high_down], [zero, o[1]]],
            [[zero, o[1]], [low, o[0]], [zero, o[2]]],
            [[o[2], zero], [o[1], zero], [o[3], high]],
            [[o[3], high], [o[2], zero], [low_up, own_up]],
        ]
        centre = []
        for j in range(4):
            left = cat([a[u, j, 0], a[u, j, 3], a[u, j, 4]], 1)
            centre.append(dot(left, cat([cat(r, 1) for r in right[j]], 0)).astype(BF16))
        left_part = [value[:, :B] for value in centre]
        right_part = [value[:, B:] for value in centre]
        beside = link_products(a, u, NEAR[2 * u][1], [own[1 - u, j] for j in range(4)],
                               [sides[1 - u, k] for k in range(2)])
        first = cat([beside[0], left_part[0]], 1)
        middle = [cat([beside[1][0], right_part[0]], 1), cat([beside[1][1], right_part[1]], 1),
                  cat([beside[1][2], left_part[2]], 1), cat([beside[1][3], left_part[3]], 1)]
        last = cat([beside[2], right_part[3]], 1)
        slots = reduce_units(own, u, (first, middle, last), 2)
        slots[0][1] = slots[0][1] + dot_t(o[1], left_part[1])
        slots[2][1] = slots[2][1] + dot_t(o[2], right_part[2])
        beyond = dot(halo_o[tile(7 * u + 4)], cat([jnp.where(even, low, o[3]), jnp.where(even, o[0], high)], 1))
        given = dot_t(jnp.where(even, high, low),
                      cat([jnp.where(even, middle[3], first), jnp.where(even, last, middle[0])], 1))
        for i in range(2):
            k = 2 * u + i
            for t in range(3):
                row[k, t] = slots[t][i]
            for s in range(2):
                if i == 0:
                    extra = halo_o[tile(7 * u + 5 + s)].astype(F32)
                else:
                    extra = halo_o[tile(7 * u + 2 + s)].astype(F32) + beyond[:, s * B:(s + 1) * B]
                row[k, core + s] += extra
                part = given[:, (2 * s + i) * B:(2 * s + i + 1) * B]
                for_e[k, s] = part
                message[tile(5 * k + 3 + s)] = part.astype(BF16)
            for t in range(3):
                message[tile(5 * k + t)] = row[k, t].astype(BF16)


def far_kernel(own, a, sides, from_west, from_east, row, for_e, for_o):
    even = lax.rem(lax.axis_index("gy"), 2) == 0
    for k, (u, d) in enumerate(FAR):
        arrived = from_west if d == 0 else from_east
        first, middle, last = link_products(a, u, d, [arrived[j] for j in range(4)], [arrived[4], arrived[5]])
        slots = reduce_units(own, u, (first, middle, last), 1)
        for t in range(3):
            row[k, t] = slots[t][0]
        down = dot_t(sides[u, 0], cat([first, middle[0]], 1))
        up = dot_t(sides[u, 1], cat([middle[3], last], 1))
        to_e, to_o = jnp.where(even, up, down), jnp.where(even, down, up)
        for s in range(2):
            for_e[k, s] = to_e[:, s * B:(s + 1) * B]
            for_o[2 * k + s] = to_o[:, s * B:(s + 1) * B].astype(BF16)


def merge_kernel(row, for_e, from_o, row_out, message):
    core = lax.rem(lax.axis_index("gy"), 2)
    for k in range(len(FAR)):
        for t in range(3):
            row_out[k, t] = row[k, t]
        for s in range(2):
            row_out[k, core + s] += from_o[2 * k + s].astype(F32)
            message[tile(5 * k + 3 + s)] = for_e[k, s].astype(BF16)
        for t in range(3):
            message[tile(5 * k + t)] = row_out[k, t].astype(BF16)


def complete(core, row, for_e, message, k, t):
    mine = row[k, t]
    theirs = message(5 * k + t).astype(F32)
    if t == 1:
        mine = mine + message(5 * k + 3 + core).astype(F32)
        theirs = theirs + for_e[k, 1 - core]
    else:
        gets = (core == 0) == (t == 2)
        s = 1 if t == 2 else 0
        mine = mine + jnp.where(gets, message(5 * k + 3 + s).astype(F32), 0.0)
        theirs = theirs + jnp.where(gets, 0.0, for_e[k, s])
    return mine, theirs


def masks(codes, u, position, core):
    code = codes[u * PAD // 2:u * PAD // 2 + 1]
    other = position + 1 - 2 * core
    return (jnp.broadcast_to(code == position.astype(F32), (B, B)),
            jnp.broadcast_to(code == other.astype(F32), (B, B)))


def choose(units, core, position, codes, row, for_e, message, out):
    for k, (u, _) in enumerate(units):
        use_mine, use_theirs = masks(codes, u, position, core)
        for t in range(3):
            mine, theirs = complete(core, row, for_e, message, k, t)
            out[3 * k + t] = jnp.where(use_mine, mine, jnp.where(use_theirs, theirs, 0.0)).astype(BF16)


def choose_near_kernel(mine, row, for_e, message, halo_e, halo_o, row_far, out, wanted):
    del row_far
    c = lax.axis_index("gy")
    core, position = lax.rem(c, 2), lax.rem(c, 4)
    outer = jnp.logical_or(position == 0, position == 3)
    inferred = 6.0 - mine[...] - halo_e[1 - core, pl.ds(4 * B, PAD)].astype(F32)
    inferred = inferred - halo_o[pl.ds(14 * B, PAD)].astype(F32)
    codes = jnp.where(outer, message[pl.ds(20 * B, PAD)].astype(F32), inferred)
    wanted[...] = codes
    choose(NEAR, core, position, codes, row, for_e, lambda i: message[tile(i)], out)


def choose_far_kernel(wanted, row, for_e, message, out):
    c = lax.axis_index("gy")
    core, position = lax.rem(c, 2), lax.rem(c, 4)
    choose(FAR, core, position, wanted[...], row, for_e, lambda i: message[1 - core, tile(i)], out)


def finish(units, core, position, codes, row, for_e, message, arrived, out, buffer, sems):
    copies = []
    for k, (u, d) in enumerate(units):
        use_mine, use_theirs = masks(codes, u, position, core)
        for t in range(3):
            mine, theirs = complete(core, row, for_e, message, k, t)
            far = arrived[3 * k + t].astype(F32)
            buffer[k, t] = jnp.where(use_mine, mine, jnp.where(use_theirs, theirs, far))
        copies.append(pltpu.make_async_copy(buffer.at[k], out.at[u, 0, d], sems.at[k]))
        copies[-1].start()
    for copy in copies:
        copy.wait()


def finish_near_kernel(mine, row, for_e, message, arrived, out, buffer, sems):
    c = lax.axis_index("gy")
    core, position = lax.rem(c, 2), lax.rem(c, 4)
    finish(NEAR, core, position, mine[...], row, for_e, lambda i: message[tile(i)], arrived, out, buffer, sems)


def finish_far_kernel(mine, row, for_e, message, arrived, started, out, buffer, sems):
    del started
    c = lax.axis_index("gy")
    core, position = lax.rem(c, 2), lax.rem(c, 4)
    finish(FAR, core, position, mine[...], row, for_e, lambda i: message[1 - core, tile(i)], arrived, out, buffer, sems)


def on_device(a_tiles, a_links, p_own, p_side, p_links, coarse_pick):
    count, columns = lax.axis_size("gy"), lax.axis_size("gx")
    pairs = [(2 * g, 2 * g + 1) for g in range(count // 2)]
    cores = [list(pair) for pair in pairs]
    inside = pairs + [(b, a) for a, b in pairs]
    outside = [(i + 1, i + 2) for i in range(0, count - 2, 2)]
    outside = outside + [(b, a) for a, b in outside]
    across = [(i, i ^ 2) for i in range(count)]
    eastward = [(i, i + 1) for i in range(columns - 1)]
    westward = [(b, a) for a, b in eastward]
    bb = (B, B)
    near, far = len(NEAR), len(FAR)

    own, a, sides, east, west, msg_o, msg_e, mine = call(
        begin_kernel,
        [pltpu.with_memory_space_constraint(x, pltpu.HBM)
         for x in (a_links, p_links, coarse_pick.T, p_own, p_side, a_tiles)],
        [(p_own.shape, BF16), (a_tiles.shape, BF16), ((2, 2) + bb, BF16), ((6,) + bb, BF16), ((6,) + bb, BF16),
         ((14 * B + PAD, B), BF16), ((4 * B + PAD, B), BF16), ((PAD, B), F32)],
        in_specs=[HBM] * 6,
        scratch=[pltpu.SMEM(a_links.shape, jnp.int32), pltpu.SMEM(p_links.shape, jnp.int32),
                 pltpu.SMEM((1, 2), jnp.int32), pltpu.VMEM(p_side.shape, BF16), pltpu.SemaphoreType.DMA((6,))])
    halo_o = lax.ppermute(msg_o, "gy", outside)
    from_west = lax.ppermute(east, "gx", eastward)
    from_east = lax.ppermute(west, "gx", westward)
    halo_e = lax.all_gather(msg_e, "gy", axis_index_groups=cores)
    row_n, for_e_n, message_n = call(
        near_kernel, (own, a, sides, halo_e, halo_o),
        [((near, 3) + bb, F32), ((near, 2) + bb, F32), ((5 * near * B + PAD, B), BF16)])
    message_n = lax.ppermute(message_n, "gy", inside)
    row_f, for_e_f, for_o_f = call(
        far_kernel, (own, a, sides, from_west, from_east),
        [((far, 3) + bb, F32), ((far, 2) + bb, F32), ((2 * far,) + bb, BF16)], cost=2 * 10**10)
    chosen_n, wanted = call(
        choose_near_kernel, (mine, row_n, for_e_n, message_n, halo_e, halo_o, row_f),
        [((3 * near,) + bb, BF16), ((PAD, B), F32)])
    arrived_n = lax.ppermute(chosen_n, "gy", across)
    from_o_f = lax.ppermute(for_o_f, "gy", outside)
    row_f, message_f = call(
        merge_kernel, (row_f, for_e_f, from_o_f), [((far, 3) + bb, F32), ((5 * far * B, B), BF16)])
    message_f = lax.all_gather(message_f, "gy", axis_index_groups=cores)
    (chosen_f,) = call(choose_far_kernel, (wanted, row_f, for_e_f, message_f), [((3 * far,) + bb, BF16)])
    arrived_f = lax.ppermute(chosen_f, "gy", across)
    shape = (2, 1, 3, 3) + bb
    (out,) = call(
        finish_near_kernel, (mine, row_n, for_e_n, message_n, arrived_n), [(shape, F32)], out_specs=[HBM],
        scratch=[pltpu.VMEM((near, 3) + bb, F32), pltpu.SemaphoreType.DMA((near,))], cost=2 * 10**10)
    (out,) = call(
        finish_far_kernel, (mine, row_f, for_e_f, message_f, arrived_f, out), [(shape, F32)],
        in_specs=[VMEM] * 5 + [HBM], out_specs=[HBM], aliases={5: 0},
        scratch=[pltpu.VMEM((far, 3) + bb, F32), pltpu.SemaphoreType.DMA((far,))])
    return out


def solution(mesh):
    return jax.shard_map(
        on_device,
        mesh=mesh,
        in_specs=(
            P("gx", "gy", None, None, None),
            P("gx", "gy", None),
            P("gx", "gy", None, None),
            P("gx", "gy", None, None, None),
            P("gx", "gy", None),
            P("gx", "gy"),
        ),
        out_specs=P("gx", "gy", None, None, None, None),
        check_vma=False,
    )
```

```python
import jax
import jax.numpy as jnp
from jax import lax
from jax.experimental import pallas as pl
from jax.experimental.pallas import tpu as pltpu
from jax.sharding import PartitionSpec as P

B = 128
PAD = 16
F32 = jnp.float32
BF16 = jnp.bfloat16
VMEM = pl.BlockSpec(memory_space=pltpu.VMEM)
HBM = pl.BlockSpec(memory_space=pltpu.HBM)

NEAR = ((0, 2), (0, 1), (1, 0), (1, 1))
FAR = ((0, 0), (1, 2))
LINK_TILE = {0: 1, 2: 2}


def call(kernel, args, shapes, in_specs=None, out_specs=None, scratch=(), aliases=None, cost=0):
    return pl.pallas_call(
        kernel,
        in_specs=in_specs or [VMEM] * len(args),
        out_specs=out_specs or [VMEM] * len(shapes),
        out_shape=[jax.ShapeDtypeStruct(shape, dtype) for shape, dtype in shapes],
        scratch_shapes=list(scratch),
        input_output_aliases=aliases or {},
        compiler_params=pltpu.CompilerParams(vmem_limit_bytes=32 * 2**20),
        cost_estimate=pl.CostEstimate(flops=cost, bytes_accessed=cost, transcendentals=0),
    )(*args)


def tile(index):
    return pl.ds(index * B, B)


def dot(a, b):
    return lax.dot_general(a, b, (((1,), (0,)), ((), ())), preferred_element_type=F32)


def dot_t(a, b):
    return lax.dot_general(a, b, (((0,), (0,)), ((), ())), preferred_element_type=F32)


def cat(parts, axis):
    return jnp.concatenate(parts, axis=axis)


def begin_kernel(a_links, p_links, picks, own_in, side_in, a_in,
                 own, a, sides, east, west, msg_o, msg_e, mine,
                 s_links, s_side, s_picks, raw, sems):
    copies = [
        pltpu.make_async_copy(src, dst, sems.at[i])
        for i, (src, dst) in enumerate(((p_links, s_side), (own_in, own), (side_in, raw), (a_links, s_links),
                                        (picks, s_picks), (a_in, a)))
    ]
    for copy in copies:
        copy.start()
    c = lax.axis_index("gy")
    core = lax.rem(c, 2)
    keep = [c > 0, c < lax.axis_size("gy") - 1]
    for copy in copies[:3]:
        copy.wait()
    for u in range(2):
        for k in range(2):
            factor = jnp.where(keep[k], s_side[u, 0, k], 0).astype(F32).astype(BF16)
            sides[u, k] = raw[u, 0, k] * factor
    for u, message in ((1, east), (0, west)):
        for j in range(4):
            message[j] = own[u, j]
        for k in range(2):
            message[4 + k] = sides[u, k]
    for copy in copies[3:5]:
        copy.wait()
    rows = lax.broadcasted_iota(jnp.int32, (PAD, B), 0)
    codes = jnp.where(rows < PAD // 2, s_picks[0, 0], s_picks[0, 1]).astype(F32)
    mine[...] = codes
    msg_o[pl.ds(14 * B, PAD)] = codes.astype(BF16)
    msg_e[pl.ds(4 * B, PAD)] = codes.astype(BF16)
    copies[5].wait()
    for u in range(2):
        for j in range(4):
            for k in range(4):
                a[u, j, k + 1] = a[u, j, k + 1] * s_links[u, j, k].astype(F32).astype(BF16)

    def fill_e(j, k):
        for u in range(2):
            msg_e[tile(2 * u)] = own[u, j]
            msg_e[tile(2 * u + 1)] = sides[u, k]

    def fill_o(j_o, k_o):
        for u in range(2):
            side, block = sides[u, k_o], own[u, j_o]
            other_side, other_block = sides[1 - u, k_o], own[1 - u, j_o]
            zero = jnp.zeros((B, B), BF16)
            inner = 1 if j_o == 0 else 2
            if j_o == 0:
                right = cat([cat([side, block], 1), cat([zero, own[u, inner]], 1)], 0)
                left = cat([a[u, j_o, 0], a[u, j_o, 4]], 1)
                beyond = a[u, j_o, 3]
                panel = cat([other_side, other_block], 1)
            else:
                right = cat([cat([block, side], 1), cat([own[u, inner], zero], 1)], 0)
                left = cat([a[u, j_o, 0], a[u, j_o, 3]], 1)
                beyond = a[u, j_o, 4]
                panel = cat([other_block, other_side], 1)
            centre = dot(left, right).astype(BF16)
            beside = dot(a[u, j_o, LINK_TILE[NEAR[2 * u][1]]], panel).astype(BF16)
            result = dot_t(side, cat([centre, beyond, beside], 1)).astype(BF16)
            msg_o[tile(7 * u)] = block
            msg_o[tile(7 * u + 1)] = side
            for i in range(5):
                msg_o[tile(7 * u + 2 + i)] = result[:, i * B:(i + 1) * B]

    pl.when(core == 0)(lambda: fill_e(3, 1))
    pl.when(core == 1)(lambda: fill_e(0, 0))
    pl.when(jnp.logical_and(core == 0, keep[0]))(lambda: fill_o(0, 0))
    pl.when(jnp.logical_and(core == 1, keep[1]))(lambda: fill_o(3, 1))


def reduce_units(own, u, products, count):
    firsts, middles, lasts = products
    blocks = cat([own[u, j] for j in range(4)], 0)
    slot1 = dot_t(blocks, cat(middles, 0))
    slot0 = dot_t(own[u, 0], firsts)
    slot2 = dot_t(own[u, 3], lasts)
    return [[value[:, i * B:(i + 1) * B] for i in range(count)] for value in (slot0, slot1, slot2)]


def link_products(a, u, d, tiles, side_tiles):
    k = LINK_TILE[d]
    first = dot(a[u, 0, k], cat([side_tiles[0], tiles[0]], 1)).astype(BF16)
    last = dot(a[u, 3, k], cat([tiles[3], side_tiles[1]], 1)).astype(BF16)
    inner = [dot(a[u, j, k], tiles[j]).astype(BF16) for j in (1, 2)]
    return first[:, :B], [first[:, B:], inner[0], inner[1], last[:, :B]], last[:, B:]


def near_kernel(own, a, sides, halo_e, halo_o, row, for_e, message):
    core = lax.rem(lax.axis_index("gy"), 2)
    even = core == 0
    zero = jnp.zeros((B, B), BF16)
    message[pl.ds(20 * B, PAD)] = halo_o[pl.ds(14 * B, PAD)]
    for u in range(2):
        def edge(k):
            from_e, from_o = halo_e[1 - core, tile(2 * u + k)], halo_o[tile(7 * u + k)]
            return jnp.where(even, from_o, from_e), jnp.where(even, from_e, from_o)

        own_down, own_up = edge(0)
        high_down, low_up = edge(1)
        low, high = sides[u, 0], sides[u, 1]
        o = [own[u, j] for j in range(4)]
        right = [
            [[low, o[0]], [own_down, high_down], [zero, o[1]]],
            [[zero, o[1]], [low, o[0]], [zero, o[2]]],
            [[o[2], zero], [o[1], zero], [o[3], high]],
            [[o[3], high], [o[2], zero], [low_up, own_up]],
        ]
        centre = []
        for j in range(4):
            left = cat([a[u, j, 0], a[u, j, 3], a[u, j, 4]], 1)
            centre.append(dot(left, cat([cat(r, 1) for r in right[j]], 0)).astype(BF16))
        left_part = [value[:, :B] for value in centre]
        right_part = [value[:, B:] for value in centre]
        beside = link_products(a, u, NEAR[2 * u][1], [own[1 - u, j] for j in range(4)],
                               [sides[1 - u, k] for k in range(2)])
        first = cat([beside[0], left_part[0]], 1)
        middle = [cat([beside[1][0], right_part[0]], 1), cat([beside[1][1], right_part[1]], 1),
                  cat([beside[1][2], left_part[2]], 1), cat([beside[1][3], left_part[3]], 1)]
        last = cat([beside[2], right_part[3]], 1)
        slots = reduce_units(own, u, (first, middle, last), 2)
        slots[0][1] = slots[0][1] + dot_t(o[1], left_part[1])
        slots[2][1] = slots[2][1] + dot_t(o[2], right_part[2])
        beyond = dot(halo_o[tile(7 * u + 4)], cat([jnp.where(even, low, o[3]), jnp.where(even, o[0], high)], 1))
        given = dot_t(jnp.where(even, high, low),
                      cat([jnp.where(even, middle[3], first), jnp.where(even, last, middle[0])], 1))
        for i in range(2):
            k = 2 * u + i
            for t in range(3):
                row[k, t] = slots[t][i]
            for s in range(2):
                if i == 0:
                    extra = halo_o[tile(7 * u + 5 + s)].astype(F32)
                else:
                    extra = halo_o[tile(7 * u + 2 + s)].astype(F32) + beyond[:, s * B:(s + 1) * B]
                row[k, core + s] += extra
                part = given[:, (2 * s + i) * B:(2 * s + i + 1) * B]
                for_e[k, s] = part
                message[tile(5 * k + 3 + s)] = part.astype(BF16)
            for t in range(3):
                message[tile(5 * k + t)] = row[k, t].astype(BF16)


def far_kernel(own, a, sides, from_west, from_east, row, for_e, message):
    even = lax.rem(lax.axis_index("gy"), 2) == 0
    for k, (u, d) in enumerate(FAR):
        arrived = from_west if d == 0 else from_east
        first, middle, last = link_products(a, u, d, [arrived[j] for j in range(4)], [arrived[4], arrived[5]])
        slots = reduce_units(own, u, (first, middle, last), 1)
        down = dot_t(sides[u, 0], cat([first, middle[0]], 1))
        up = dot_t(sides[u, 1], cat([middle[3], last], 1))
        to_e, to_o = jnp.where(even, up, down), jnp.where(even, down, up)
        for t in range(3):
            row[k, t] = slots[t][0]
            message[tile(7 * k + t)] = slots[t][0].astype(BF16)
        for s in range(2):
            at = slice(s * B, (s + 1) * B)
            for_e[k, s] = to_e[:, at]
            message[tile(7 * k + 3 + s)] = to_e[:, at].astype(BF16)
            message[tile(7 * k + 5 + s)] = to_o[:, at].astype(BF16)


def between_kernel(message, out):
    half = lax.rem(lax.axis_index("gy"), 4) // 2
    for k in range(len(FAR)):
        for s in range(2):
            out[2 * k + s] = message[half, tile(7 * k + 5 + s)]


def far_tiles(core, half, row, for_e, message, from_group, k, t):
    def theirs_at(i):
        return message[1 - core, tile(7 * k + i)].astype(F32)

    def slot(get, shift):
        if t == 1:
            return get(1 - shift)
        return jnp.where(shift == t // 2, get(t // 2), 0.0)

    mine = row[k, t] + slot(lambda s: theirs_at(3 + s), 1 - core)
    theirs = theirs_at(t) + slot(lambda s: for_e[k, s], core)
    group = slot(lambda s: from_group[2 * k + s].astype(F32), half)
    inner = slot(lambda s: message[1 - half, tile(7 * k + 5 + s)].astype(F32), half)
    border = core == half
    return mine + jnp.where(border, group, 0.0), theirs + jnp.where(border, 0.0, group), inner


def complete(core, row, for_e, message, k, t):
    mine = row[k, t]
    theirs = message[tile(5 * k + t)].astype(F32)
    if t == 1:
        mine = mine + message[tile(5 * k + 3 + core)].astype(F32)
        theirs = theirs + for_e[k, 1 - core]
    else:
        gets = (core == 0) == (t == 2)
        s = 1 if t == 2 else 0
        mine = mine + jnp.where(gets, message[tile(5 * k + 3 + s)].astype(F32), 0.0)
        theirs = theirs + jnp.where(gets, 0.0, for_e[k, s])
    return mine, theirs


def masks(codes, u, position, core):
    code = codes[u * PAD // 2:u * PAD // 2 + 1]
    other = position + 1 - 2 * core
    return (jnp.broadcast_to(code == position.astype(F32), (B, B)),
            jnp.broadcast_to(code == other.astype(F32), (B, B)))


def choose_near_kernel(mine, row, for_e, message, halo_e, halo_o, row_far, out, wanted):
    del row_far
    c = lax.axis_index("gy")
    core, position = lax.rem(c, 2), lax.rem(c, 4)
    outer = jnp.logical_or(position == 0, position == 3)
    inferred = 6.0 - mine[...] - halo_e[1 - core, pl.ds(4 * B, PAD)].astype(F32)
    inferred = inferred - halo_o[pl.ds(14 * B, PAD)].astype(F32)
    codes = jnp.where(outer, message[pl.ds(20 * B, PAD)].astype(F32), inferred)
    wanted[...] = codes
    for k, (u, _) in enumerate(NEAR):
        use_mine, use_theirs = masks(codes, u, position, core)
        for t in range(3):
            own_row, other_row = complete(core, row, for_e, message, k, t)
            out[3 * k + t] = jnp.where(use_mine, own_row, jnp.where(use_theirs, other_row, 0.0)).astype(BF16)


def choose_far_kernel(wanted, row, for_e, message, from_group, out):
    c = lax.axis_index("gy")
    core, position = lax.rem(c, 2), lax.rem(c, 4)
    for k, (u, _) in enumerate(FAR):
        use_mine, use_theirs = masks(wanted[...], u, position, core)
        for t in range(3):
            mine, theirs, inner = far_tiles(core, position // 2, row, for_e, message, from_group, k, t)
            out[3 * k + t] = jnp.where(use_mine, mine, jnp.where(use_theirs, theirs, inner)).astype(BF16)


def finish_near_kernel(mine, row, for_e, message, arrived, out, buffer, sems):
    c = lax.axis_index("gy")
    core, position = lax.rem(c, 2), lax.rem(c, 4)
    copies = []
    for k, (u, d) in enumerate(NEAR):
        use_mine, use_theirs = masks(mine[...], u, position, core)
        for t in range(3):
            own_row, other_row = complete(core, row, for_e, message, k, t)
            got = arrived[3 * k + t].astype(F32)
            buffer[k, t] = jnp.where(use_mine, own_row, jnp.where(use_theirs, other_row, got))
        copies.append(pltpu.make_async_copy(buffer.at[k], out.at[u, 0, d], sems.at[k]))
        copies[-1].start()
    for copy in copies:
        copy.wait()


def finish_far_kernel(mine, row, for_e, message, from_group, arrived, started, out, buffer, sems):
    del started
    c = lax.axis_index("gy")
    core, position = lax.rem(c, 2), lax.rem(c, 4)
    half = position // 2
    copies = []
    for k, (u, d) in enumerate(FAR):
        use_mine, use_theirs = masks(mine[...], u, position, core)
        code = mine[u * PAD // 2:u * PAD // 2 + 1]
        add_arrived = jnp.broadcast_to(code == (1 + half).astype(F32), (B, B))
        add_inner = jnp.broadcast_to(code == (2 - half).astype(F32), (B, B))
        for t in range(3):
            own_row, other_row, inner = far_tiles(core, half, row, for_e, message, from_group, k, t)
            got = arrived[3 * k + t].astype(F32)
            here = jnp.where(use_mine, own_row, other_row) + jnp.where(add_arrived, got, 0.0)
            there = got + jnp.where(add_inner, inner, 0.0)
            buffer[k, t] = jnp.where(jnp.logical_or(use_mine, use_theirs), here, there)
        copies.append(pltpu.make_async_copy(buffer.at[k], out.at[u, 0, d], sems.at[k]))
        copies[-1].start()
    for copy in copies:
        copy.wait()


def on_device(a_tiles, a_links, p_own, p_side, p_links, coarse_pick):
    count, columns = lax.axis_size("gy"), lax.axis_size("gx")
    pairs = [(2 * g, 2 * g + 1) for g in range(count // 2)]
    cores = [list(pair) for pair in pairs]
    inside = pairs + [(b, a) for a, b in pairs]
    outside = [(i + 1, i + 2) for i in range(0, count - 2, 2)]
    outside = outside + [(b, a) for a, b in outside]
    between = [(i, i + 2) for i in range(count - 2) if i % 4 > 1]
    between = between + [(b, a) for a, b in between]
    across = [(i, i ^ 2) for i in range(count)]
    eastward = [(i, i + 1) for i in range(columns - 1)]
    westward = [(b, a) for a, b in eastward]
    bb = (B, B)
    near, far = len(NEAR), len(FAR)

    own, a, sides, east, west, msg_o, msg_e, mine = call(
        begin_kernel,
        [pltpu.with_memory_space_constraint(x, pltpu.HBM)
         for x in (a_links, p_links, coarse_pick.T, p_own, p_side, a_tiles)],
        [(p_own.shape, BF16), (a_tiles.shape, BF16), ((2, 2) + bb, BF16), ((6,) + bb, BF16), ((6,) + bb, BF16),
         ((14 * B + PAD, B), BF16), ((4 * B + PAD, B), BF16), ((PAD, B), F32)],
        in_specs=[HBM] * 6,
        scratch=[pltpu.SMEM(a_links.shape, jnp.int32), pltpu.SMEM(p_links.shape, jnp.int32),
                 pltpu.SMEM((1, 2), jnp.int32), pltpu.VMEM(p_side.shape, BF16), pltpu.SemaphoreType.DMA((6,))])
    halo_o = lax.ppermute(msg_o, "gy", outside)
    from_west = lax.ppermute(east, "gx", eastward)
    from_east = lax.ppermute(west, "gx", westward)
    halo_e = lax.all_gather(msg_e, "gy", axis_index_groups=cores)
    row_n, for_e_n, message_n = call(
        near_kernel, (own, a, sides, halo_e, halo_o),
        [((near, 3) + bb, F32), ((near, 2) + bb, F32), ((5 * near * B + PAD, B), BF16)])
    message_n = lax.ppermute(message_n, "gy", inside)
    row_f, for_e_f, message_f = call(
        far_kernel, (own, a, sides, from_west, from_east),
        [((far, 3) + bb, F32), ((far, 2) + bb, F32), ((7 * far * B, B), BF16)], cost=2 * 10**10)
    chosen_n, wanted = call(
        choose_near_kernel, (mine, row_n, for_e_n, message_n, halo_e, halo_o, row_f),
        [((3 * near,) + bb, BF16), ((PAD, B), F32)])
    arrived_n = lax.ppermute(chosen_n, "gy", across)
    message_f = lax.all_gather(message_f, "gy", axis_index_groups=cores)
    (for_group,) = call(between_kernel, (message_f,), [((2 * far,) + bb, BF16)])
    from_group = lax.ppermute(for_group, "gy", between)
    (chosen_f,) = call(
        choose_far_kernel, (wanted, row_f, for_e_f, message_f, from_group), [((3 * far,) + bb, BF16)])
    arrived_f = lax.ppermute(chosen_f, "gy", across)
    shape = (2, 1, 3, 3) + bb
    (out,) = call(
        finish_near_kernel, (mine, row_n, for_e_n, message_n, arrived_n), [(shape, F32)], out_specs=[HBM],
        scratch=[pltpu.VMEM((near, 3) + bb, F32), pltpu.SemaphoreType.DMA((near,))], cost=2 * 10**10)
    (out,) = call(
        finish_far_kernel, (mine, row_f, for_e_f, message_f, from_group, arrived_f, out), [(shape, F32)],
        in_specs=[VMEM] * 6 + [HBM], out_specs=[HBM], aliases={6: 0},
        scratch=[pltpu.VMEM((far, 3) + bb, F32), pltpu.SemaphoreType.DMA((far,))])
    return out


def solution(mesh):
    return jax.shard_map(
        on_device,
        mesh=mesh,
        in_specs=(
            P("gx", "gy", None, None, None),
            P("gx", "gy", None),
            P("gx", "gy", None, None),
            P("gx", "gy", None, None, None),
            P("gx", "gy", None),
            P("gx", "gy"),
        ),
        out_specs=P("gx", "gy", None, None, None, None),
        check_vma=False,
    )
```

```python
import jax
import jax.numpy as jnp
from jax import lax
from jax.experimental import pallas as pl
from jax.experimental.pallas import tpu as pltpu
from jax.sharding import PartitionSpec as P

B = 128
PAD = 16
F32 = jnp.float32
BF16 = jnp.bfloat16
VMEM = pl.BlockSpec(memory_space=pltpu.VMEM)
HBM = pl.BlockSpec(memory_space=pltpu.HBM)

NEAR = ((0, 2), (0, 1), (1, 0), (1, 1))
FAR = ((0, 0), (1, 2))
LINK_TILE = {0: 1, 2: 2}


def call(kernel, args, shapes, in_specs=None, out_specs=None, scratch=(), aliases=None, cost=0):
    return pl.pallas_call(
        kernel,
        in_specs=in_specs or [VMEM] * len(args),
        out_specs=out_specs or [VMEM] * len(shapes),
        out_shape=[jax.ShapeDtypeStruct(shape, dtype) for shape, dtype in shapes],
        scratch_shapes=list(scratch),
        input_output_aliases=aliases or {},
        compiler_params=pltpu.CompilerParams(vmem_limit_bytes=32 * 2**20),
        cost_estimate=pl.CostEstimate(flops=cost, bytes_accessed=cost, transcendentals=0),
    )(*args)


def tile(index):
    return pl.ds(index * B, B)


def dot(a, b):
    return lax.dot_general(a, b, (((1,), (0,)), ((), ())), preferred_element_type=F32)


def dot_t(a, b):
    return lax.dot_general(a, b, (((0,), (0,)), ((), ())), preferred_element_type=F32)


def cat(parts, axis):
    return jnp.concatenate(parts, axis=axis)


def begin_kernel(a_links, p_links, picks, own_in, side_in, a_in,
                 own, a, sides, east, west, msg_o, msg_e, mine,
                 s_links, s_side, s_picks, raw, sems):
    copies = [
        pltpu.make_async_copy(src, dst, sems.at[i])
        for i, (src, dst) in enumerate(((p_links, s_side), (own_in, own), (side_in, raw), (a_links, s_links),
                                        (picks, s_picks), (a_in, a)))
    ]
    for copy in copies:
        copy.start()
    c = lax.axis_index("gy")
    core = lax.rem(c, 2)
    keep = [c > 0, c < lax.axis_size("gy") - 1]
    for copy in copies[:3]:
        copy.wait()
    for u in range(2):
        for k in range(2):
            factor = jnp.where(keep[k], s_side[u, 0, k], 0).astype(F32).astype(BF16)
            sides[u, k] = raw[u, 0, k] * factor
    for u, message in ((1, east), (0, west)):
        for j in range(4):
            message[j] = own[u, j]
        for k in range(2):
            message[4 + k] = sides[u, k]
    for copy in copies[3:5]:
        copy.wait()
    rows = lax.broadcasted_iota(jnp.int32, (PAD, B), 0)
    codes = jnp.where(rows < PAD // 2, s_picks[0, 0], s_picks[0, 1]).astype(F32)
    mine[...] = codes
    msg_o[pl.ds(14 * B, PAD)] = codes.astype(BF16)
    msg_e[pl.ds(4 * B, PAD)] = codes.astype(BF16)
    copies[5].wait()
    for u in range(2):
        for j in range(4):
            for k in range(4):
                a[u, j, k + 1] = a[u, j, k + 1] * s_links[u, j, k].astype(F32).astype(BF16)

    def fill_e(j, k):
        for u in range(2):
            msg_e[tile(2 * u)] = own[u, j]
            msg_e[tile(2 * u + 1)] = sides[u, k]

    def fill_o(j_o, k_o):
        for u in range(2):
            side, block = sides[u, k_o], own[u, j_o]
            other_side, other_block = sides[1 - u, k_o], own[1 - u, j_o]
            zero = jnp.zeros((B, B), BF16)
            inner = 1 if j_o == 0 else 2
            if j_o == 0:
                right = cat([cat([side, block], 1), cat([zero, own[u, inner]], 1)], 0)
                left = cat([a[u, j_o, 0], a[u, j_o, 4]], 1)
                beyond = a[u, j_o, 3]
                panel = cat([other_side, other_block], 1)
            else:
                right = cat([cat([block, side], 1), cat([own[u, inner], zero], 1)], 0)
                left = cat([a[u, j_o, 0], a[u, j_o, 3]], 1)
                beyond = a[u, j_o, 4]
                panel = cat([other_block, other_side], 1)
            centre = dot(left, right).astype(BF16)
            beside = dot(a[u, j_o, LINK_TILE[NEAR[2 * u][1]]], panel).astype(BF16)
            result = dot_t(side, cat([centre, beyond, beside], 1)).astype(BF16)
            msg_o[tile(7 * u)] = block
            msg_o[tile(7 * u + 1)] = side
            for i in range(5):
                msg_o[tile(7 * u + 2 + i)] = result[:, i * B:(i + 1) * B]

    pl.when(core == 0)(lambda: fill_e(3, 1))
    pl.when(core == 1)(lambda: fill_e(0, 0))
    pl.when(jnp.logical_and(core == 0, keep[0]))(lambda: fill_o(0, 0))
    pl.when(jnp.logical_and(core == 1, keep[1]))(lambda: fill_o(3, 1))


def reduce_units(own, u, products, count):
    firsts, middles, lasts = products
    blocks = cat([own[u, j] for j in range(4)], 0)
    slot1 = dot_t(blocks, cat(middles, 0))
    slot0 = dot_t(own[u, 0], firsts)
    slot2 = dot_t(own[u, 3], lasts)
    return [[value[:, i * B:(i + 1) * B] for i in range(count)] for value in (slot0, slot1, slot2)]


def link_products(a, u, d, tiles, side_tiles):
    k = LINK_TILE[d]
    first = dot(a[u, 0, k], cat([side_tiles[0], tiles[0]], 1)).astype(BF16)
    last = dot(a[u, 3, k], cat([tiles[3], side_tiles[1]], 1)).astype(BF16)
    inner = [dot(a[u, j, k], tiles[j]).astype(BF16) for j in (1, 2)]
    return first[:, :B], [first[:, B:], inner[0], inner[1], last[:, :B]], last[:, B:]


def near_kernel(own, a, sides, halo_e, halo_o, row, for_e, message):
    core = lax.rem(lax.axis_index("gy"), 2)
    even = core == 0
    zero = jnp.zeros((B, B), BF16)
    message[pl.ds(20 * B, PAD)] = halo_o[pl.ds(14 * B, PAD)]
    for u in range(2):
        def edge(k):
            from_e, from_o = halo_e[1 - core, tile(2 * u + k)], halo_o[tile(7 * u + k)]
            return jnp.where(even, from_o, from_e), jnp.where(even, from_e, from_o)

        own_down, own_up = edge(0)
        high_down, low_up = edge(1)
        low, high = sides[u, 0], sides[u, 1]
        o = [own[u, j] for j in range(4)]
        right = [
            [[low, o[0]], [own_down, high_down], [zero, o[1]]],
            [[zero, o[1]], [low, o[0]], [zero, o[2]]],
            [[o[2], zero], [o[1], zero], [o[3], high]],
            [[o[3], high], [o[2], zero], [low_up, own_up]],
        ]
        centre = []
        for j in range(4):
            left = cat([a[u, j, 0], a[u, j, 3], a[u, j, 4]], 1)
            centre.append(dot(left, cat([cat(r, 1) for r in right[j]], 0)).astype(BF16))
        left_part = [value[:, :B] for value in centre]
        right_part = [value[:, B:] for value in centre]
        beside = link_products(a, u, NEAR[2 * u][1], [own[1 - u, j] for j in range(4)],
                               [sides[1 - u, k] for k in range(2)])
        first = cat([beside[0], left_part[0]], 1)
        middle = [cat([beside[1][0], right_part[0]], 1), cat([beside[1][1], right_part[1]], 1),
                  cat([beside[1][2], left_part[2]], 1), cat([beside[1][3], left_part[3]], 1)]
        last = cat([beside[2], right_part[3]], 1)
        slots = reduce_units(own, u, (first, middle, last), 2)
        slots[0][1] = slots[0][1] + dot_t(o[1], left_part[1])
        slots[2][1] = slots[2][1] + dot_t(o[2], right_part[2])
        beyond = dot(halo_o[tile(7 * u + 4)], cat([jnp.where(even, low, o[3]), jnp.where(even, o[0], high)], 1))
        given = dot_t(jnp.where(even, high, low),
                      cat([jnp.where(even, middle[3], first), jnp.where(even, last, middle[0])], 1))
        for i in range(2):
            k = 2 * u + i
            for t in range(3):
                row[k, t] = slots[t][i]
            for s in range(2):
                if i == 0:
                    extra = halo_o[tile(7 * u + 5 + s)].astype(F32)
                else:
                    extra = halo_o[tile(7 * u + 2 + s)].astype(F32) + beyond[:, s * B:(s + 1) * B]
                row[k, core + s] += extra
                part = given[:, (2 * s + i) * B:(2 * s + i + 1) * B]
                for_e[k, s] = part
                message[tile(5 * k + 3 + s)] = part.astype(BF16)
            for t in range(3):
                message[tile(5 * k + t)] = row[k, t].astype(BF16)


def far_kernel(own, a, sides, from_west, from_east, row, for_e, for_o):
    even = lax.rem(lax.axis_index("gy"), 2) == 0
    for k, (u, d) in enumerate(FAR):
        arrived = from_west if d == 0 else from_east
        first, middle, last = link_products(a, u, d, [arrived[j] for j in range(4)], [arrived[4], arrived[5]])
        slots = reduce_units(own, u, (first, middle, last), 1)
        down = dot_t(sides[u, 0], cat([first, middle[0]], 1))
        up = dot_t(sides[u, 1], cat([middle[3], last], 1))
        to_e, to_o = jnp.where(even, up, down), jnp.where(even, down, up)
        for t in range(3):
            row[k, t] = slots[t][0]
        for s in range(2):
            at = slice(s * B, (s + 1) * B)
            for_e[k, s] = to_e[:, at]
            for_o[2 * k + s] = to_o[:, at].astype(BF16)


def merge_kernel(row, for_e, for_o, from_group, row_out, message):
    core = lax.rem(lax.axis_index("gy"), 2)
    for k in range(len(FAR)):
        for t in range(3):
            row_out[k, t] = row[k, t]
        for s in range(2):
            row_out[k, core + s] += from_group[2 * k + s].astype(F32)
            message[tile(7 * k + 3 + s)] = for_e[k, s].astype(BF16)
            message[tile(7 * k + 5 + s)] = for_o[2 * k + s]
        for t in range(3):
            message[tile(7 * k + t)] = row_out[k, t].astype(BF16)


def far_tiles(core, half, row, for_e, message, k, t):
    def theirs_at(i):
        return message[1 - core, tile(7 * k + i)].astype(F32)

    def slot(get, shift):
        if t == 1:
            return get(1 - shift)
        return jnp.where(shift == t // 2, get(t // 2), 0.0)

    mine = row[k, t] + slot(lambda s: theirs_at(3 + s), 1 - core)
    theirs = theirs_at(t) + slot(lambda s: for_e[k, s], core)
    inner = slot(lambda s: message[1 - half, tile(7 * k + 5 + s)].astype(F32), half)
    return mine, theirs, inner


def complete(core, row, for_e, message, k, t):
    mine = row[k, t]
    theirs = message[tile(5 * k + t)].astype(F32)
    if t == 1:
        mine = mine + message[tile(5 * k + 3 + core)].astype(F32)
        theirs = theirs + for_e[k, 1 - core]
    else:
        gets = (core == 0) == (t == 2)
        s = 1 if t == 2 else 0
        mine = mine + jnp.where(gets, message[tile(5 * k + 3 + s)].astype(F32), 0.0)
        theirs = theirs + jnp.where(gets, 0.0, for_e[k, s])
    return mine, theirs


def masks(codes, u, position, core):
    code = codes[u * PAD // 2:u * PAD // 2 + 1]
    other = position + 1 - 2 * core
    return (jnp.broadcast_to(code == position.astype(F32), (B, B)),
            jnp.broadcast_to(code == other.astype(F32), (B, B)))


def choose_near_kernel(mine, row, for_e, message, halo_e, halo_o, row_far, out, wanted):
    del row_far
    c = lax.axis_index("gy")
    core, position = lax.rem(c, 2), lax.rem(c, 4)
    outer = jnp.logical_or(position == 0, position == 3)
    inferred = 6.0 - mine[...] - halo_e[1 - core, pl.ds(4 * B, PAD)].astype(F32)
    inferred = inferred - halo_o[pl.ds(14 * B, PAD)].astype(F32)
    codes = jnp.where(outer, message[pl.ds(20 * B, PAD)].astype(F32), inferred)
    wanted[...] = codes
    for k, (u, _) in enumerate(NEAR):
        use_mine, use_theirs = masks(codes, u, position, core)
        for t in range(3):
            own_row, other_row = complete(core, row, for_e, message, k, t)
            out[3 * k + t] = jnp.where(use_mine, own_row, jnp.where(use_theirs, other_row, 0.0)).astype(BF16)


def choose_far_kernel(wanted, row, for_e, message, out):
    c = lax.axis_index("gy")
    core, position = lax.rem(c, 2), lax.rem(c, 4)
    for k, (u, _) in enumerate(FAR):
        use_mine, use_theirs = masks(wanted[...], u, position, core)
        for t in range(3):
            mine, theirs, inner = far_tiles(core, position // 2, row, for_e, message, k, t)
            out[3 * k + t] = jnp.where(use_mine, mine, jnp.where(use_theirs, theirs, inner)).astype(BF16)


def finish_near_kernel(mine, row, for_e, message, arrived, out, buffer, sems):
    c = lax.axis_index("gy")
    core, position = lax.rem(c, 2), lax.rem(c, 4)
    copies = []
    for k, (u, d) in enumerate(NEAR):
        use_mine, use_theirs = masks(mine[...], u, position, core)
        for t in range(3):
            own_row, other_row = complete(core, row, for_e, message, k, t)
            got = arrived[3 * k + t].astype(F32)
            buffer[k, t] = jnp.where(use_mine, own_row, jnp.where(use_theirs, other_row, got))
        copies.append(pltpu.make_async_copy(buffer.at[k], out.at[u, 0, d], sems.at[k]))
        copies[-1].start()
    for copy in copies:
        copy.wait()


def finish_far_kernel(mine, row, for_e, message, arrived, started, out, buffer, sems):
    del started
    c = lax.axis_index("gy")
    core, position = lax.rem(c, 2), lax.rem(c, 4)
    half = position // 2
    copies = []
    for k, (u, d) in enumerate(FAR):
        use_mine, use_theirs = masks(mine[...], u, position, core)
        code = mine[u * PAD // 2:u * PAD // 2 + 1]
        add_arrived = jnp.broadcast_to(code == (1 + half).astype(F32), (B, B))
        add_inner = jnp.broadcast_to(code == (2 - half).astype(F32), (B, B))
        for t in range(3):
            own_row, other_row, inner = far_tiles(core, half, row, for_e, message, k, t)
            got = arrived[3 * k + t].astype(F32)
            here = jnp.where(use_mine, own_row, other_row) + jnp.where(add_arrived, got, 0.0)
            there = got + jnp.where(add_inner, inner, 0.0)
            buffer[k, t] = jnp.where(jnp.logical_or(use_mine, use_theirs), here, there)
        copies.append(pltpu.make_async_copy(buffer.at[k], out.at[u, 0, d], sems.at[k]))
        copies[-1].start()
    for copy in copies:
        copy.wait()


def on_device(a_tiles, a_links, p_own, p_side, p_links, coarse_pick):
    count, columns = lax.axis_size("gy"), lax.axis_size("gx")
    pairs = [(2 * g, 2 * g + 1) for g in range(count // 2)]
    cores = [list(pair) for pair in pairs]
    inside = pairs + [(b, a) for a, b in pairs]
    outside = [(i + 1, i + 2) for i in range(0, count - 2, 2)]
    outside = outside + [(b, a) for a, b in outside]
    between = [(i, i + 1) for i in range(3, count - 1, 4)]
    between = between + [(b, a) for a, b in between]
    across = [(i, i ^ 2) for i in range(count)]
    eastward = [(i, i + 1) for i in range(columns - 1)]
    westward = [(b, a) for a, b in eastward]
    bb = (B, B)
    near, far = len(NEAR), len(FAR)

    own, a, sides, east, west, msg_o, msg_e, mine = call(
        begin_kernel,
        [pltpu.with_memory_space_constraint(x, pltpu.HBM)
         for x in (a_links, p_links, coarse_pick.T, p_own, p_side, a_tiles)],
        [(p_own.shape, BF16), (a_tiles.shape, BF16), ((2, 2) + bb, BF16), ((6,) + bb, BF16), ((6,) + bb, BF16),
         ((14 * B + PAD, B), BF16), ((4 * B + PAD, B), BF16), ((PAD, B), F32)],
        in_specs=[HBM] * 6,
        scratch=[pltpu.SMEM(a_links.shape, jnp.int32), pltpu.SMEM(p_links.shape, jnp.int32),
                 pltpu.SMEM((1, 2), jnp.int32), pltpu.VMEM(p_side.shape, BF16), pltpu.SemaphoreType.DMA((6,))])
    halo_o = lax.ppermute(msg_o, "gy", outside)
    from_west = lax.ppermute(east, "gx", eastward)
    from_east = lax.ppermute(west, "gx", westward)
    halo_e = lax.all_gather(msg_e, "gy", axis_index_groups=cores)
    row_n, for_e_n, message_n = call(
        near_kernel, (own, a, sides, halo_e, halo_o),
        [((near, 3) + bb, F32), ((near, 2) + bb, F32), ((5 * near * B + PAD, B), BF16)])
    message_n = lax.ppermute(message_n, "gy", inside)
    row_f, for_e_f, for_o_f = call(
        far_kernel, (own, a, sides, from_west, from_east),
        [((far, 3) + bb, F32), ((far, 2) + bb, F32), ((2 * far,) + bb, BF16)], cost=2 * 10**10)
    chosen_n, wanted = call(
        choose_near_kernel, (mine, row_n, for_e_n, message_n, halo_e, halo_o, row_f),
        [((3 * near,) + bb, BF16), ((PAD, B), F32)])
    arrived_n = lax.ppermute(chosen_n, "gy", across)
    from_group = lax.ppermute(for_o_f, "gy", between)
    row_f, message_f = call(
        merge_kernel, (row_f, for_e_f, for_o_f, from_group), [((far, 3) + bb, F32), ((7 * far * B, B), BF16)])
    message_f = lax.all_gather(message_f, "gy", axis_index_groups=cores)
    (chosen_f,) = call(choose_far_kernel, (wanted, row_f, for_e_f, message_f), [((3 * far,) + bb, BF16)])
    arrived_f = lax.ppermute(chosen_f, "gy", across)
    shape = (2, 1, 3, 3) + bb
    (out,) = call(
        finish_near_kernel, (mine, row_n, for_e_n, message_n, arrived_n), [(shape, F32)], out_specs=[HBM],
        scratch=[pltpu.VMEM((near, 3) + bb, F32), pltpu.SemaphoreType.DMA((near,))], cost=2 * 10**10)
    (out,) = call(
        finish_far_kernel, (mine, row_f, for_e_f, message_f, arrived_f, out), [(shape, F32)],
        in_specs=[VMEM] * 5 + [HBM], out_specs=[HBM], aliases={5: 0},
        scratch=[pltpu.VMEM((far, 3) + bb, F32), pltpu.SemaphoreType.DMA((far,))])
    return out


def solution(mesh):
    return jax.shard_map(
        on_device,
        mesh=mesh,
        in_specs=(
            P("gx", "gy", None, None, None),
            P("gx", "gy", None),
            P("gx", "gy", None, None),
            P("gx", "gy", None, None, None),
            P("gx", "gy", None),
            P("gx", "gy"),
        ),
        out_specs=P("gx", "gy", None, None, None, None),
        check_vma=False,
    )
```

```python
import jax
import jax.numpy as jnp
from jax import lax
from jax.experimental import pallas as pl
from jax.experimental.pallas import tpu as pltpu
from jax.sharding import PartitionSpec as P

B = 128
PAD = 16
F32 = jnp.float32
BF16 = jnp.bfloat16
VMEM = pl.BlockSpec(memory_space=pltpu.VMEM)
HBM = pl.BlockSpec(memory_space=pltpu.HBM)

NEAR = ((0, 2), (0, 1), (1, 0), (1, 1))
FAR = ((0, 0), (1, 2))
LINK_TILE = {0: 1, 2: 2}


def call(kernel, args, shapes, in_specs=None, out_specs=None, scratch=(), aliases=None, cost=0):
    return pl.pallas_call(
        kernel,
        in_specs=in_specs or [VMEM] * len(args),
        out_specs=out_specs or [VMEM] * len(shapes),
        out_shape=[jax.ShapeDtypeStruct(shape, dtype) for shape, dtype in shapes],
        scratch_shapes=list(scratch),
        input_output_aliases=aliases or {},
        compiler_params=pltpu.CompilerParams(vmem_limit_bytes=32 * 2**20),
        cost_estimate=pl.CostEstimate(flops=cost, bytes_accessed=cost, transcendentals=0),
    )(*args)


def tile(index):
    return pl.ds(index * B, B)


def dot(a, b):
    return lax.dot_general(a, b, (((1,), (0,)), ((), ())), preferred_element_type=F32)


def dot_t(a, b):
    return lax.dot_general(a, b, (((0,), (0,)), ((), ())), preferred_element_type=F32)


def cat(parts, axis):
    return jnp.concatenate(parts, axis=axis)


def begin_kernel(a_links, p_links, picks, own_in, side_in, a_in,
                 own, a, sides, east, west, msg_o, msg_e, mine,
                 s_links, s_side, s_picks, raw, sems):
    copies = [
        pltpu.make_async_copy(src, dst, sems.at[i])
        for i, (src, dst) in enumerate(((p_links, s_side), (own_in, own), (side_in, raw), (a_links, s_links),
                                        (picks, s_picks), (a_in, a)))
    ]
    for copy in copies:
        copy.start()
    c = lax.axis_index("gy")
    core = lax.rem(c, 2)
    keep = [c > 0, c < lax.axis_size("gy") - 1]
    for copy in copies[:3]:
        copy.wait()
    for u in range(2):
        for k in range(2):
            factor = jnp.where(keep[k], s_side[u, 0, k], 0).astype(F32).astype(BF16)
            sides[u, k] = raw[u, 0, k] * factor
    for u, message in ((1, east), (0, west)):
        for j in range(4):
            message[j] = own[u, j]
        for k in range(2):
            message[4 + k] = sides[u, k]
    for copy in copies[3:5]:
        copy.wait()
    rows = lax.broadcasted_iota(jnp.int32, (PAD, B), 0)
    codes = jnp.where(rows < PAD // 2, s_picks[0, 0], s_picks[0, 1]).astype(F32)
    mine[...] = codes
    msg_o[pl.ds(14 * B, PAD)] = codes.astype(BF16)
    msg_e[pl.ds(4 * B, PAD)] = codes.astype(BF16)
    copies[5].wait()
    for u in range(2):
        for j in range(4):
            for k in range(4):
                a[u, j, k + 1] = a[u, j, k + 1] * s_links[u, j, k].astype(F32).astype(BF16)

    def fill_e(j, k):
        for u in range(2):
            msg_e[tile(2 * u)] = own[u, j]
            msg_e[tile(2 * u + 1)] = sides[u, k]

    def fill_o(j_o, k_o):
        for u in range(2):
            side, block = sides[u, k_o], own[u, j_o]
            other_side, other_block = sides[1 - u, k_o], own[1 - u, j_o]
            zero = jnp.zeros((B, B), BF16)
            inner = 1 if j_o == 0 else 2
            if j_o == 0:
                right = cat([cat([side, block], 1), cat([zero, own[u, inner]], 1)], 0)
                left = cat([a[u, j_o, 0], a[u, j_o, 4]], 1)
                beyond = a[u, j_o, 3]
                panel = cat([other_side, other_block], 1)
            else:
                right = cat([cat([block, side], 1), cat([own[u, inner], zero], 1)], 0)
                left = cat([a[u, j_o, 0], a[u, j_o, 3]], 1)
                beyond = a[u, j_o, 4]
                panel = cat([other_block, other_side], 1)
            centre = dot(left, right).astype(BF16)
            beside = dot(a[u, j_o, LINK_TILE[NEAR[2 * u][1]]], panel).astype(BF16)
            result = dot_t(side, cat([centre, beyond, beside], 1)).astype(BF16)
            msg_o[tile(7 * u)] = block
            msg_o[tile(7 * u + 1)] = side
            for i in range(5):
                msg_o[tile(7 * u + 2 + i)] = result[:, i * B:(i + 1) * B]

    pl.when(core == 0)(lambda: fill_e(3, 1))
    pl.when(core == 1)(lambda: fill_e(0, 0))
    pl.when(jnp.logical_and(core == 0, keep[0]))(lambda: fill_o(0, 0))
    pl.when(jnp.logical_and(core == 1, keep[1]))(lambda: fill_o(3, 1))


def reduce_units(own, u, products, count):
    firsts, middles, lasts = products
    blocks = cat([own[u, j] for j in range(4)], 0)
    slot1 = dot_t(blocks, cat(middles, 0))
    slot0 = dot_t(own[u, 0], firsts)
    slot2 = dot_t(own[u, 3], lasts)
    return [[value[:, i * B:(i + 1) * B] for i in range(count)] for value in (slot0, slot1, slot2)]


def link_products(a, u, d, tiles, side_tiles):
    k = LINK_TILE[d]
    first = dot(a[u, 0, k], cat([side_tiles[0], tiles[0]], 1)).astype(BF16)
    last = dot(a[u, 3, k], cat([tiles[3], side_tiles[1]], 1)).astype(BF16)
    inner = [dot(a[u, j, k], tiles[j]).astype(BF16) for j in (1, 2)]
    return first[:, :B], [first[:, B:], inner[0], inner[1], last[:, :B]], last[:, B:]


def near_kernel(own, a, sides, halo_e, halo_o, row, for_e, message):
    core = lax.rem(lax.axis_index("gy"), 2)
    even = core == 0
    zero = jnp.zeros((B, B), BF16)
    message[pl.ds(20 * B, PAD)] = halo_o[pl.ds(14 * B, PAD)]
    for u in range(2):
        def edge(k):
            from_e, from_o = halo_e[1 - core, tile(2 * u + k)], halo_o[tile(7 * u + k)]
            return jnp.where(even, from_o, from_e), jnp.where(even, from_e, from_o)

        own_down, own_up = edge(0)
        high_down, low_up = edge(1)
        low, high = sides[u, 0], sides[u, 1]
        o = [own[u, j] for j in range(4)]
        right = [
            [[low, o[0]], [own_down, high_down], [zero, o[1]]],
            [[zero, o[1]], [low, o[0]], [zero, o[2]]],
            [[o[2], zero], [o[1], zero], [o[3], high]],
            [[o[3], high], [o[2], zero], [low_up, own_up]],
        ]
        centre = []
        for j in range(4):
            left = cat([a[u, j, 0], a[u, j, 3], a[u, j, 4]], 1)
            centre.append(dot(left, cat([cat(r, 1) for r in right[j]], 0)).astype(BF16))
        left_part = [value[:, :B] for value in centre]
        right_part = [value[:, B:] for value in centre]
        beside = link_products(a, u, NEAR[2 * u][1], [own[1 - u, j] for j in range(4)],
                               [sides[1 - u, k] for k in range(2)])
        first = cat([beside[0], left_part[0]], 1)
        middle = [cat([beside[1][0], right_part[0]], 1), cat([beside[1][1], right_part[1]], 1),
                  cat([beside[1][2], left_part[2]], 1), cat([beside[1][3], left_part[3]], 1)]
        last = cat([beside[2], right_part[3]], 1)
        slots = reduce_units(own, u, (first, middle, last), 2)
        slots[0][1] = slots[0][1] + dot_t(o[1], left_part[1])
        slots[2][1] = slots[2][1] + dot_t(o[2], right_part[2])
        beyond = dot(halo_o[tile(7 * u + 4)], cat([jnp.where(even, low, o[3]), jnp.where(even, o[0], high)], 1))
        given = dot_t(jnp.where(even, high, low),
                      cat([jnp.where(even, middle[3], first), jnp.where(even, last, middle[0])], 1))
        for i in range(2):
            k = 2 * u + i
            for t in range(3):
                row[k, t] = slots[t][i]
            for s in range(2):
                if i == 0:
                    extra = halo_o[tile(7 * u + 5 + s)].astype(F32)
                else:
                    extra = halo_o[tile(7 * u + 2 + s)].astype(F32) + beyond[:, s * B:(s + 1) * B]
                row[k, core + s] += extra
                part = given[:, (2 * s + i) * B:(2 * s + i + 1) * B]
                for_e[k, s] = part
                message[tile(5 * k + 3 + s)] = part.astype(BF16)
            for t in range(3):
                message[tile(5 * k + t)] = row[k, t].astype(BF16)


def far_kernel(own, a, sides, from_west, from_east, row, for_e, for_o):
    even = lax.rem(lax.axis_index("gy"), 2) == 0
    for k, (u, d) in enumerate(FAR):
        arrived = from_west if d == 0 else from_east
        first, middle, last = link_products(a, u, d, [arrived[j] for j in range(4)], [arrived[4], arrived[5]])
        slots = reduce_units(own, u, (first, middle, last), 1)
        down = dot_t(sides[u, 0], cat([first, middle[0]], 1))
        up = dot_t(sides[u, 1], cat([middle[3], last], 1))
        to_e, to_o = jnp.where(even, up, down), jnp.where(even, down, up)
        for t in range(3):
            row[k, t] = slots[t][0]
        for s in range(2):
            at = slice(s * B, (s + 1) * B)
            for_e[k, s] = to_e[:, at]
            for_o[2 * k + s] = to_o[:, at].astype(BF16)


def merge_kernel(row, for_e, for_o, from_group, chosen, row_out, message):
    core = lax.rem(lax.axis_index("gy"), 2)
    for k in range(len(FAR)):
        for t in range(3):
            row_out[k, t] = row[k, t]
        for s in range(2):
            row_out[k, core + s] += from_group[2 * k + s].astype(F32)
            message[tile(7 * k + 3 + s)] = for_e[k, s].astype(BF16)
            message[tile(7 * k + 5 + s)] = for_o[2 * k + s]
        for t in range(3):
            message[tile(7 * k + t)] = row_out[k, t].astype(BF16)


def far_tiles(core, half, row, for_e, message, k, t):
    def theirs_at(i):
        return message[1 - core, tile(7 * k + i)].astype(F32)

    def slot(get, shift):
        if t == 1:
            return get(1 - shift)
        return jnp.where(shift == t // 2, get(t // 2), 0.0)

    mine = row[k, t] + slot(lambda s: theirs_at(3 + s), 1 - core)
    theirs = theirs_at(t) + slot(lambda s: for_e[k, s], core)
    inner = slot(lambda s: message[1 - half, tile(7 * k + 5 + s)].astype(F32), half)
    return mine, theirs, inner


def complete(core, row, for_e, message, k, t):
    mine = row[k, t]
    theirs = message[tile(5 * k + t)].astype(F32)
    if t == 1:
        mine = mine + message[tile(5 * k + 3 + core)].astype(F32)
        theirs = theirs + for_e[k, 1 - core]
    else:
        gets = (core == 0) == (t == 2)
        s = 1 if t == 2 else 0
        mine = mine + jnp.where(gets, message[tile(5 * k + 3 + s)].astype(F32), 0.0)
        theirs = theirs + jnp.where(gets, 0.0, for_e[k, s])
    return mine, theirs


def masks(codes, u, position, core):
    code = codes[u * PAD // 2:u * PAD // 2 + 1]
    other = position + 1 - 2 * core
    return (jnp.broadcast_to(code == position.astype(F32), (B, B)),
            jnp.broadcast_to(code == other.astype(F32), (B, B)))


def choose_near_kernel(mine, row, for_e, message, halo_e, halo_o, row_far, out, wanted):
    del row_far
    c = lax.axis_index("gy")
    core, position = lax.rem(c, 2), lax.rem(c, 4)
    outer = jnp.logical_or(position == 0, position == 3)
    inferred = 6.0 - mine[...] - halo_e[1 - core, pl.ds(4 * B, PAD)].astype(F32)
    inferred = inferred - halo_o[pl.ds(14 * B, PAD)].astype(F32)
    codes = jnp.where(outer, message[pl.ds(20 * B, PAD)].astype(F32), inferred)
    wanted[...] = codes
    for k, (u, _) in enumerate(NEAR):
        use_mine, use_theirs = masks(codes, u, position, core)
        for t in range(3):
            own_row, other_row = complete(core, row, for_e, message, k, t)
            out[3 * k + t] = jnp.where(use_mine, own_row, jnp.where(use_theirs, other_row, 0.0)).astype(BF16)


def choose_far_kernel(wanted, row, for_e, message, out):
    c = lax.axis_index("gy")
    core, position = lax.rem(c, 2), lax.rem(c, 4)
    for k, (u, _) in enumerate(FAR):
        use_mine, use_theirs = masks(wanted[...], u, position, core)
        for t in range(3):
            mine, theirs, inner = far_tiles(core, position // 2, row, for_e, message, k, t)
            out[3 * k + t] = jnp.where(use_mine, mine, jnp.where(use_theirs, theirs, inner)).astype(BF16)


def finish_near_kernel(mine, row, for_e, message, arrived, out, buffer, sems):
    c = lax.axis_index("gy")
    core, position = lax.rem(c, 2), lax.rem(c, 4)
    copies = []
    for k, (u, d) in enumerate(NEAR):
        use_mine, use_theirs = masks(mine[...], u, position, core)
        for t in range(3):
            own_row, other_row = complete(core, row, for_e, message, k, t)
            got = arrived[3 * k + t].astype(F32)
            buffer[k, t] = jnp.where(use_mine, own_row, jnp.where(use_theirs, other_row, got))
        copies.append(pltpu.make_async_copy(buffer.at[k], out.at[u, 0, d], sems.at[k]))
        copies[-1].start()
    for copy in copies:
        copy.wait()


def finish_far_kernel(mine, row, for_e, message, arrived, started, out, buffer, sems):
    del started
    c = lax.axis_index("gy")
    core, position = lax.rem(c, 2), lax.rem(c, 4)
    half = position // 2
    copies = []
    for k, (u, d) in enumerate(FAR):
        use_mine, use_theirs = masks(mine[...], u, position, core)
        code = mine[u * PAD // 2:u * PAD // 2 + 1]
        add_arrived = jnp.broadcast_to(code == (1 + half).astype(F32), (B, B))
        add_inner = jnp.broadcast_to(code == (2 - half).astype(F32), (B, B))
        for t in range(3):
            own_row, other_row, inner = far_tiles(core, half, row, for_e, message, k, t)
            got = arrived[3 * k + t].astype(F32)
            here = jnp.where(use_mine, own_row, other_row) + jnp.where(add_arrived, got, 0.0)
            there = got + jnp.where(add_inner, inner, 0.0)
            buffer[k, t] = jnp.where(jnp.logical_or(use_mine, use_theirs), here, there)
        copies.append(pltpu.make_async_copy(buffer.at[k], out.at[u, 0, d], sems.at[k]))
        copies[-1].start()
    for copy in copies:
        copy.wait()


def on_device(a_tiles, a_links, p_own, p_side, p_links, coarse_pick):
    count, columns = lax.axis_size("gy"), lax.axis_size("gx")
    pairs = [(2 * g, 2 * g + 1) for g in range(count // 2)]
    cores = [list(pair) for pair in pairs]
    inside = pairs + [(b, a) for a, b in pairs]
    outside = [(i + 1, i + 2) for i in range(0, count - 2, 2)]
    outside = outside + [(b, a) for a, b in outside]
    between = [(i, i + 1) for i in range(3, count - 1, 4)]
    between = between + [(b, a) for a, b in between]
    across = [(i, i ^ 2) for i in range(count)]
    eastward = [(i, i + 1) for i in range(columns - 1)]
    westward = [(b, a) for a, b in eastward]
    bb = (B, B)
    near, far = len(NEAR), len(FAR)

    own, a, sides, east, west, msg_o, msg_e, mine = call(
        begin_kernel,
        [pltpu.with_memory_space_constraint(x, pltpu.HBM)
         for x in (a_links, p_links, coarse_pick.T, p_own, p_side, a_tiles)],
        [(p_own.shape, BF16), (a_tiles.shape, BF16), ((2, 2) + bb, BF16), ((6,) + bb, BF16), ((6,) + bb, BF16),
         ((14 * B + PAD, B), BF16), ((4 * B + PAD, B), BF16), ((PAD, B), F32)],
        in_specs=[HBM] * 6,
        scratch=[pltpu.SMEM(a_links.shape, jnp.int32), pltpu.SMEM(p_links.shape, jnp.int32),
                 pltpu.SMEM((1, 2), jnp.int32), pltpu.VMEM(p_side.shape, BF16), pltpu.SemaphoreType.DMA((6,))])
    halo_o = lax.ppermute(msg_o, "gy", outside)
    from_west = lax.ppermute(east, "gx", eastward)
    from_east = lax.ppermute(west, "gx", westward)
    halo_e = lax.all_gather(msg_e, "gy", axis_index_groups=cores)
    row_n, for_e_n, message_n = call(
        near_kernel, (own, a, sides, halo_e, halo_o),
        [((near, 3) + bb, F32), ((near, 2) + bb, F32), ((5 * near * B + PAD, B), BF16)])
    message_n = lax.ppermute(message_n, "gy", inside)
    row_f, for_e_f, for_o_f = call(
        far_kernel, (own, a, sides, from_west, from_east),
        [((far, 3) + bb, F32), ((far, 2) + bb, F32), ((2 * far,) + bb, BF16)], cost=20000000000)
    chosen_n, wanted = call(
        choose_near_kernel, (mine, row_n, for_e_n, message_n, halo_e, halo_o, row_f),
        [((3 * near,) + bb, BF16), ((PAD, B), F32)])
    arrived_n = lax.ppermute(chosen_n, "gy", across)
    from_group = lax.ppermute(for_o_f, "gy", between)
    row_f, message_f = call(
        merge_kernel, (row_f, for_e_f, for_o_f, from_group, chosen_n), [((far, 3) + bb, F32), ((7 * far * B, B), BF16)])
    message_f = lax.all_gather(message_f, "gy", axis_index_groups=cores)
    (chosen_f,) = call(choose_far_kernel, (wanted, row_f, for_e_f, message_f), [((3 * far,) + bb, BF16)])
    arrived_f = lax.ppermute(chosen_f, "gy", across)
    shape = (2, 1, 3, 3) + bb
    (out,) = call(
        finish_near_kernel, (mine, row_n, for_e_n, message_n, arrived_n), [(shape, F32)], out_specs=[HBM],
        scratch=[pltpu.VMEM((near, 3) + bb, F32), pltpu.SemaphoreType.DMA((near,))], cost=0)
    (out,) = call(
        finish_far_kernel, (mine, row_f, for_e_f, message_f, arrived_f, out), [(shape, F32)],
        in_specs=[VMEM] * 5 + [HBM], out_specs=[HBM], aliases={5: 0},
        scratch=[pltpu.VMEM((far, 3) + bb, F32), pltpu.SemaphoreType.DMA((far,))])
    return out


def solution(mesh):
    return jax.shard_map(
        on_device,
        mesh=mesh,
        in_specs=(
            P("gx", "gy", None, None, None),
            P("gx", "gy", None),
            P("gx", "gy", None, None),
            P("gx", "gy", None, None, None),
            P("gx", "gy", None),
            P("gx", "gy"),
        ),
        out_specs=P("gx", "gy", None, None, None, None),
        check_vma=False,
    )
```

```python
import jax
import jax.numpy as jnp
from jax import lax
from jax.experimental import pallas as pl
from jax.experimental.pallas import tpu as pltpu
from jax.sharding import PartitionSpec as P

B = 128
PAD = 16
F32 = jnp.float32
BF16 = jnp.bfloat16
VMEM = pl.BlockSpec(memory_space=pltpu.VMEM)
HBM = pl.BlockSpec(memory_space=pltpu.HBM)

A = ((0, 2), (1, 0))
M = ((0, 1), (1, 1))
FAR = ((0, 0), (1, 2))
LINK_TILE = {0: 1, 2: 2}


def call(kernel, args, shapes, in_specs=None, out_specs=None, scratch=(), aliases=None, cost=0):
    return pl.pallas_call(
        kernel,
        in_specs=in_specs or [VMEM] * len(args),
        out_specs=out_specs or [VMEM] * len(shapes),
        out_shape=[jax.ShapeDtypeStruct(shape, dtype) for shape, dtype in shapes],
        scratch_shapes=list(scratch),
        input_output_aliases=aliases or {},
        compiler_params=pltpu.CompilerParams(vmem_limit_bytes=32 * 2**20),
        cost_estimate=pl.CostEstimate(flops=cost, bytes_accessed=cost, transcendentals=0),
    )(*args)


def tile(index):
    return pl.ds(index * B, B)


def dot(a, b):
    return lax.dot_general(a, b, (((1,), (0,)), ((), ())), preferred_element_type=F32)


def dot_t(a, b):
    return lax.dot_general(a, b, (((0,), (0,)), ((), ())), preferred_element_type=F32)


def cat(parts, axis):
    return jnp.concatenate(parts, axis=axis)


def begin_kernel(a_links, p_links, picks, own_in, side_in, a_in,
                 own, a, sides, east, west, msg_o, mine,
                 s_links, s_side, s_picks, raw, sems):
    copies = [
        pltpu.make_async_copy(src, dst, sems.at[i])
        for i, (src, dst) in enumerate(((p_links, s_side), (own_in, own), (side_in, raw), (a_links, s_links),
                                        (picks, s_picks), (a_in, a)))
    ]
    for copy in copies:
        copy.start()
    c = lax.axis_index("gy")
    core = lax.rem(c, 2)
    keep = [c > 0, c < lax.axis_size("gy") - 1]
    for copy in copies[:3]:
        copy.wait()
    for u in range(2):
        for k in range(2):
            factor = jnp.where(keep[k], s_side[u, 0, k], 0).astype(F32).astype(BF16)
            sides[u, k] = raw[u, 0, k] * factor
    for u, message in ((1, east), (0, west)):
        for j in range(4):
            message[j] = own[u, j]
        for k in range(2):
            message[4 + k] = sides[u, k]
    for copy in copies[3:5]:
        copy.wait()
    rows = lax.broadcasted_iota(jnp.int32, (PAD, B), 0)
    codes = jnp.where(rows < PAD // 2, s_picks[0, 0], s_picks[0, 1]).astype(F32)
    mine[...] = codes
    msg_o[pl.ds(14 * B, PAD)] = codes.astype(BF16)
    copies[5].wait()
    for u in range(2):
        for j in range(4):
            for k in range(4):
                a[u, j, k + 1] = a[u, j, k + 1] * s_links[u, j, k].astype(F32).astype(BF16)

    def fill_o(j_o, k_o):
        for u in range(2):
            side, block = sides[u, k_o], own[u, j_o]
            other_side, other_block = sides[1 - u, k_o], own[1 - u, j_o]
            zero = jnp.zeros((B, B), BF16)
            inner = 1 if j_o == 0 else 2
            if j_o == 0:
                right = cat([cat([side, block], 1), cat([zero, own[u, inner]], 1)], 0)
                left = cat([a[u, j_o, 0], a[u, j_o, 4]], 1)
                beyond = a[u, j_o, 3]
                panel = cat([other_side, other_block], 1)
            else:
                right = cat([cat([block, side], 1), cat([own[u, inner], zero], 1)], 0)
                left = cat([a[u, j_o, 0], a[u, j_o, 3]], 1)
                beyond = a[u, j_o, 4]
                panel = cat([other_block, other_side], 1)
            centre = dot(left, right).astype(BF16)
            beside = dot(a[u, j_o, LINK_TILE[A[u][1]]], panel).astype(BF16)
            result = dot_t(side, cat([centre, beyond, beside], 1)).astype(BF16)
            msg_o[tile(7 * u)] = block
            msg_o[tile(7 * u + 1)] = side
            for i in range(5):
                msg_o[tile(7 * u + 2 + i)] = result[:, i * B:(i + 1) * B]

    pl.when(jnp.logical_and(core == 0, keep[0]))(lambda: fill_o(0, 0))
    pl.when(jnp.logical_and(core == 1, keep[1]))(lambda: fill_o(3, 1))


def reduce_units(own, u, products, count):
    firsts, middles, lasts = products
    blocks = cat([own[u, j] for j in range(4)], 0)
    slot1 = dot_t(blocks, cat(middles, 0))
    slot0 = dot_t(own[u, 0], firsts)
    slot2 = dot_t(own[u, 3], lasts)
    return [[value[:, i * B:(i + 1) * B] for i in range(count)] for value in (slot0, slot1, slot2)]


def link_products(a, u, d, tiles, side_tiles):
    k = LINK_TILE[d]
    first = dot(a[u, 0, k], cat([side_tiles[0], tiles[0]], 1)).astype(BF16)
    last = dot(a[u, 3, k], cat([tiles[3], side_tiles[1]], 1)).astype(BF16)
    inner = [dot(a[u, j, k], tiles[j]).astype(BF16) for j in (1, 2)]
    return first[:, :B], [first[:, B:], inner[0], inner[1], last[:, :B]], last[:, B:]


def first_kernel(own, a, sides, halo_o, mine, row, for_e, message):
    core = lax.rem(lax.axis_index("gy"), 2)
    even = core == 0
    message[pl.ds(14 * B, PAD)] = mine[...].astype(BF16)
    message[pl.ds(14 * B + PAD, PAD)] = halo_o[pl.ds(14 * B, PAD)]
    for u, d in A:
        message[tile(10 + 2 * u)] = jnp.where(even, own[u, 3], own[u, 0])
        message[tile(10 + 2 * u + 1)] = jnp.where(even, sides[u, 1], sides[u, 0])
        first, middle, last = link_products(a, u, d, [own[1 - u, j] for j in range(4)],
                                            [sides[1 - u, k] for k in range(2)])
        slots = reduce_units(own, u, (first, middle, last), 1)
        given = dot_t(jnp.where(even, sides[u, 1], sides[u, 0]),
                      cat([jnp.where(even, middle[3], first), jnp.where(even, last, middle[0])], 1))
        emit(core, row, for_e, message, u, [value[0] for value in slots],
             [halo_o[tile(7 * u + 5 + s)].astype(F32) for s in range(2)],
             [given[:, s * B:(s + 1) * B] for s in range(2)])


def emit(core, row, for_e, message, k, slots, extras, given):
    for t in range(3):
        row[k, t] = slots[t]
    for s in range(2):
        row[k, core + s] += extras[s]
        for_e[k, s] = given[s]
        message[tile(5 * k + 3 + s)] = given[s].astype(BF16)
    for t in range(3):
        message[tile(5 * k + t)] = row[k, t].astype(BF16)


def second_kernel(own, a, sides, halo_e, halo_o, started, row, for_e, message):
    del started
    core = lax.rem(lax.axis_index("gy"), 2)
    even = core == 0
    zero = jnp.zeros((B, B), BF16)
    for u in range(2):
        def edge(k):
            from_e, from_o = halo_e[1 - core, tile(10 + 2 * u + k)], halo_o[tile(7 * u + k)]
            return jnp.where(even, from_o, from_e), jnp.where(even, from_e, from_o)

        own_down, own_up = edge(0)
        high_down, low_up = edge(1)
        low, high = sides[u, 0], sides[u, 1]
        o = [own[u, j] for j in range(4)]
        right = [
            [[low, o[0]], [own_down, high_down], [zero, o[1]]],
            [[zero, o[1]], [low, o[0]], [zero, o[2]]],
            [[o[2], zero], [o[1], zero], [o[3], high]],
            [[o[3], high], [o[2], zero], [low_up, own_up]],
        ]
        centre = []
        for j in range(4):
            left = cat([a[u, j, 0], a[u, j, 3], a[u, j, 4]], 1)
            centre.append(dot(left, cat([cat(r, 1) for r in right[j]], 0)).astype(BF16))
        left_part = [value[:, :B] for value in centre]
        right_part = [value[:, B:] for value in centre]
        first, last = left_part[0], right_part[3]
        middle = [right_part[0], right_part[1], left_part[2], left_part[3]]
        slots = [value[0] for value in reduce_units(own, u, (first, middle, last), 1)]
        slots[0] = slots[0] + dot_t(o[1], left_part[1])
        slots[2] = slots[2] + dot_t(o[2], right_part[2])
        beyond = dot(halo_o[tile(7 * u + 4)], cat([jnp.where(even, low, o[3]), jnp.where(even, o[0], high)], 1))
        given = dot_t(jnp.where(even, high, low),
                      cat([jnp.where(even, middle[3], first), jnp.where(even, last, middle[0])], 1))
        emit(core, row, for_e, message, u, slots,
             [halo_o[tile(7 * u + 2 + s)].astype(F32) + beyond[:, s * B:(s + 1) * B] for s in range(2)],
             [given[:, s * B:(s + 1) * B] for s in range(2)])


def far_kernel(own, a, sides, from_east, from_west, started, row, for_e, for_o):
    del started
    even = lax.rem(lax.axis_index("gy"), 2) == 0
    for k, (u, d) in enumerate(FAR):
        arrived = from_west if d == 0 else from_east
        first, middle, last = link_products(a, u, d, [arrived[j] for j in range(4)], [arrived[4], arrived[5]])
        slots = reduce_units(own, u, (first, middle, last), 1)
        down = dot_t(sides[u, 0], cat([first, middle[0]], 1))
        up = dot_t(sides[u, 1], cat([middle[3], last], 1))
        to_e, to_o = jnp.where(even, up, down), jnp.where(even, down, up)
        for t in range(3):
            row[k, t] = slots[t][0]
        for s in range(2):
            at = slice(s * B, (s + 1) * B)
            for_e[k, s] = to_e[:, at]
            for_o[2 * k + s] = to_o[:, at].astype(BF16)


def merge_kernel(row, for_e, for_o, from_group, started, row_out, message):
    del started
    core = lax.rem(lax.axis_index("gy"), 2)
    for k in range(len(FAR)):
        for t in range(3):
            row_out[k, t] = row[k, t]
        for s in range(2):
            row_out[k, core + s] += from_group[2 * k + s].astype(F32)
            message[tile(7 * k + 3 + s)] = for_e[k, s].astype(BF16)
            message[tile(7 * k + 5 + s)] = for_o[2 * k + s]
        for t in range(3):
            message[tile(7 * k + t)] = row_out[k, t].astype(BF16)


def far_tiles(core, half, row, for_e, message, k, t):
    def theirs_at(i):
        return message[1 - core, tile(7 * k + i)].astype(F32)

    def slot(get, shift):
        if t == 1:
            return get(1 - shift)
        return jnp.where(shift == t // 2, get(t // 2), 0.0)

    mine = row[k, t] + slot(lambda s: theirs_at(3 + s), 1 - core)
    theirs = theirs_at(t) + slot(lambda s: for_e[k, s], core)
    inner = slot(lambda s: message[1 - half, tile(7 * k + 5 + s)].astype(F32), half)
    return mine, theirs, inner


def complete(core, row, for_e, message, k, t):
    def theirs_at(i):
        return message[1 - core, tile(5 * k + i)].astype(F32)

    mine = row[k, t]
    theirs = theirs_at(t)
    if t == 1:
        mine = mine + theirs_at(3 + core)
        theirs = theirs + for_e[k, 1 - core]
    else:
        gets = (core == 0) == (t == 2)
        s = 1 if t == 2 else 0
        mine = mine + jnp.where(gets, theirs_at(3 + s), 0.0)
        theirs = theirs + jnp.where(gets, 0.0, for_e[k, s])
    return mine, theirs


def masks(codes, u, position, core):
    code = codes[u * PAD // 2:u * PAD // 2 + 1]
    other = position + 1 - 2 * core
    return (jnp.broadcast_to(code == position.astype(F32), (B, B)),
            jnp.broadcast_to(code == other.astype(F32), (B, B)))


def choose(units, core, position, codes, row, for_e, message, out):
    for k, (u, _) in enumerate(units):
        use_mine, use_theirs = masks(codes, u, position, core)
        for t in range(3):
            own_row, other_row = complete(core, row, for_e, message, k, t)
            out[3 * k + t] = jnp.where(use_mine, own_row, jnp.where(use_theirs, other_row, 0.0)).astype(BF16)


def choose_first_kernel(mine, row, for_e, message, halo_o, out, wanted):
    c = lax.axis_index("gy")
    core, position = lax.rem(c, 2), lax.rem(c, 4)
    outer = jnp.logical_or(position == 0, position == 3)
    inferred = 6.0 - mine[...] - message[1 - core, pl.ds(14 * B, PAD)].astype(F32)
    inferred = inferred - halo_o[pl.ds(14 * B, PAD)].astype(F32)
    codes = jnp.where(outer, message[1 - core, pl.ds(14 * B + PAD, PAD)].astype(F32), inferred)
    wanted[...] = codes
    choose(A, core, position, codes, row, for_e, message, out)


def choose_second_kernel(wanted, row, for_e, message, out):
    c = lax.axis_index("gy")
    choose(M, lax.rem(c, 2), lax.rem(c, 4), wanted[...], row, for_e, message, out)


def choose_far_kernel(wanted, row, for_e, message, out):
    c = lax.axis_index("gy")
    core, position = lax.rem(c, 2), lax.rem(c, 4)
    for k, (u, _) in enumerate(FAR):
        use_mine, use_theirs = masks(wanted[...], u, position, core)
        for t in range(3):
            mine, theirs, inner = far_tiles(core, position // 2, row, for_e, message, k, t)
            out[3 * k + t] = jnp.where(use_mine, mine, jnp.where(use_theirs, theirs, inner)).astype(BF16)


def finish_near_kernel(mine, row_a, for_e_a, message_a, arrived_a, row_m, for_e_m, message_m, arrived_m,
                       out, buffer, sems):
    c = lax.axis_index("gy")
    core, position = lax.rem(c, 2), lax.rem(c, 4)
    copies = []
    for units, row, for_e, message, arrived in ((A, row_a, for_e_a, message_a, arrived_a),
                                                (M, row_m, for_e_m, message_m, arrived_m)):
        for k, (u, d) in enumerate(units):
            use_mine, use_theirs = masks(mine[...], u, position, core)
            at = len(copies)
            for t in range(3):
                own_row, other_row = complete(core, row, for_e, message, k, t)
                got = arrived[3 * k + t].astype(F32)
                buffer[at, t] = jnp.where(use_mine, own_row, jnp.where(use_theirs, other_row, got))
            copies.append(pltpu.make_async_copy(buffer.at[at], out.at[u, 0, d], sems.at[at]))
            copies[-1].start()
    for copy in copies:
        copy.wait()


def finish_far_kernel(mine, row, for_e, message, arrived, started, out, buffer, sems):
    del started
    c = lax.axis_index("gy")
    core, position = lax.rem(c, 2), lax.rem(c, 4)
    half = position // 2
    copies = []
    for k, (u, d) in enumerate(FAR):
        use_mine, use_theirs = masks(mine[...], u, position, core)
        code = mine[u * PAD // 2:u * PAD // 2 + 1]
        add_arrived = jnp.broadcast_to(code == (1 + half).astype(F32), (B, B))
        add_inner = jnp.broadcast_to(code == (2 - half).astype(F32), (B, B))
        for t in range(3):
            own_row, other_row, inner = far_tiles(core, half, row, for_e, message, k, t)
            got = arrived[3 * k + t].astype(F32)
            here = jnp.where(use_mine, own_row, other_row) + jnp.where(add_arrived, got, 0.0)
            there = got + jnp.where(add_inner, inner, 0.0)
            buffer[k, t] = jnp.where(jnp.logical_or(use_mine, use_theirs), here, there)
        copies.append(pltpu.make_async_copy(buffer.at[k], out.at[u, 0, d], sems.at[k]))
        copies[-1].start()
    for copy in copies:
        copy.wait()


def on_device(a_tiles, a_links, p_own, p_side, p_links, coarse_pick):
    count, columns = lax.axis_size("gy"), lax.axis_size("gx")
    pairs = [(2 * g, 2 * g + 1) for g in range(count // 2)]
    cores = [list(pair) for pair in pairs]
    inside = pairs + [(b, a) for a, b in pairs]
    outside = [(i + 1, i + 2) for i in range(0, count - 2, 2)]
    outside = outside + [(b, a) for a, b in outside]
    between = [(i, i + 1) for i in range(3, count - 1, 4)]
    between = between + [(b, a) for a, b in between]
    across = [(i, i ^ 2) for i in range(count)]
    eastward = [(i, i + 1) for i in range(columns - 1)]
    westward = [(b, a) for a, b in eastward]
    bb = (B, B)
    pair, six = ((2, 3) + bb, F32), ((6,) + bb, BF16)
    give = ((2, 2) + bb, F32)
    four = ((4,) + bb, BF16)

    own, a, sides, east, west, msg_o, mine = call(
        begin_kernel,
        [pltpu.with_memory_space_constraint(x, pltpu.HBM)
         for x in (a_links, p_links, coarse_pick.T, p_own, p_side, a_tiles)],
        [(p_own.shape, BF16), (a_tiles.shape, BF16), ((2, 2) + bb, BF16), six, six,
         ((14 * B + PAD, B), BF16), ((PAD, B), F32)],
        in_specs=[HBM] * 6,
        scratch=[pltpu.SMEM(a_links.shape, jnp.int32), pltpu.SMEM(p_links.shape, jnp.int32),
                 pltpu.SMEM((1, 2), jnp.int32), pltpu.VMEM(p_side.shape, BF16), pltpu.SemaphoreType.DMA((6,))])
    from_east = lax.ppermute(west, "gx", westward)
    from_west = lax.ppermute(east, "gx", eastward)
    halo_o = lax.ppermute(msg_o, "gy", outside)

    row_a, for_e_a, message_a = call(
        first_kernel, (own, a, sides, halo_o, mine), [pair, give, ((14 * B + 2 * PAD, B), BF16)])
    message_a = lax.all_gather(message_a, "gy", axis_index_groups=cores)
    chosen_a, wanted = call(
        choose_first_kernel, (mine, row_a, for_e_a, message_a, halo_o), [six, ((PAD, B), F32)])
    arrived_a = lax.ppermute(chosen_a, "gy", across)

    row_f, for_e_f, for_o_f = call(
        far_kernel, (own, a, sides, from_east, from_west, chosen_a), [pair, give, four], cost=0)
    from_group = lax.ppermute(for_o_f, "gy", between)

    row_m, for_e_m, message_m = call(
        second_kernel, (own, a, sides, message_a, halo_o, row_f), [pair, give, ((10 * B, B), BF16)], cost=0)
    message_m = lax.all_gather(message_m, "gy", axis_index_groups=cores)
    (chosen_m,) = call(choose_second_kernel, (wanted, row_m, for_e_m, message_m), [six])
    arrived_m = lax.ppermute(chosen_m, "gy", across)

    row_f, message_f = call(
        merge_kernel, (row_f, for_e_f, for_o_f, from_group, arrived_a), [pair, ((14 * B, B), BF16)])
    message_f = lax.all_gather(message_f, "gy", axis_index_groups=cores)
    (chosen_f,) = call(choose_far_kernel, (wanted, row_f, for_e_f, message_f), [six])
    arrived_f = lax.ppermute(chosen_f, "gy", across)

    shape = (2, 1, 3, 3) + bb
    (out,) = call(
        finish_near_kernel, (mine, row_a, for_e_a, message_a, arrived_a, row_m, for_e_m, message_m, arrived_m),
        [(shape, F32)], out_specs=[HBM], cost=0,
        scratch=[pltpu.VMEM((4, 3) + bb, F32), pltpu.SemaphoreType.DMA((4,))])
    (out,) = call(
        finish_far_kernel, (mine, row_f, for_e_f, message_f, arrived_f, out), [(shape, F32)],
        in_specs=[VMEM] * 5 + [HBM], out_specs=[HBM], aliases={5: 0},
        scratch=[pltpu.VMEM((2, 3) + bb, F32), pltpu.SemaphoreType.DMA((2,))])
    return out


def solution(mesh):
    return jax.shard_map(
        on_device,
        mesh=mesh,
        in_specs=(
            P("gx", "gy", None, None, None),
            P("gx", "gy", None),
            P("gx", "gy", None, None),
            P("gx", "gy", None, None, None),
            P("gx", "gy", None),
            P("gx", "gy"),
        ),
        out_specs=P("gx", "gy", None, None, None, None),
        check_vma=False,
    )
```

```python
import jax
import jax.numpy as jnp
from jax import lax
from jax.experimental import pallas as pl
from jax.experimental.pallas import tpu as pltpu
from jax.sharding import PartitionSpec as P

B = 128
PAD = 16
F32 = jnp.float32
BF16 = jnp.bfloat16
VMEM = pl.BlockSpec(memory_space=pltpu.VMEM)
HBM = pl.BlockSpec(memory_space=pltpu.HBM)

A = ((0, 2), (1, 0))
M = ((0, 1), (1, 1))
FAR = ((0, 0), (1, 2))
LINK_TILE = {0: 1, 2: 2}


def call(kernel, args, shapes, in_specs=None, out_specs=None, scratch=(), aliases=None, cost=0):
    return pl.pallas_call(
        kernel,
        in_specs=in_specs or [VMEM] * len(args),
        out_specs=out_specs or [VMEM] * len(shapes),
        out_shape=[jax.ShapeDtypeStruct(shape, dtype) for shape, dtype in shapes],
        scratch_shapes=list(scratch),
        input_output_aliases=aliases or {},
        compiler_params=pltpu.CompilerParams(vmem_limit_bytes=32 * 2**20),
        cost_estimate=pl.CostEstimate(flops=cost, bytes_accessed=cost, transcendentals=0),
    )(*args)


def tile(index):
    return pl.ds(index * B, B)


def dot(a, b):
    return lax.dot_general(a, b, (((1,), (0,)), ((), ())), preferred_element_type=F32)


def dot_t(a, b):
    return lax.dot_general(a, b, (((0,), (0,)), ((), ())), preferred_element_type=F32)


def cat(parts, axis):
    return jnp.concatenate(parts, axis=axis)


def begin_kernel(a_links, p_links, picks, own_in, side_in, a_in,
                 own, a, sides, east, west, msg_o, mine,
                 s_links, s_side, s_picks, raw, sems):
    copies = [
        pltpu.make_async_copy(src, dst, sems.at[i])
        for i, (src, dst) in enumerate(((p_links, s_side), (own_in, own), (side_in, raw), (a_links, s_links),
                                        (picks, s_picks), (a_in, a)))
    ]
    for copy in copies:
        copy.start()
    c = lax.axis_index("gy")
    core = lax.rem(c, 2)
    keep = [c > 0, c < lax.axis_size("gy") - 1]
    for copy in copies[:3]:
        copy.wait()
    for u in range(2):
        for k in range(2):
            factor = jnp.where(keep[k], s_side[u, 0, k], 0).astype(F32).astype(BF16)
            sides[u, k] = raw[u, 0, k] * factor
    for u, message in ((1, east), (0, west)):
        for j in range(4):
            message[j] = own[u, j]
        for k in range(2):
            message[4 + k] = sides[u, k]
    for copy in copies[3:5]:
        copy.wait()
    rows = lax.broadcasted_iota(jnp.int32, (PAD, B), 0)
    codes = jnp.where(rows < PAD // 2, s_picks[0, 0], s_picks[0, 1]).astype(F32)
    mine[...] = codes
    msg_o[pl.ds(14 * B, PAD)] = codes.astype(BF16)
    copies[5].wait()
    for u in range(2):
        for j in range(4):
            for k in range(4):
                a[u, j, k + 1] = a[u, j, k + 1] * s_links[u, j, k].astype(F32).astype(BF16)

    def fill_o(j_o, k_o):
        for u in range(2):
            side, block = sides[u, k_o], own[u, j_o]
            other_side, other_block = sides[1 - u, k_o], own[1 - u, j_o]
            zero = jnp.zeros((B, B), BF16)
            inner = 1 if j_o == 0 else 2
            if j_o == 0:
                right = cat([cat([side, block], 1), cat([zero, own[u, inner]], 1)], 0)
                left = cat([a[u, j_o, 0], a[u, j_o, 4]], 1)
                beyond = a[u, j_o, 3]
                panel = cat([other_side, other_block], 1)
            else:
                right = cat([cat([block, side], 1), cat([own[u, inner], zero], 1)], 0)
                left = cat([a[u, j_o, 0], a[u, j_o, 3]], 1)
                beyond = a[u, j_o, 4]
                panel = cat([other_block, other_side], 1)
            centre = dot(left, right).astype(BF16)
            beside = dot(a[u, j_o, LINK_TILE[A[u][1]]], panel).astype(BF16)
            result = dot_t(side, cat([centre, beyond, beside], 1)).astype(BF16)
            msg_o[tile(7 * u)] = block
            msg_o[tile(7 * u + 1)] = side
            for i in range(5):
                msg_o[tile(7 * u + 2 + i)] = result[:, i * B:(i + 1) * B]

    pl.when(jnp.logical_and(core == 0, keep[0]))(lambda: fill_o(0, 0))
    pl.when(jnp.logical_and(core == 1, keep[1]))(lambda: fill_o(3, 1))


def reduce_units(own, u, products, count):
    firsts, middles, lasts = products
    blocks = cat([own[u, j] for j in range(4)], 0)
    slot1 = dot_t(blocks, cat(middles, 0))
    slot0 = dot_t(own[u, 0], firsts)
    slot2 = dot_t(own[u, 3], lasts)
    return [[value[:, i * B:(i + 1) * B] for i in range(count)] for value in (slot0, slot1, slot2)]


def link_products(a, u, d, tiles, side_tiles):
    k = LINK_TILE[d]
    first = dot(a[u, 0, k], cat([side_tiles[0], tiles[0]], 1)).astype(BF16)
    last = dot(a[u, 3, k], cat([tiles[3], side_tiles[1]], 1)).astype(BF16)
    inner = [dot(a[u, j, k], tiles[j]).astype(BF16) for j in (1, 2)]
    return first[:, :B], [first[:, B:], inner[0], inner[1], last[:, :B]], last[:, B:]


def first_kernel(own, a, sides, halo_o, mine, row, for_e, message):
    core = lax.rem(lax.axis_index("gy"), 2)
    even = core == 0
    message[pl.ds(14 * B, PAD)] = mine[...].astype(BF16)
    message[pl.ds(14 * B + PAD, PAD)] = halo_o[pl.ds(14 * B, PAD)]
    for u, d in A:
        message[tile(10 + 2 * u)] = jnp.where(even, own[u, 3], own[u, 0])
        message[tile(10 + 2 * u + 1)] = jnp.where(even, sides[u, 1], sides[u, 0])
        first, middle, last = link_products(a, u, d, [own[1 - u, j] for j in range(4)],
                                            [sides[1 - u, k] for k in range(2)])
        slots = reduce_units(own, u, (first, middle, last), 1)
        given = dot_t(jnp.where(even, sides[u, 1], sides[u, 0]),
                      cat([jnp.where(even, middle[3], first), jnp.where(even, last, middle[0])], 1))
        emit(core, row, for_e, message, u, [value[0] for value in slots],
             [halo_o[tile(7 * u + 5 + s)].astype(F32) for s in range(2)],
             [given[:, s * B:(s + 1) * B] for s in range(2)])


def emit(core, row, for_e, message, k, slots, extras, given):
    for t in range(3):
        row[k, t] = slots[t]
    for s in range(2):
        row[k, core + s] += extras[s]
        for_e[k, s] = given[s]
        message[tile(5 * k + 3 + s)] = given[s].astype(BF16)
    for t in range(3):
        message[tile(5 * k + t)] = row[k, t].astype(BF16)


def second_kernel(own, a, sides, halo_e, halo_o, started, row, for_e, message):
    del started
    core = lax.rem(lax.axis_index("gy"), 2)
    even = core == 0
    zero = jnp.zeros((B, B), BF16)
    for u in range(2):
        def edge(k):
            from_e, from_o = halo_e[1 - core, tile(10 + 2 * u + k)], halo_o[tile(7 * u + k)]
            return jnp.where(even, from_o, from_e), jnp.where(even, from_e, from_o)

        own_down, own_up = edge(0)
        high_down, low_up = edge(1)
        low, high = sides[u, 0], sides[u, 1]
        o = [own[u, j] for j in range(4)]
        right = [
            [[low, o[0]], [own_down, high_down], [zero, o[1]]],
            [[zero, o[1]], [low, o[0]], [zero, o[2]]],
            [[o[2], zero], [o[1], zero], [o[3], high]],
            [[o[3], high], [o[2], zero], [low_up, own_up]],
        ]
        centre = []
        for j in range(4):
            left = cat([a[u, j, 0], a[u, j, 3], a[u, j, 4]], 1)
            centre.append(dot(left, cat([cat(r, 1) for r in right[j]], 0)).astype(BF16))
        left_part = [value[:, :B] for value in centre]
        right_part = [value[:, B:] for value in centre]
        first, last = left_part[0], right_part[3]
        middle = [right_part[0], right_part[1], left_part[2], left_part[3]]
        slots = [value[0] for value in reduce_units(own, u, (first, middle, last), 1)]
        slots[0] = slots[0] + dot_t(o[1], left_part[1])
        slots[2] = slots[2] + dot_t(o[2], right_part[2])
        beyond = dot(halo_o[tile(7 * u + 4)], cat([jnp.where(even, low, o[3]), jnp.where(even, o[0], high)], 1))
        given = dot_t(jnp.where(even, high, low),
                      cat([jnp.where(even, middle[3], first), jnp.where(even, last, middle[0])], 1))
        emit(core, row, for_e, message, u, slots,
             [halo_o[tile(7 * u + 2 + s)].astype(F32) + beyond[:, s * B:(s + 1) * B] for s in range(2)],
             [given[:, s * B:(s + 1) * B] for s in range(2)])


def far_kernel(own, a, sides, from_west, from_east, started, row, for_e, for_o):
    del started
    even = lax.rem(lax.axis_index("gy"), 2) == 0
    for k, (u, d) in enumerate(FAR):
        arrived = from_west if d == 0 else from_east
        first, middle, last = link_products(a, u, d, [arrived[j] for j in range(4)], [arrived[4], arrived[5]])
        slots = reduce_units(own, u, (first, middle, last), 1)
        down = dot_t(sides[u, 0], cat([first, middle[0]], 1))
        up = dot_t(sides[u, 1], cat([middle[3], last], 1))
        to_e, to_o = jnp.where(even, up, down), jnp.where(even, down, up)
        for t in range(3):
            row[k, t] = slots[t][0]
        for s in range(2):
            at = slice(s * B, (s + 1) * B)
            for_e[k, s] = to_e[:, at]
            for_o[2 * k + s] = to_o[:, at].astype(BF16)


def merge_kernel(row, for_e, for_o, from_group, started, chosen, row_out, message):
    del started, chosen
    core = lax.rem(lax.axis_index("gy"), 2)
    for k in range(len(FAR)):
        for t in range(3):
            row_out[k, t] = row[k, t]
        for s in range(2):
            row_out[k, core + s] += from_group[2 * k + s].astype(F32)
            message[tile(7 * k + 3 + s)] = for_e[k, s].astype(BF16)
            message[tile(7 * k + 5 + s)] = for_o[2 * k + s]
        for t in range(3):
            message[tile(7 * k + t)] = row_out[k, t].astype(BF16)


def far_tiles(core, half, row, for_e, message, k, t):
    def theirs_at(i):
        return message[1 - core, tile(7 * k + i)].astype(F32)

    def slot(get, shift):
        if t == 1:
            return get(1 - shift)
        return jnp.where(shift == t // 2, get(t // 2), 0.0)

    mine = row[k, t] + slot(lambda s: theirs_at(3 + s), 1 - core)
    theirs = theirs_at(t) + slot(lambda s: for_e[k, s], core)
    inner = slot(lambda s: message[1 - half, tile(7 * k + 5 + s)].astype(F32), half)
    return mine, theirs, inner


def complete(core, row, for_e, message, k, t):
    def theirs_at(i):
        value = message[1 - core, tile(5 * k + i)] if len(message.shape) == 3 else message[tile(5 * k + i)]
        return value.astype(F32)

    mine = row[k, t]
    theirs = theirs_at(t)
    if t == 1:
        mine = mine + theirs_at(3 + core)
        theirs = theirs + for_e[k, 1 - core]
    else:
        gets = (core == 0) == (t == 2)
        s = 1 if t == 2 else 0
        mine = mine + jnp.where(gets, theirs_at(3 + s), 0.0)
        theirs = theirs + jnp.where(gets, 0.0, for_e[k, s])
    return mine, theirs


def masks(codes, u, position, core):
    code = codes[u * PAD // 2:u * PAD // 2 + 1]
    other = position + 1 - 2 * core
    return (jnp.broadcast_to(code == position.astype(F32), (B, B)),
            jnp.broadcast_to(code == other.astype(F32), (B, B)))


def choose(units, core, position, codes, row, for_e, message, out):
    for k, (u, _) in enumerate(units):
        use_mine, use_theirs = masks(codes, u, position, core)
        for t in range(3):
            own_row, other_row = complete(core, row, for_e, message, k, t)
            out[3 * k + t] = jnp.where(use_mine, own_row, jnp.where(use_theirs, other_row, 0.0)).astype(BF16)


def choose_first_kernel(mine, row, for_e, message, halo_o, out, wanted):
    c = lax.axis_index("gy")
    core, position = lax.rem(c, 2), lax.rem(c, 4)
    outer = jnp.logical_or(position == 0, position == 3)
    inferred = 6.0 - mine[...] - message[1 - core, pl.ds(14 * B, PAD)].astype(F32)
    inferred = inferred - halo_o[pl.ds(14 * B, PAD)].astype(F32)
    codes = jnp.where(outer, message[1 - core, pl.ds(14 * B + PAD, PAD)].astype(F32), inferred)
    wanted[...] = codes
    choose(A, core, position, codes, row, for_e, message, out)


def choose_second_kernel(wanted, row, for_e, message, started, out):
    del started
    c = lax.axis_index("gy")
    choose(M, lax.rem(c, 2), lax.rem(c, 4), wanted[...], row, for_e, message, out)


def choose_far_kernel(wanted, row, for_e, message, out):
    c = lax.axis_index("gy")
    core, position = lax.rem(c, 2), lax.rem(c, 4)
    for k, (u, _) in enumerate(FAR):
        use_mine, use_theirs = masks(wanted[...], u, position, core)
        for t in range(3):
            mine, theirs, inner = far_tiles(core, position // 2, row, for_e, message, k, t)
            out[3 * k + t] = jnp.where(use_mine, mine, jnp.where(use_theirs, theirs, inner)).astype(BF16)


def finish_near_kernel(mine, row_a, for_e_a, message_a, arrived_a, row_m, for_e_m, message_m, arrived_m,
                       out, buffer, sems):
    c = lax.axis_index("gy")
    core, position = lax.rem(c, 2), lax.rem(c, 4)
    copies = []
    for units, row, for_e, message, arrived in ((A, row_a, for_e_a, message_a, arrived_a),
                                                (M, row_m, for_e_m, message_m, arrived_m)):
        for k, (u, d) in enumerate(units):
            use_mine, use_theirs = masks(mine[...], u, position, core)
            at = len(copies)
            for t in range(3):
                own_row, other_row = complete(core, row, for_e, message, k, t)
                got = arrived[3 * k + t].astype(F32)
                buffer[at, t] = jnp.where(use_mine, own_row, jnp.where(use_theirs, other_row, got))
            copies.append(pltpu.make_async_copy(buffer.at[at], out.at[u, 0, d], sems.at[at]))
            copies[-1].start()
    for copy in copies:
        copy.wait()


def finish_far_kernel(mine, row, for_e, message, arrived, started, out, buffer, sems):
    del started
    c = lax.axis_index("gy")
    core, position = lax.rem(c, 2), lax.rem(c, 4)
    half = position // 2
    copies = []
    for k, (u, d) in enumerate(FAR):
        use_mine, use_theirs = masks(mine[...], u, position, core)
        code = mine[u * PAD // 2:u * PAD // 2 + 1]
        add_arrived = jnp.broadcast_to(code == (1 + half).astype(F32), (B, B))
        add_inner = jnp.broadcast_to(code == (2 - half).astype(F32), (B, B))
        for t in range(3):
            own_row, other_row, inner = far_tiles(core, half, row, for_e, message, k, t)
            got = arrived[3 * k + t].astype(F32)
            here = jnp.where(use_mine, own_row, other_row) + jnp.where(add_arrived, got, 0.0)
            there = got + jnp.where(add_inner, inner, 0.0)
            buffer[k, t] = jnp.where(jnp.logical_or(use_mine, use_theirs), here, there)
        copies.append(pltpu.make_async_copy(buffer.at[k], out.at[u, 0, d], sems.at[k]))
        copies[-1].start()
    for copy in copies:
        copy.wait()


def on_device(a_tiles, a_links, p_own, p_side, p_links, coarse_pick):
    count, columns = lax.axis_size("gy"), lax.axis_size("gx")
    pairs = [(2 * g, 2 * g + 1) for g in range(count // 2)]
    cores = [list(pair) for pair in pairs]
    inside = pairs + [(b, a) for a, b in pairs]
    outside = [(i + 1, i + 2) for i in range(0, count - 2, 2)]
    outside = outside + [(b, a) for a, b in outside]
    between = [(i, i + 1) for i in range(3, count - 1, 4)]
    between = between + [(b, a) for a, b in between]
    across = [(i, i ^ 2) for i in range(count)]
    eastward = [(i, i + 1) for i in range(columns - 1)]
    westward = [(b, a) for a, b in eastward]
    bb = (B, B)
    pair, six = ((2, 3) + bb, F32), ((6,) + bb, BF16)
    give = ((2, 2) + bb, F32)
    four = ((4,) + bb, BF16)

    own, a, sides, east, west, msg_o, mine = call(
        begin_kernel,
        [pltpu.with_memory_space_constraint(x, pltpu.HBM)
         for x in (a_links, p_links, coarse_pick.T, p_own, p_side, a_tiles)],
        [(p_own.shape, BF16), (a_tiles.shape, BF16), ((2, 2) + bb, BF16), six, six,
         ((14 * B + PAD, B), BF16), ((PAD, B), F32)],
        in_specs=[HBM] * 6,
        scratch=[pltpu.SMEM(a_links.shape, jnp.int32), pltpu.SMEM(p_links.shape, jnp.int32),
                 pltpu.SMEM((1, 2), jnp.int32), pltpu.VMEM(p_side.shape, BF16), pltpu.SemaphoreType.DMA((6,))])
    from_east = lax.ppermute(west, "gx", westward)
    from_west = lax.ppermute(east, "gx", eastward)
    halo_o = lax.ppermute(msg_o, "gy", outside)

    row_a, for_e_a, message_a = call(
        first_kernel, (own, a, sides, halo_o, mine), [pair, give, ((14 * B + 2 * PAD, B), BF16)])
    message_a = lax.all_gather(message_a, "gy", axis_index_groups=cores)
    chosen_a, wanted = call(
        choose_first_kernel, (mine, row_a, for_e_a, message_a, halo_o), [six, ((PAD, B), F32)])
    arrived_a = lax.ppermute(chosen_a, "gy", across)

    row_m, for_e_m, message_m = call(
        second_kernel, (own, a, sides, message_a, halo_o, chosen_a), [pair, give, ((10 * B, B), BF16)], cost=0)
    message_m = lax.ppermute(message_m, "gy", inside)
    row_f, for_e_f, for_o_f = call(
        far_kernel, (own, a, sides, from_west, from_east, row_m), [pair, give, four], cost=20000000000)
    from_group = lax.ppermute(for_o_f, "gy", between)

    (chosen_m,) = call(choose_second_kernel, (wanted, row_m, for_e_m, message_m, row_f), [six])
    arrived_m = lax.ppermute(chosen_m, "gy", across)

    row_f, message_f = call(
        merge_kernel, (row_f, for_e_f, for_o_f, from_group, arrived_a, chosen_m), [pair, ((14 * B, B), BF16)])
    message_f = lax.all_gather(message_f, "gy", axis_index_groups=cores)
    (chosen_f,) = call(choose_far_kernel, (wanted, row_f, for_e_f, message_f), [six])
    arrived_f = lax.ppermute(chosen_f, "gy", across)

    shape = (2, 1, 3, 3) + bb
    (out,) = call(
        finish_near_kernel, (mine, row_a, for_e_a, message_a, arrived_a, row_m, for_e_m, message_m, arrived_m),
        [(shape, F32)], out_specs=[HBM], cost=0,
        scratch=[pltpu.VMEM((4, 3) + bb, F32), pltpu.SemaphoreType.DMA((4,))])
    (out,) = call(
        finish_far_kernel, (mine, row_f, for_e_f, message_f, arrived_f, out), [(shape, F32)],
        in_specs=[VMEM] * 5 + [HBM], out_specs=[HBM], aliases={5: 0},
        scratch=[pltpu.VMEM((2, 3) + bb, F32), pltpu.SemaphoreType.DMA((2,))])
    return out


def solution(mesh):
    return jax.shard_map(
        on_device,
        mesh=mesh,
        in_specs=(
            P("gx", "gy", None, None, None),
            P("gx", "gy", None),
            P("gx", "gy", None, None),
            P("gx", "gy", None, None, None),
            P("gx", "gy", None),
            P("gx", "gy"),
        ),
        out_specs=P("gx", "gy", None, None, None, None),
        check_vma=False,
    )
```

```python
import jax
import jax.numpy as jnp
from jax import lax
from jax.experimental import pallas as pl
from jax.experimental.pallas import tpu as pltpu
from jax.sharding import PartitionSpec as P

B = 128
PAD = 16
F32 = jnp.float32
BF16 = jnp.bfloat16
VMEM = pl.BlockSpec(memory_space=pltpu.VMEM)
HBM = pl.BlockSpec(memory_space=pltpu.HBM)

NEAR = ((0, 2), (0, 1), (1, 0), (1, 1))
FAR = ((0, 0), (1, 2))
LINK_TILE = {0: 1, 2: 2}


def call(kernel, args, shapes, in_specs=None, out_specs=None, scratch=(), aliases=None, cost=0):
    return pl.pallas_call(
        kernel,
        in_specs=in_specs or [VMEM] * len(args),
        out_specs=out_specs or [VMEM] * len(shapes),
        out_shape=[jax.ShapeDtypeStruct(shape, dtype) for shape, dtype in shapes],
        scratch_shapes=list(scratch),
        input_output_aliases=aliases or {},
        compiler_params=pltpu.CompilerParams(vmem_limit_bytes=32 * 2**20),
        cost_estimate=pl.CostEstimate(flops=cost, bytes_accessed=cost, transcendentals=0),
    )(*args)


def tile(index):
    return pl.ds(index * B, B)


def dot(a, b):
    return lax.dot_general(a, b, (((1,), (0,)), ((), ())), preferred_element_type=F32)


def dot_t(a, b):
    return lax.dot_general(a, b, (((0,), (0,)), ((), ())), preferred_element_type=F32)


def cat(parts, axis):
    return jnp.concatenate(parts, axis=axis)


def begin_kernel(a_links, p_links, picks, own_in, side_in, a_in,
                 own, a, sides, east, west, msg_o, msg_e, mine,
                 s_links, s_side, s_picks, raw, sems):
    copies = [
        pltpu.make_async_copy(src, dst, sems.at[i])
        for i, (src, dst) in enumerate(((p_links, s_side), (own_in, own), (side_in, raw), (a_links, s_links),
                                        (picks, s_picks), (a_in, a)))
    ]
    for copy in copies:
        copy.start()
    c = lax.axis_index("gy")
    core = lax.rem(c, 2)
    keep = [c > 0, c < lax.axis_size("gy") - 1]
    for copy in copies[:3]:
        copy.wait()
    for u in range(2):
        for k in range(2):
            factor = jnp.where(keep[k], s_side[u, 0, k], 0).astype(F32).astype(BF16)
            sides[u, k] = raw[u, 0, k] * factor
    for u, message in ((1, east), (0, west)):
        for j in range(4):
            message[j] = own[u, j]
        for k in range(2):
            message[4 + k] = sides[u, k]
    for copy in copies[3:5]:
        copy.wait()
    rows = lax.broadcasted_iota(jnp.int32, (PAD, B), 0)
    codes = jnp.where(rows < PAD // 2, s_picks[0, 0], s_picks[0, 1]).astype(F32)
    mine[...] = codes
    msg_o[pl.ds(14 * B, PAD)] = codes.astype(BF16)
    msg_e[pl.ds(4 * B, PAD)] = codes.astype(BF16)
    copies[5].wait()
    for u in range(2):
        for j in range(4):
            for k in range(4):
                a[u, j, k + 1] = a[u, j, k + 1] * s_links[u, j, k].astype(F32).astype(BF16)

    def fill_e(j, k):
        for u in range(2):
            msg_e[tile(2 * u)] = own[u, j]
            msg_e[tile(2 * u + 1)] = sides[u, k]

    def fill_o(j_o, k_o):
        for u in range(2):
            side, block = sides[u, k_o], own[u, j_o]
            other_side, other_block = sides[1 - u, k_o], own[1 - u, j_o]
            zero = jnp.zeros((B, B), BF16)
            inner = 1 if j_o == 0 else 2
            if j_o == 0:
                right = cat([cat([side, block], 1), cat([zero, own[u, inner]], 1)], 0)
                left = cat([a[u, j_o, 0], a[u, j_o, 4]], 1)
                beyond = a[u, j_o, 3]
                panel = cat([other_side, other_block], 1)
            else:
                right = cat([cat([block, side], 1), cat([own[u, inner], zero], 1)], 0)
                left = cat([a[u, j_o, 0], a[u, j_o, 3]], 1)
                beyond = a[u, j_o, 4]
                panel = cat([other_block, other_side], 1)
            centre = dot(left, right).astype(BF16)
            beside = dot(a[u, j_o, LINK_TILE[NEAR[2 * u][1]]], panel).astype(BF16)
            result = dot_t(side, cat([centre, beyond, beside], 1)).astype(BF16)
            msg_o[tile(7 * u)] = block
            msg_o[tile(7 * u + 1)] = side
            for i in range(5):
                msg_o[tile(7 * u + 2 + i)] = result[:, i * B:(i + 1) * B]

    pl.when(core == 0)(lambda: fill_e(3, 1))
    pl.when(core == 1)(lambda: fill_e(0, 0))
    pl.when(jnp.logical_and(core == 0, keep[0]))(lambda: fill_o(0, 0))
    pl.when(jnp.logical_and(core == 1, keep[1]))(lambda: fill_o(3, 1))


def reduce_units(own, u, products, count):
    firsts, middles, lasts = products
    blocks = cat([own[u, j] for j in range(4)], 0)
    slot1 = dot_t(blocks, cat(middles, 0))
    slot0 = dot_t(own[u, 0], firsts)
    slot2 = dot_t(own[u, 3], lasts)
    return [[value[:, i * B:(i + 1) * B] for i in range(count)] for value in (slot0, slot1, slot2)]


def link_products(a, u, d, tiles, side_tiles):
    k = LINK_TILE[d]
    first = dot(a[u, 0, k], cat([side_tiles[0], tiles[0]], 1)).astype(BF16)
    last = dot(a[u, 3, k], cat([tiles[3], side_tiles[1]], 1)).astype(BF16)
    inner = [dot(a[u, j, k], tiles[j]).astype(BF16) for j in (1, 2)]
    return first[:, :B], [first[:, B:], inner[0], inner[1], last[:, :B]], last[:, B:]


def near_kernel(own, a, sides, halo_e, halo_o, row, for_e, message):
    core = lax.rem(lax.axis_index("gy"), 2)
    even = core == 0
    zero = jnp.zeros((B, B), BF16)
    message[pl.ds(20 * B, PAD)] = halo_o[pl.ds(14 * B, PAD)]
    for u in range(2):
        def edge(k):
            from_e, from_o = halo_e[1 - core, tile(2 * u + k)], halo_o[tile(7 * u + k)]
            return jnp.where(even, from_o, from_e), jnp.where(even, from_e, from_o)

        own_down, own_up = edge(0)
        high_down, low_up = edge(1)
        low, high = sides[u, 0], sides[u, 1]
        o = [own[u, j] for j in range(4)]
        right = [
            [[low, o[0]], [own_down, high_down], [zero, o[1]]],
            [[zero, o[1]], [low, o[0]], [zero, o[2]]],
            [[o[2], zero], [o[1], zero], [o[3], high]],
            [[o[3], high], [o[2], zero], [low_up, own_up]],
        ]
        centre = []
        for j in range(4):
            left = cat([a[u, j, 0], a[u, j, 3], a[u, j, 4]], 1)
            centre.append(dot(left, cat([cat(r, 1) for r in right[j]], 0)).astype(BF16))
        left_part = [value[:, :B] for value in centre]
        right_part = [value[:, B:] for value in centre]
        beside = link_products(a, u, NEAR[2 * u][1], [own[1 - u, j] for j in range(4)],
                               [sides[1 - u, k] for k in range(2)])
        first = cat([beside[0], left_part[0]], 1)
        middle = [cat([beside[1][0], right_part[0]], 1), cat([beside[1][1], right_part[1]], 1),
                  cat([beside[1][2], left_part[2]], 1), cat([beside[1][3], left_part[3]], 1)]
        last = cat([beside[2], right_part[3]], 1)
        slots = reduce_units(own, u, (first, middle, last), 2)
        slots[0][1] = slots[0][1] + dot_t(o[1], left_part[1])
        slots[2][1] = slots[2][1] + dot_t(o[2], right_part[2])
        beyond = dot(halo_o[tile(7 * u + 4)], cat([jnp.where(even, low, o[3]), jnp.where(even, o[0], high)], 1))
        given = dot_t(jnp.where(even, high, low),
                      cat([jnp.where(even, middle[3], first), jnp.where(even, last, middle[0])], 1))
        for i in range(2):
            k = 2 * u + i
            for t in range(3):
                row[k, t] = slots[t][i]
            for s in range(2):
                if i == 0:
                    extra = halo_o[tile(7 * u + 5 + s)].astype(F32)
                else:
                    extra = halo_o[tile(7 * u + 2 + s)].astype(F32) + beyond[:, s * B:(s + 1) * B]
                row[k, core + s] += extra
                part = given[:, (2 * s + i) * B:(2 * s + i + 1) * B]
                for_e[k, s] = part
                message[tile(5 * k + 3 + s)] = part.astype(BF16)
            for t in range(3):
                message[tile(5 * k + t)] = row[k, t].astype(BF16)


def border_kernel(a, sides, from_west, from_east, out):
    c = lax.axis_index("gy")
    position = lax.rem(c, 4)

    def fill(j, side):
        for k, (u, d) in enumerate(FAR):
            arrived = from_west if d == 0 else from_east
            tiles = [arrived[4], arrived[0]] if j == 0 else [arrived[3], arrived[5]]
            product = dot(a[u, j, LINK_TILE[d]], cat(tiles, 1)).astype(BF16)
            result = dot_t(sides[u, side], product).astype(BF16)
            for s in range(2):
                out[2 * k + s] = result[:, s * B:(s + 1) * B]

    pl.when(jnp.logical_and(position == 0, c > 0))(lambda: fill(0, 0))
    pl.when(jnp.logical_and(position == 3, c < lax.axis_size("gy") - 1))(lambda: fill(3, 1))


def far_kernel(own, a, sides, from_west, from_east, chosen, row, for_e, for_o):
    del chosen
    even = lax.rem(lax.axis_index("gy"), 2) == 0
    for k, (u, d) in enumerate(FAR):
        arrived = from_west if d == 0 else from_east
        first, middle, last = link_products(a, u, d, [arrived[j] for j in range(4)], [arrived[4], arrived[5]])
        slots = reduce_units(own, u, (first, middle, last), 1)
        down = dot_t(sides[u, 0], cat([first, middle[0]], 1))
        up = dot_t(sides[u, 1], cat([middle[3], last], 1))
        to_e, to_o = jnp.where(even, up, down), jnp.where(even, down, up)
        for t in range(3):
            row[k, t] = slots[t][0]
        for s in range(2):
            at = slice(s * B, (s + 1) * B)
            for_e[k, s] = to_e[:, at]
            for_o[2 * k + s] = to_o[:, at].astype(BF16)


def merge_kernel(row, for_e, for_o, from_group, chosen, row_out, message):
    core = lax.rem(lax.axis_index("gy"), 2)
    for k in range(len(FAR)):
        for t in range(3):
            row_out[k, t] = row[k, t]
        for s in range(2):
            row_out[k, core + s] += from_group[2 * k + s].astype(F32)
            message[tile(7 * k + 3 + s)] = for_e[k, s].astype(BF16)
            message[tile(7 * k + 5 + s)] = for_o[2 * k + s]
        for t in range(3):
            message[tile(7 * k + t)] = row_out[k, t].astype(BF16)


def far_tiles(core, half, row, for_e, message, k, t):
    def theirs_at(i):
        return message[1 - core, tile(7 * k + i)].astype(F32)

    def slot(get, shift):
        if t == 1:
            return get(1 - shift)
        return jnp.where(shift == t // 2, get(t // 2), 0.0)

    mine = row[k, t] + slot(lambda s: theirs_at(3 + s), 1 - core)
    theirs = theirs_at(t) + slot(lambda s: for_e[k, s], core)
    inner = slot(lambda s: message[1 - half, tile(7 * k + 5 + s)].astype(F32), half)
    return mine, theirs, inner


def complete(core, row, for_e, message, k, t):
    mine = row[k, t]
    theirs = message[tile(5 * k + t)].astype(F32)
    if t == 1:
        mine = mine + message[tile(5 * k + 3 + core)].astype(F32)
        theirs = theirs + for_e[k, 1 - core]
    else:
        gets = (core == 0) == (t == 2)
        s = 1 if t == 2 else 0
        mine = mine + jnp.where(gets, message[tile(5 * k + 3 + s)].astype(F32), 0.0)
        theirs = theirs + jnp.where(gets, 0.0, for_e[k, s])
    return mine, theirs


def masks(codes, u, position, core):
    code = codes[u * PAD // 2:u * PAD // 2 + 1]
    other = position + 1 - 2 * core
    return (jnp.broadcast_to(code == position.astype(F32), (B, B)),
            jnp.broadcast_to(code == other.astype(F32), (B, B)))


def choose_near_kernel(mine, row, for_e, message, halo_e, halo_o, border, out, wanted):
    del border
    c = lax.axis_index("gy")
    core, position = lax.rem(c, 2), lax.rem(c, 4)
    outer = jnp.logical_or(position == 0, position == 3)
    inferred = 6.0 - mine[...] - halo_e[1 - core, pl.ds(4 * B, PAD)].astype(F32)
    inferred = inferred - halo_o[pl.ds(14 * B, PAD)].astype(F32)
    codes = jnp.where(outer, message[pl.ds(20 * B, PAD)].astype(F32), inferred)
    wanted[...] = codes
    for k, (u, _) in enumerate(NEAR):
        use_mine, use_theirs = masks(codes, u, position, core)
        for t in range(3):
            own_row, other_row = complete(core, row, for_e, message, k, t)
            out[3 * k + t] = jnp.where(use_mine, own_row, jnp.where(use_theirs, other_row, 0.0)).astype(BF16)


def choose_far_kernel(wanted, row, for_e, message, out):
    c = lax.axis_index("gy")
    core, position = lax.rem(c, 2), lax.rem(c, 4)
    for k, (u, _) in enumerate(FAR):
        use_mine, use_theirs = masks(wanted[...], u, position, core)
        for t in range(3):
            mine, theirs, inner = far_tiles(core, position // 2, row, for_e, message, k, t)
            out[3 * k + t] = jnp.where(use_mine, mine, jnp.where(use_theirs, theirs, inner)).astype(BF16)


def finish_near_kernel(mine, row, for_e, message, arrived, out, buffer, sems):
    c = lax.axis_index("gy")
    core, position = lax.rem(c, 2), lax.rem(c, 4)
    copies = []
    for k, (u, d) in enumerate(NEAR):
        use_mine, use_theirs = masks(mine[...], u, position, core)
        for t in range(3):
            own_row, other_row = complete(core, row, for_e, message, k, t)
            got = arrived[3 * k + t].astype(F32)
            buffer[k, t] = jnp.where(use_mine, own_row, jnp.where(use_theirs, other_row, got))
        copies.append(pltpu.make_async_copy(buffer.at[k], out.at[u, 0, d], sems.at[k]))
        copies[-1].start()
    for copy in copies:
        copy.wait()


def finish_far_kernel(mine, row, for_e, message, arrived, started, out, buffer, sems):
    del started
    c = lax.axis_index("gy")
    core, position = lax.rem(c, 2), lax.rem(c, 4)
    half = position // 2
    copies = []
    for k, (u, d) in enumerate(FAR):
        use_mine, use_theirs = masks(mine[...], u, position, core)
        code = mine[u * PAD // 2:u * PAD // 2 + 1]
        add_arrived = jnp.broadcast_to(code == (1 + half).astype(F32), (B, B))
        add_inner = jnp.broadcast_to(code == (2 - half).astype(F32), (B, B))
        for t in range(3):
            own_row, other_row, inner = far_tiles(core, half, row, for_e, message, k, t)
            got = arrived[3 * k + t].astype(F32)
            here = jnp.where(use_mine, own_row, other_row) + jnp.where(add_arrived, got, 0.0)
            there = got + jnp.where(add_inner, inner, 0.0)
            buffer[k, t] = jnp.where(jnp.logical_or(use_mine, use_theirs), here, there)
        copies.append(pltpu.make_async_copy(buffer.at[k], out.at[u, 0, d], sems.at[k]))
        copies[-1].start()
    for copy in copies:
        copy.wait()


def on_device(a_tiles, a_links, p_own, p_side, p_links, coarse_pick):
    count, columns = lax.axis_size("gy"), lax.axis_size("gx")
    pairs = [(2 * g, 2 * g + 1) for g in range(count // 2)]
    cores = [list(pair) for pair in pairs]
    inside = pairs + [(b, a) for a, b in pairs]
    outside = [(i + 1, i + 2) for i in range(0, count - 2, 2)]
    outside = outside + [(b, a) for a, b in outside]
    between = [(i, i + 1) for i in range(3, count - 1, 4)]
    between = between + [(b, a) for a, b in between]
    across = [(i, i ^ 2) for i in range(count)]
    eastward = [(i, i + 1) for i in range(columns - 1)]
    westward = [(b, a) for a, b in eastward]
    bb = (B, B)
    near, far = len(NEAR), len(FAR)

    own, a, sides, east, west, msg_o, msg_e, mine = call(
        begin_kernel,
        [pltpu.with_memory_space_constraint(x, pltpu.HBM)
         for x in (a_links, p_links, coarse_pick.T, p_own, p_side, a_tiles)],
        [(p_own.shape, BF16), (a_tiles.shape, BF16), ((2, 2) + bb, BF16), ((6,) + bb, BF16), ((6,) + bb, BF16),
         ((14 * B + PAD, B), BF16), ((4 * B + PAD, B), BF16), ((PAD, B), F32)],
        in_specs=[HBM] * 6,
        scratch=[pltpu.SMEM(a_links.shape, jnp.int32), pltpu.SMEM(p_links.shape, jnp.int32),
                 pltpu.SMEM((1, 2), jnp.int32), pltpu.VMEM(p_side.shape, BF16), pltpu.SemaphoreType.DMA((6,))])
    halo_o = lax.ppermute(msg_o, "gy", outside)
    from_west = lax.ppermute(east, "gx", eastward)
    from_east = lax.ppermute(west, "gx", westward)
    halo_e = lax.all_gather(msg_e, "gy", axis_index_groups=cores)
    row_n, for_e_n, message_n = call(
        near_kernel, (own, a, sides, halo_e, halo_o),
        [((near, 3) + bb, F32), ((near, 2) + bb, F32), ((5 * near * B + PAD, B), BF16)])
    message_n = lax.ppermute(message_n, "gy", inside)
    (for_group,) = call(
        border_kernel, (a, sides, from_west, from_east), [((2 * far,) + bb, BF16)], cost=20000000000)
    from_group = lax.ppermute(for_group, "gy", between)
    chosen_n, wanted = call(
        choose_near_kernel, (mine, row_n, for_e_n, message_n, halo_e, halo_o, for_group),
        [((3 * near,) + bb, BF16), ((PAD, B), F32)])
    arrived_n = lax.ppermute(chosen_n, "gy", across)
    row_f, for_e_f, for_o_f = call(
        far_kernel, (own, a, sides, from_west, from_east, chosen_n),
        [((far, 3) + bb, F32), ((far, 2) + bb, F32), ((2 * far,) + bb, BF16)], cost=0)
    row_f, message_f = call(
        merge_kernel, (row_f, for_e_f, for_o_f, from_group, chosen_n), [((far, 3) + bb, F32), ((7 * far * B, B), BF16)])
    message_f = lax.all_gather(message_f, "gy", axis_index_groups=cores)
    (chosen_f,) = call(choose_far_kernel, (wanted, row_f, for_e_f, message_f), [((3 * far,) + bb, BF16)])
    arrived_f = lax.ppermute(chosen_f, "gy", across)
    shape = (2, 1, 3, 3) + bb
    (out,) = call(
        finish_near_kernel, (mine, row_n, for_e_n, message_n, arrived_n), [(shape, F32)], out_specs=[HBM],
        scratch=[pltpu.VMEM((near, 3) + bb, F32), pltpu.SemaphoreType.DMA((near,))], cost=0)
    (out,) = call(
        finish_far_kernel, (mine, row_f, for_e_f, message_f, arrived_f, out), [(shape, F32)],
        in_specs=[VMEM] * 5 + [HBM], out_specs=[HBM], aliases={5: 0},
        scratch=[pltpu.VMEM((far, 3) + bb, F32), pltpu.SemaphoreType.DMA((far,))])
    return out


def solution(mesh):
    return jax.shard_map(
        on_device,
        mesh=mesh,
        in_specs=(
            P("gx", "gy", None, None, None),
            P("gx", "gy", None),
            P("gx", "gy", None, None),
            P("gx", "gy", None, None, None),
            P("gx", "gy", None),
            P("gx", "gy"),
        ),
        out_specs=P("gx", "gy", None, None, None, None),
        check_vma=False,
    )
```

```python
import jax
import jax.numpy as jnp
from jax import lax
from jax.experimental import pallas as pl
from jax.experimental.pallas import tpu as pltpu
from jax.sharding import PartitionSpec as P

B = 128
PAD = 16
F32 = jnp.float32
BF16 = jnp.bfloat16
VMEM = pl.BlockSpec(memory_space=pltpu.VMEM)
HBM = pl.BlockSpec(memory_space=pltpu.HBM)

NEAR = ((0, 2), (0, 1), (1, 0), (1, 1))
FAR = ((0, 0), (1, 2))
LINK_TILE = {0: 1, 2: 2}


def call(kernel, args, shapes, in_specs=None, out_specs=None, scratch=(), aliases=None, cost=0):
    return pl.pallas_call(
        kernel,
        in_specs=in_specs or [VMEM] * len(args),
        out_specs=out_specs or [VMEM] * len(shapes),
        out_shape=[jax.ShapeDtypeStruct(shape, dtype) for shape, dtype in shapes],
        scratch_shapes=list(scratch),
        input_output_aliases=aliases or {},
        compiler_params=pltpu.CompilerParams(vmem_limit_bytes=32 * 2**20),
        cost_estimate=pl.CostEstimate(flops=cost, bytes_accessed=cost, transcendentals=0),
    )(*args)


def tile(index):
    return pl.ds(index * B, B)


def dot(a, b):
    return lax.dot_general(a, b, (((1,), (0,)), ((), ())), preferred_element_type=F32)


def dot_t(a, b):
    return lax.dot_general(a, b, (((0,), (0,)), ((), ())), preferred_element_type=F32)


def cat(parts, axis):
    return jnp.concatenate(parts, axis=axis)


def begin_kernel(a_links, p_links, picks, own_in, side_in, a_in,
                 own, a, sides, east, west, msg_o, mine,
                 s_links, s_side, s_picks, raw, sems):
    copies = [
        pltpu.make_async_copy(src, dst, sems.at[i])
        for i, (src, dst) in enumerate(((p_links, s_side), (own_in, own), (side_in, raw), (a_links, s_links),
                                        (picks, s_picks), (a_in, a)))
    ]
    for copy in copies:
        copy.start()
    c = lax.axis_index("gy")
    core = lax.rem(c, 2)
    keep = [c > 0, c < lax.axis_size("gy") - 1]
    for copy in copies[:3]:
        copy.wait()
    for u in range(2):
        for k in range(2):
            factor = jnp.where(keep[k], s_side[u, 0, k], 0).astype(F32).astype(BF16)
            sides[u, k] = raw[u, 0, k] * factor
    for u, message in ((1, east), (0, west)):
        for j in range(4):
            message[j] = own[u, j]
        for k in range(2):
            message[4 + k] = sides[u, k]
    for copy in copies[3:5]:
        copy.wait()
    rows = lax.broadcasted_iota(jnp.int32, (PAD, B), 0)
    codes = jnp.where(rows < PAD // 2, s_picks[0, 0], s_picks[0, 1]).astype(F32)
    mine[...] = codes
    msg_o[pl.ds(14 * B, PAD)] = codes.astype(BF16)
    copies[5].wait()
    for u in range(2):
        for j in range(4):
            for k in range(4):
                a[u, j, k + 1] = a[u, j, k + 1] * s_links[u, j, k].astype(F32).astype(BF16)

    def fill_o(j_o, k_o):
        for u in range(2):
            side, block = sides[u, k_o], own[u, j_o]
            other_side, other_block = sides[1 - u, k_o], own[1 - u, j_o]
            zero = jnp.zeros((B, B), BF16)
            inner = 1 if j_o == 0 else 2
            if j_o == 0:
                right = cat([cat([side, block], 1), cat([zero, own[u, inner]], 1)], 0)
                left = cat([a[u, j_o, 0], a[u, j_o, 4]], 1)
                beyond = a[u, j_o, 3]
                panel = cat([other_side, other_block], 1)
            else:
                right = cat([cat([block, side], 1), cat([own[u, inner], zero], 1)], 0)
                left = cat([a[u, j_o, 0], a[u, j_o, 3]], 1)
                beyond = a[u, j_o, 4]
                panel = cat([other_block, other_side], 1)
            centre = dot(left, right).astype(BF16)
            beside = dot(a[u, j_o, LINK_TILE[NEAR[2 * u][1]]], panel).astype(BF16)
            result = dot_t(side, cat([centre, beyond, beside], 1)).astype(BF16)
            msg_o[tile(7 * u)] = block
            msg_o[tile(7 * u + 1)] = side
            for i in range(5):
                msg_o[tile(7 * u + 2 + i)] = result[:, i * B:(i + 1) * B]

    pl.when(jnp.logical_and(core == 0, keep[0]))(lambda: fill_o(0, 0))
    pl.when(jnp.logical_and(core == 1, keep[1]))(lambda: fill_o(3, 1))


def reduce_units(own, u, products, count):
    firsts, middles, lasts = products
    blocks = cat([own[u, j] for j in range(4)], 0)
    slot1 = dot_t(blocks, cat(middles, 0))
    slot0 = dot_t(own[u, 0], firsts)
    slot2 = dot_t(own[u, 3], lasts)
    return [[value[:, i * B:(i + 1) * B] for i in range(count)] for value in (slot0, slot1, slot2)]


def link_products(a, u, d, tiles, side_tiles):
    k = LINK_TILE[d]
    first = dot(a[u, 0, k], cat([side_tiles[0], tiles[0]], 1)).astype(BF16)
    last = dot(a[u, 3, k], cat([tiles[3], side_tiles[1]], 1)).astype(BF16)
    inner = [dot(a[u, j, k], tiles[j]).astype(BF16) for j in (1, 2)]
    return first[:, :B], [first[:, B:], inner[0], inner[1], last[:, :B]], last[:, B:]


def near_kernel(own, a, sides, halo_o, mine, row, for_e, message):
    core = lax.rem(lax.axis_index("gy"), 2)
    even = core == 0
    zero = jnp.zeros((B, B), BF16)
    message[pl.ds(28 * B, PAD)] = halo_o[pl.ds(14 * B, PAD)]
    message[pl.ds(28 * B + PAD, PAD)] = mine[...].astype(BF16)
    for u in range(2):
        def edge(k):
            from_o = halo_o[tile(7 * u + k)]
            return jnp.where(even, from_o, zero), jnp.where(even, zero, from_o)

        own_down, own_up = edge(0)
        high_down, low_up = edge(1)
        low, high = sides[u, 0], sides[u, 1]
        o = [own[u, j] for j in range(4)]
        message[tile(20 + 4 * u)] = jnp.where(even, o[3], low)
        message[tile(21 + 4 * u)] = jnp.where(even, high, o[0])
        before = dot_t(jnp.where(even, cat([o[3], high], 1), cat([o[0], low], 1)),
                       jnp.where(even, a[u, 3, 4], a[u, 0, 3]))
        message[tile(22 + 4 * u)] = before[:B].astype(BF16)
        message[tile(23 + 4 * u)] = before[B:].astype(BF16)
        right = [
            [[low, o[0]], [own_down, high_down], [zero, o[1]]],
            [[zero, o[1]], [low, o[0]], [zero, o[2]]],
            [[o[2], zero], [o[1], zero], [o[3], high]],
            [[o[3], high], [o[2], zero], [low_up, own_up]],
        ]
        centre = []
        for j in range(4):
            left = cat([a[u, j, 0], a[u, j, 3], a[u, j, 4]], 1)
            centre.append(dot(left, cat([cat(r, 1) for r in right[j]], 0)).astype(BF16))
        left_part = [value[:, :B] for value in centre]
        right_part = [value[:, B:] for value in centre]
        beside = link_products(a, u, NEAR[2 * u][1], [own[1 - u, j] for j in range(4)],
                               [sides[1 - u, k] for k in range(2)])
        first = cat([beside[0], left_part[0]], 1)
        middle = [cat([beside[1][0], right_part[0]], 1), cat([beside[1][1], right_part[1]], 1),
                  cat([beside[1][2], left_part[2]], 1), cat([beside[1][3], left_part[3]], 1)]
        last = cat([beside[2], right_part[3]], 1)
        slots = reduce_units(own, u, (first, middle, last), 2)
        slots[0][1] = slots[0][1] + dot_t(o[1], left_part[1])
        slots[2][1] = slots[2][1] + dot_t(o[2], right_part[2])
        beyond = dot(halo_o[tile(7 * u + 4)], cat([jnp.where(even, low, o[3]), jnp.where(even, o[0], high)], 1))
        given = dot_t(jnp.where(even, high, low),
                      cat([jnp.where(even, middle[3], first), jnp.where(even, last, middle[0])], 1))
        for i in range(2):
            k = 2 * u + i
            for t in range(3):
                row[k, t] = slots[t][i]
            for s in range(2):
                if i == 0:
                    extra = halo_o[tile(7 * u + 5 + s)].astype(F32)
                else:
                    extra = halo_o[tile(7 * u + 2 + s)].astype(F32) + beyond[:, s * B:(s + 1) * B]
                row[k, core + s] += extra
                part = given[:, (2 * s + i) * B:(2 * s + i + 1) * B]
                for_e[k, s] = part
                message[tile(5 * k + 3 + s)] = part.astype(BF16)
            for t in range(3):
                message[tile(5 * k + t)] = row[k, t].astype(BF16)


def border_kernel(a, sides, from_west, from_east, out):
    c = lax.axis_index("gy")
    position = lax.rem(c, 4)

    def fill(j, side):
        for k, (u, d) in enumerate(FAR):
            arrived = from_west if d == 0 else from_east
            tiles = [arrived[4], arrived[0]] if j == 0 else [arrived[3], arrived[5]]
            product = dot(a[u, j, LINK_TILE[d]], cat(tiles, 1)).astype(BF16)
            result = dot_t(sides[u, side], product).astype(BF16)
            for s in range(2):
                out[2 * k + s] = result[:, s * B:(s + 1) * B]

    pl.when(jnp.logical_and(position == 0, c > 0))(lambda: fill(0, 0))
    pl.when(jnp.logical_and(position == 3, c < lax.axis_size("gy") - 1))(lambda: fill(3, 1))


def far_kernel(own, a, sides, from_west, from_east, chosen, row, for_e, for_o):
    del chosen
    even = lax.rem(lax.axis_index("gy"), 2) == 0
    for k, (u, d) in enumerate(FAR):
        arrived = from_west if d == 0 else from_east
        first, middle, last = link_products(a, u, d, [arrived[j] for j in range(4)], [arrived[4], arrived[5]])
        slots = reduce_units(own, u, (first, middle, last), 1)
        down = dot_t(sides[u, 0], cat([first, middle[0]], 1))
        up = dot_t(sides[u, 1], cat([middle[3], last], 1))
        to_e, to_o = jnp.where(even, up, down), jnp.where(even, down, up)
        for t in range(3):
            row[k, t] = slots[t][0]
        for s in range(2):
            at = slice(s * B, (s + 1) * B)
            for_e[k, s] = to_e[:, at]
            for_o[2 * k + s] = to_o[:, at].astype(BF16)


def merge_kernel(row, for_e, for_o, from_group, chosen, row_out, message):
    core = lax.rem(lax.axis_index("gy"), 2)
    for k in range(len(FAR)):
        for t in range(3):
            row_out[k, t] = row[k, t]
        for s in range(2):
            row_out[k, core + s] += from_group[2 * k + s].astype(F32)
            message[tile(7 * k + 3 + s)] = for_e[k, s].astype(BF16)
            message[tile(7 * k + 5 + s)] = for_o[2 * k + s]
        for t in range(3):
            message[tile(7 * k + t)] = row_out[k, t].astype(BF16)


def far_tiles(core, half, row, for_e, message, k, t):
    def theirs_at(i):
        return message[1 - core, tile(7 * k + i)].astype(F32)

    def slot(get, shift):
        if t == 1:
            return get(1 - shift)
        return jnp.where(shift == t // 2, get(t // 2), 0.0)

    mine = row[k, t] + slot(lambda s: theirs_at(3 + s), 1 - core)
    theirs = theirs_at(t) + slot(lambda s: for_e[k, s], core)
    inner = slot(lambda s: message[1 - half, tile(7 * k + 5 + s)].astype(F32), half)
    return mine, theirs, inner


def complete(core, row, for_e, message, joint, k, t):
    def to_mine(s):
        value = message[tile(5 * k + 3 + s)].astype(F32)
        return value + joint[k // 2, 0, s] if k % 2 else value

    def to_theirs(s):
        return for_e[k, s] + joint[k // 2, 1, s] if k % 2 else for_e[k, s]

    mine = row[k, t]
    theirs = message[tile(5 * k + t)].astype(F32)
    if t == 1:
        return mine + to_mine(core), theirs + to_theirs(1 - core)
    gets = (core == 0) == (t == 2)
    s = 1 if t == 2 else 0
    return mine + jnp.where(gets, to_mine(s), 0.0), theirs + jnp.where(gets, 0.0, to_theirs(s))


def masks(codes, u, position, core):
    code = codes[u * PAD // 2:u * PAD // 2 + 1]
    other = position + 1 - 2 * core
    return (jnp.broadcast_to(code == position.astype(F32), (B, B)),
            jnp.broadcast_to(code == other.astype(F32), (B, B)))


def choose_near_kernel(mine, row, for_e, message, sent, halo_o, border, out, wanted, joint):
    del border
    c = lax.axis_index("gy")
    core, position = lax.rem(c, 2), lax.rem(c, 4)
    outer = jnp.logical_or(position == 0, position == 3)
    inferred = 6.0 - mine[...] - message[pl.ds(28 * B + PAD, PAD)].astype(F32)
    inferred = inferred - halo_o[pl.ds(14 * B, PAD)].astype(F32)
    codes = jnp.where(outer, message[pl.ds(28 * B, PAD)].astype(F32), inferred)
    wanted[...] = codes
    for u in range(2):
        def part(ref, i):
            return ref[tile(20 + 4 * u + i)]

        ours, got = cat([part(sent, 0), part(sent, 1)], 1), cat([part(message, 0), part(message, 1)], 1)
        to_mine = dot(cat([part(sent, 2), part(message, 3)], 1), cat([got, ours], 0))
        to_theirs = dot(cat([part(message, 2), part(sent, 3)], 1), cat([ours, got], 0))
        for s in range(2):
            joint[u, 0, s] = to_mine[:, s * B:(s + 1) * B]
            joint[u, 1, s] = to_theirs[:, s * B:(s + 1) * B]
    for k, (u, _) in enumerate(NEAR):
        use_mine, use_theirs = masks(codes, u, position, core)
        for t in range(3):
            own_row, other_row = complete(core, row, for_e, message, joint, k, t)
            out[3 * k + t] = jnp.where(use_mine, own_row, jnp.where(use_theirs, other_row, 0.0)).astype(BF16)


def choose_far_kernel(wanted, row, for_e, message, out):
    c = lax.axis_index("gy")
    core, position = lax.rem(c, 2), lax.rem(c, 4)
    for k, (u, _) in enumerate(FAR):
        use_mine, use_theirs = masks(wanted[...], u, position, core)
        for t in range(3):
            mine, theirs, inner = far_tiles(core, position // 2, row, for_e, message, k, t)
            out[3 * k + t] = jnp.where(use_mine, mine, jnp.where(use_theirs, theirs, inner)).astype(BF16)


def finish_near_kernel(mine, row, for_e, message, joint, arrived, out, buffer, sems):
    c = lax.axis_index("gy")
    core, position = lax.rem(c, 2), lax.rem(c, 4)
    copies = []
    for k, (u, d) in enumerate(NEAR):
        use_mine, use_theirs = masks(mine[...], u, position, core)
        for t in range(3):
            own_row, other_row = complete(core, row, for_e, message, joint, k, t)
            got = arrived[3 * k + t].astype(F32)
            buffer[k, t] = jnp.where(use_mine, own_row, jnp.where(use_theirs, other_row, got))
        copies.append(pltpu.make_async_copy(buffer.at[k], out.at[u, 0, d], sems.at[k]))
        copies[-1].start()
    for copy in copies:
        copy.wait()


def finish_far_kernel(mine, row, for_e, message, arrived, started, out, buffer, sems):
    del started
    c = lax.axis_index("gy")
    core, position = lax.rem(c, 2), lax.rem(c, 4)
    half = position // 2
    copies = []
    for k, (u, d) in enumerate(FAR):
        use_mine, use_theirs = masks(mine[...], u, position, core)
        code = mine[u * PAD // 2:u * PAD // 2 + 1]
        add_arrived = jnp.broadcast_to(code == (1 + half).astype(F32), (B, B))
        add_inner = jnp.broadcast_to(code == (2 - half).astype(F32), (B, B))
        for t in range(3):
            own_row, other_row, inner = far_tiles(core, half, row, for_e, message, k, t)
            got = arrived[3 * k + t].astype(F32)
            here = jnp.where(use_mine, own_row, other_row) + jnp.where(add_arrived, got, 0.0)
            there = got + jnp.where(add_inner, inner, 0.0)
            buffer[k, t] = jnp.where(jnp.logical_or(use_mine, use_theirs), here, there)
        copies.append(pltpu.make_async_copy(buffer.at[k], out.at[u, 0, d], sems.at[k]))
        copies[-1].start()
    for copy in copies:
        copy.wait()


def on_device(a_tiles, a_links, p_own, p_side, p_links, coarse_pick):
    count, columns = lax.axis_size("gy"), lax.axis_size("gx")
    pairs = [(2 * g, 2 * g + 1) for g in range(count // 2)]
    cores = [list(pair) for pair in pairs]
    inside = pairs + [(b, a) for a, b in pairs]
    outside = [(i + 1, i + 2) for i in range(0, count - 2, 2)]
    outside = outside + [(b, a) for a, b in outside]
    between = [(i, i + 1) for i in range(3, count - 1, 4)]
    between = between + [(b, a) for a, b in between]
    across = [(i, i ^ 2) for i in range(count)]
    eastward = [(i, i + 1) for i in range(columns - 1)]
    westward = [(b, a) for a, b in eastward]
    bb = (B, B)
    near, far = len(NEAR), len(FAR)

    own, a, sides, east, west, msg_o, mine = call(
        begin_kernel,
        [pltpu.with_memory_space_constraint(x, pltpu.HBM)
         for x in (a_links, p_links, coarse_pick.T, p_own, p_side, a_tiles)],
        [(p_own.shape, BF16), (a_tiles.shape, BF16), ((2, 2) + bb, BF16), ((6,) + bb, BF16), ((6,) + bb, BF16),
         ((14 * B + PAD, B), BF16), ((PAD, B), F32)],
        in_specs=[HBM] * 6,
        scratch=[pltpu.SMEM(a_links.shape, jnp.int32), pltpu.SMEM(p_links.shape, jnp.int32),
                 pltpu.SMEM((1, 2), jnp.int32), pltpu.VMEM(p_side.shape, BF16), pltpu.SemaphoreType.DMA((6,))])
    halo_o = lax.ppermute(msg_o, "gy", outside)
    from_west = lax.ppermute(east, "gx", eastward)
    from_east = lax.ppermute(west, "gx", westward)
    row_n, for_e_n, message_n = call(
        near_kernel, (own, a, sides, halo_o, mine),
        [((near, 3) + bb, F32), ((near, 2) + bb, F32), ((28 * B + 2 * PAD, B), BF16)])
    sent_n = message_n
    message_n = lax.ppermute(message_n, "gy", inside)
    (for_group,) = call(
        border_kernel, (a, sides, from_west, from_east), [((2 * far,) + bb, BF16)], cost=20000000000)
    from_group = lax.ppermute(for_group, "gy", between)
    chosen_n, wanted, joint = call(
        choose_near_kernel, (mine, row_n, for_e_n, message_n, sent_n, halo_o, for_group),
        [((3 * near,) + bb, BF16), ((PAD, B), F32), ((2, 2, 2) + bb, F32)])
    arrived_n = lax.ppermute(chosen_n, "gy", across)
    row_f, for_e_f, for_o_f = call(
        far_kernel, (own, a, sides, from_west, from_east, chosen_n),
        [((far, 3) + bb, F32), ((far, 2) + bb, F32), ((2 * far,) + bb, BF16)], cost=0)
    row_f, message_f = call(
        merge_kernel, (row_f, for_e_f, for_o_f, from_group, chosen_n), [((far, 3) + bb, F32), ((7 * far * B, B), BF16)])
    message_f = lax.all_gather(message_f, "gy", axis_index_groups=cores)
    (chosen_f,) = call(choose_far_kernel, (wanted, row_f, for_e_f, message_f), [((3 * far,) + bb, BF16)])
    arrived_f = lax.ppermute(chosen_f, "gy", across)
    shape = (2, 1, 3, 3) + bb
    (out,) = call(
        finish_near_kernel, (mine, row_n, for_e_n, message_n, joint, arrived_n), [(shape, F32)], out_specs=[HBM],
        scratch=[pltpu.VMEM((near, 3) + bb, F32), pltpu.SemaphoreType.DMA((near,))], cost=0)
    (out,) = call(
        finish_far_kernel, (mine, row_f, for_e_f, message_f, arrived_f, out), [(shape, F32)],
        in_specs=[VMEM] * 5 + [HBM], out_specs=[HBM], aliases={5: 0},
        scratch=[pltpu.VMEM((far, 3) + bb, F32), pltpu.SemaphoreType.DMA((far,))])
    return out


def solution(mesh):
    return jax.shard_map(
        on_device,
        mesh=mesh,
        in_specs=(
            P("gx", "gy", None, None, None),
            P("gx", "gy", None),
            P("gx", "gy", None, None),
            P("gx", "gy", None, None, None),
            P("gx", "gy", None),
            P("gx", "gy"),
        ),
        out_specs=P("gx", "gy", None, None, None, None),
        check_vma=False,
    )
```

```python
import jax
import jax.numpy as jnp
from jax import lax
from jax.experimental import pallas as pl
from jax.experimental.pallas import tpu as pltpu
from jax.sharding import PartitionSpec as P

B = 128
PAD = 16
F32 = jnp.float32
BF16 = jnp.bfloat16
VMEM = pl.BlockSpec(memory_space=pltpu.VMEM)
HBM = pl.BlockSpec(memory_space=pltpu.HBM)

NEAR = ((0, 2), (0, 1), (1, 0), (1, 1))
FAR = ((0, 0), (1, 2))
LINK_TILE = {0: 1, 2: 2}


def call(kernel, args, shapes, in_specs=None, out_specs=None, scratch=(), aliases=None, cost=0):
    return pl.pallas_call(
        kernel,
        in_specs=in_specs or [VMEM] * len(args),
        out_specs=out_specs or [VMEM] * len(shapes),
        out_shape=[jax.ShapeDtypeStruct(shape, dtype) for shape, dtype in shapes],
        scratch_shapes=list(scratch),
        input_output_aliases=aliases or {},
        compiler_params=pltpu.CompilerParams(vmem_limit_bytes=32 * 2**20),
        cost_estimate=pl.CostEstimate(flops=cost, bytes_accessed=cost, transcendentals=0),
    )(*args)


def tile(index):
    return pl.ds(index * B, B)


def dot(a, b):
    return lax.dot_general(a, b, (((1,), (0,)), ((), ())), preferred_element_type=F32)


def dot_t(a, b):
    return lax.dot_general(a, b, (((0,), (0,)), ((), ())), preferred_element_type=F32)


def cat(parts, axis):
    return jnp.concatenate(parts, axis=axis)


def begin_kernel(a_links, p_links, picks, own_in, side_in, a_in,
                 own, a, sides, east, west, msg_o, mine,
                 s_links, s_side, s_picks, raw, sems):
    copies = [
        pltpu.make_async_copy(src, dst, sems.at[i])
        for i, (src, dst) in enumerate(((p_links, s_side), (own_in, own), (side_in, raw), (a_links, s_links),
                                        (picks, s_picks), (a_in, a)))
    ]
    for copy in copies:
        copy.start()
    c = lax.axis_index("gy")
    core = lax.rem(c, 2)
    keep = [c > 0, c < lax.axis_size("gy") - 1]
    for copy in copies[:3]:
        copy.wait()
    for u in range(2):
        for k in range(2):
            factor = jnp.where(keep[k], s_side[u, 0, k], 0).astype(F32).astype(BF16)
            sides[u, k] = raw[u, 0, k] * factor
    for u, message in ((1, east), (0, west)):
        for j in range(4):
            message[j] = own[u, j]
        for k in range(2):
            message[4 + k] = sides[u, k]
    for copy in copies[3:5]:
        copy.wait()
    rows = lax.broadcasted_iota(jnp.int32, (PAD, B), 0)
    codes = jnp.where(rows < PAD // 2, s_picks[0, 0], s_picks[0, 1]).astype(F32)
    mine[...] = codes
    msg_o[pl.ds(14 * B, PAD)] = codes.astype(BF16)
    copies[5].wait()
    for u in range(2):
        for j in range(4):
            for k in range(4):
                a[u, j, k + 1] = a[u, j, k + 1] * s_links[u, j, k].astype(F32).astype(BF16)

    def fill_o(j_o, k_o):
        for u in range(2):
            side, block = sides[u, k_o], own[u, j_o]
            other_side, other_block = sides[1 - u, k_o], own[1 - u, j_o]
            zero = jnp.zeros((B, B), BF16)
            inner = 1 if j_o == 0 else 2
            if j_o == 0:
                right = cat([cat([side, block], 1), cat([zero, own[u, inner]], 1)], 0)
                left = cat([a[u, j_o, 0], a[u, j_o, 4]], 1)
                beyond = a[u, j_o, 3]
                panel = cat([other_side, other_block], 1)
            else:
                right = cat([cat([block, side], 1), cat([own[u, inner], zero], 1)], 0)
                left = cat([a[u, j_o, 0], a[u, j_o, 3]], 1)
                beyond = a[u, j_o, 4]
                panel = cat([other_block, other_side], 1)
            centre = dot(left, right).astype(BF16)
            beside = dot(a[u, j_o, LINK_TILE[NEAR[2 * u][1]]], panel).astype(BF16)
            result = dot_t(side, cat([centre, beyond, beside], 1)).astype(BF16)
            msg_o[tile(7 * u)] = block
            msg_o[tile(7 * u + 1)] = side
            for i in range(5):
                msg_o[tile(7 * u + 2 + i)] = result[:, i * B:(i + 1) * B]

    pl.when(jnp.logical_and(core == 0, keep[0]))(lambda: fill_o(0, 0))
    pl.when(jnp.logical_and(core == 1, keep[1]))(lambda: fill_o(3, 1))


def reduce_units(own, u, products, count):
    firsts, middles, lasts = products
    blocks = cat([own[u, j] for j in range(4)], 0)
    slot1 = dot_t(blocks, cat(middles, 0))
    slot0 = dot_t(own[u, 0], firsts)
    slot2 = dot_t(own[u, 3], lasts)
    return [[value[:, i * B:(i + 1) * B] for i in range(count)] for value in (slot0, slot1, slot2)]


def link_products(a, u, d, tiles, side_tiles):
    k = LINK_TILE[d]
    first = dot(a[u, 0, k], cat([side_tiles[0], tiles[0]], 1)).astype(BF16)
    last = dot(a[u, 3, k], cat([tiles[3], side_tiles[1]], 1)).astype(BF16)
    inner = [dot(a[u, j, k], tiles[j]).astype(BF16) for j in (1, 2)]
    return first[:, :B], [first[:, B:], inner[0], inner[1], last[:, :B]], last[:, B:]


def near_kernel(own, a, sides, halo_o, mine, row, for_e, message):
    core = lax.rem(lax.axis_index("gy"), 2)
    even = core == 0
    zero = jnp.zeros((B, B), BF16)
    message[pl.ds(28 * B, PAD)] = halo_o[pl.ds(14 * B, PAD)]
    message[pl.ds(28 * B + PAD, PAD)] = mine[...].astype(BF16)
    for u in range(2):
        def edge(k):
            from_o = halo_o[tile(7 * u + k)]
            return jnp.where(even, from_o, zero), jnp.where(even, zero, from_o)

        own_down, own_up = edge(0)
        high_down, low_up = edge(1)
        low, high = sides[u, 0], sides[u, 1]
        o = [own[u, j] for j in range(4)]
        message[tile(20 + 4 * u)] = jnp.where(even, o[3], low)
        message[tile(21 + 4 * u)] = jnp.where(even, high, o[0])
        before = dot_t(jnp.where(even, cat([o[3], high], 1), cat([o[0], low], 1)),
                       jnp.where(even, a[u, 3, 4], a[u, 0, 3]))
        message[tile(22 + 4 * u)] = before[:B].astype(BF16)
        message[tile(23 + 4 * u)] = before[B:].astype(BF16)
        right = [
            [[low, o[0]], [own_down, high_down], [zero, o[1]]],
            [[zero, o[1]], [low, o[0]], [zero, o[2]]],
            [[o[2], zero], [o[1], zero], [o[3], high]],
            [[o[3], high], [o[2], zero], [low_up, own_up]],
        ]
        centre = []
        for j in range(4):
            left = cat([a[u, j, 0], a[u, j, 3], a[u, j, 4]], 1)
            centre.append(dot(left, cat([cat(r, 1) for r in right[j]], 0)).astype(BF16))
        left_part = [value[:, :B] for value in centre]
        right_part = [value[:, B:] for value in centre]
        beside = link_products(a, u, NEAR[2 * u][1], [own[1 - u, j] for j in range(4)],
                               [sides[1 - u, k] for k in range(2)])
        first = cat([beside[0], left_part[0]], 1)
        middle = [cat([beside[1][0], right_part[0]], 1), cat([beside[1][1], right_part[1]], 1),
                  cat([beside[1][2], left_part[2]], 1), cat([beside[1][3], left_part[3]], 1)]
        last = cat([beside[2], right_part[3]], 1)
        slots = reduce_units(own, u, (first, middle, last), 2)
        slots[0][1] = slots[0][1] + dot_t(o[1], left_part[1])
        slots[2][1] = slots[2][1] + dot_t(o[2], right_part[2])
        beyond = dot(halo_o[tile(7 * u + 4)], cat([jnp.where(even, low, o[3]), jnp.where(even, o[0], high)], 1))
        given = dot_t(jnp.where(even, high, low),
                      cat([jnp.where(even, middle[3], first), jnp.where(even, last, middle[0])], 1))
        for i in range(2):
            k = 2 * u + i
            for t in range(3):
                row[k, t] = slots[t][i]
            for s in range(2):
                if i == 0:
                    extra = halo_o[tile(7 * u + 5 + s)].astype(F32)
                else:
                    extra = halo_o[tile(7 * u + 2 + s)].astype(F32) + beyond[:, s * B:(s + 1) * B]
                row[k, core + s] += extra
                part = given[:, (2 * s + i) * B:(2 * s + i + 1) * B]
                for_e[k, s] = part
                message[tile(5 * k + 3 + s)] = part.astype(BF16)
            for t in range(3):
                message[tile(5 * k + t)] = row[k, t].astype(BF16)


def border_kernel(a, sides, from_west, from_east, out):
    c = lax.axis_index("gy")
    position = lax.rem(c, 4)

    def fill(j, side):
        for k, (u, d) in enumerate(FAR):
            arrived = from_west if d == 0 else from_east
            tiles = [arrived[4], arrived[0]] if j == 0 else [arrived[3], arrived[5]]
            product = dot(a[u, j, LINK_TILE[d]], cat(tiles, 1)).astype(BF16)
            result = dot_t(sides[u, side], product).astype(BF16)
            for s in range(2):
                out[2 * k + s] = result[:, s * B:(s + 1) * B]

    pl.when(jnp.logical_and(position == 0, c > 0))(lambda: fill(0, 0))
    pl.when(jnp.logical_and(position == 3, c < lax.axis_size("gy") - 1))(lambda: fill(3, 1))


def far_kernel(own, a, sides, from_west, from_east, chosen, row, for_e, for_o):
    del chosen
    even = lax.rem(lax.axis_index("gy"), 2) == 0
    for k, (u, d) in enumerate(FAR):
        arrived = from_west if d == 0 else from_east
        first, middle, last = link_products(a, u, d, [arrived[j] for j in range(4)], [arrived[4], arrived[5]])
        slots = reduce_units(own, u, (first, middle, last), 1)
        down = dot_t(sides[u, 0], cat([first, middle[0]], 1))
        up = dot_t(sides[u, 1], cat([middle[3], last], 1))
        to_e, to_o = jnp.where(even, up, down), jnp.where(even, down, up)
        for t in range(3):
            row[k, t] = slots[t][0]
        for s in range(2):
            at = slice(s * B, (s + 1) * B)
            for_e[k, s] = to_e[:, at]
            for_o[2 * k + s] = to_o[:, at].astype(BF16)


def merge_kernel(row, for_e, for_o, from_group, chosen, row_out, message):
    core = lax.rem(lax.axis_index("gy"), 2)
    for k in range(len(FAR)):
        for t in range(3):
            row_out[k, t] = row[k, t]
        for s in range(2):
            row_out[k, core + s] += from_group[2 * k + s].astype(F32)
            message[tile(7 * k + 3 + s)] = for_e[k, s].astype(BF16)
            message[tile(7 * k + 5 + s)] = for_o[2 * k + s]
        for t in range(3):
            message[tile(7 * k + t)] = row_out[k, t].astype(BF16)


def far_tiles(core, half, row, for_e, message, k, t):
    def theirs_at(i):
        return message[1 - core, tile(7 * k + i)].astype(F32)

    def slot(get, shift):
        if t == 1:
            return get(1 - shift)
        return jnp.where(shift == t // 2, get(t // 2), 0.0)

    mine = row[k, t] + slot(lambda s: theirs_at(3 + s), 1 - core)
    theirs = theirs_at(t) + slot(lambda s: for_e[k, s], core)
    inner = slot(lambda s: message[1 - half, tile(7 * k + 5 + s)].astype(F32), half)
    return mine, theirs, inner


def complete(core, row, for_e, message, joint, k, t):
    def to_mine(s):
        value = message[tile(5 * k + 3 + s)].astype(F32)
        return value + joint[k // 2, 0, s] if k % 2 else value

    def to_theirs(s):
        return for_e[k, s] + joint[k // 2, 1, s] if k % 2 else for_e[k, s]

    mine = row[k, t]
    theirs = message[tile(5 * k + t)].astype(F32)
    if t == 1:
        return mine + to_mine(core), theirs + to_theirs(1 - core)
    gets = (core == 0) == (t == 2)
    s = 1 if t == 2 else 0
    return mine + jnp.where(gets, to_mine(s), 0.0), theirs + jnp.where(gets, 0.0, to_theirs(s))


def masks(codes, u, position, core):
    code = codes[u * PAD // 2:u * PAD // 2 + 1]
    other = position + 1 - 2 * core
    return (jnp.broadcast_to(code == position.astype(F32), (B, B)),
            jnp.broadcast_to(code == other.astype(F32), (B, B)))


def choose_near_kernel(mine, row, for_e, message, sent, halo_o, border, out, wanted, joint):
    del border
    c = lax.axis_index("gy")
    core, position = lax.rem(c, 2), lax.rem(c, 4)
    outer = jnp.logical_or(position == 0, position == 3)
    inferred = 6.0 - mine[...] - message[pl.ds(28 * B + PAD, PAD)].astype(F32)
    inferred = inferred - halo_o[pl.ds(14 * B, PAD)].astype(F32)
    codes = jnp.where(outer, message[pl.ds(28 * B, PAD)].astype(F32), inferred)
    wanted[...] = codes
    for u in range(2):
        def part(ref, i):
            return ref[tile(20 + 4 * u + i)]

        ours, got = cat([part(sent, 0), part(sent, 1)], 1), cat([part(message, 0), part(message, 1)], 1)
        to_mine = dot(cat([part(sent, 2), part(message, 3)], 1), cat([got, ours], 0))
        to_theirs = dot(cat([part(message, 2), part(sent, 3)], 1), cat([ours, got], 0))
        for s in range(2):
            joint[u, 0, s] = to_mine[:, s * B:(s + 1) * B]
            joint[u, 1, s] = to_theirs[:, s * B:(s + 1) * B]
    for k, (u, _) in enumerate(NEAR):
        use_mine, use_theirs = masks(codes, u, position, core)
        for t in range(3):
            own_row, other_row = complete(core, row, for_e, message, joint, k, t)
            out[3 * k + t] = jnp.where(use_mine, own_row, jnp.where(use_theirs, other_row, 0.0)).astype(BF16)


def choose_far_kernel(wanted, row, for_e, message, out):
    c = lax.axis_index("gy")
    core, position = lax.rem(c, 2), lax.rem(c, 4)
    for k, (u, _) in enumerate(FAR):
        use_mine, use_theirs = masks(wanted[...], u, position, core)
        for t in range(3):
            mine, theirs, inner = far_tiles(core, position // 2, row, for_e, message, k, t)
            out[3 * k + t] = jnp.where(use_mine, mine, jnp.where(use_theirs, theirs, inner)).astype(BF16)


def finish_near_kernel(mine, row, for_e, message, joint, arrived, row_far, for_e_far, message_far,
                       out, base, buffer, sems):
    c = lax.axis_index("gy")
    core, position = lax.rem(c, 2), lax.rem(c, 4)
    half = position // 2
    copies = []
    for k, (u, d) in enumerate(NEAR):
        use_mine, use_theirs = masks(mine[...], u, position, core)
        for t in range(3):
            own_row, other_row = complete(core, row, for_e, message, joint, k, t)
            got = arrived[3 * k + t].astype(F32)
            buffer[k, t] = jnp.where(use_mine, own_row, jnp.where(use_theirs, other_row, got))
        copies.append(pltpu.make_async_copy(buffer.at[k], out.at[u, 0, d], sems.at[k]))
        copies[-1].start()
    for k, (u, _) in enumerate(FAR):
        use_mine, use_theirs = masks(mine[...], u, position, core)
        code = mine[u * PAD // 2:u * PAD // 2 + 1]
        add_inner = jnp.broadcast_to(code == (2 - half).astype(F32), (B, B))
        for t in range(3):
            own_row, other_row, inner = far_tiles(core, half, row_far, for_e_far, message_far, k, t)
            there = jnp.where(add_inner, inner, 0.0)
            base[k, t] = jnp.where(use_mine, own_row, jnp.where(use_theirs, other_row, there))
    for copy in copies:
        copy.wait()


def finish_far_kernel(mine, base, arrived, started, out, buffer, sems):
    del started
    outer = 3 * (lax.rem(lax.axis_index("gy"), 4) // 2)
    copies = []
    for k, (u, d) in enumerate(FAR):
        code = mine[u * PAD // 2:u * PAD // 2 + 1]
        add = jnp.broadcast_to(code != outer.astype(F32), (B, B))
        for t in range(3):
            buffer[k, t] = base[k, t] + jnp.where(add, arrived[3 * k + t].astype(F32), 0.0)
        copies.append(pltpu.make_async_copy(buffer.at[k], out.at[u, 0, d], sems.at[k]))
        copies[-1].start()
    for copy in copies:
        copy.wait()


def on_device(a_tiles, a_links, p_own, p_side, p_links, coarse_pick):
    count, columns = lax.axis_size("gy"), lax.axis_size("gx")
    pairs = [(2 * g, 2 * g + 1) for g in range(count // 2)]
    cores = [list(pair) for pair in pairs]
    inside = pairs + [(b, a) for a, b in pairs]
    outside = [(i + 1, i + 2) for i in range(0, count - 2, 2)]
    outside = outside + [(b, a) for a, b in outside]
    between = [(i, i + 1) for i in range(3, count - 1, 4)]
    between = between + [(b, a) for a, b in between]
    across = [(i, i ^ 2) for i in range(count)]
    eastward = [(i, i + 1) for i in range(columns - 1)]
    westward = [(b, a) for a, b in eastward]
    bb = (B, B)
    near, far = len(NEAR), len(FAR)

    own, a, sides, east, west, msg_o, mine = call(
        begin_kernel,
        [pltpu.with_memory_space_constraint(x, pltpu.HBM)
         for x in (a_links, p_links, coarse_pick.T, p_own, p_side, a_tiles)],
        [(p_own.shape, BF16), (a_tiles.shape, BF16), ((2, 2) + bb, BF16), ((6,) + bb, BF16), ((6,) + bb, BF16),
         ((14 * B + PAD, B), BF16), ((PAD, B), F32)],
        in_specs=[HBM] * 6,
        scratch=[pltpu.SMEM(a_links.shape, jnp.int32), pltpu.SMEM(p_links.shape, jnp.int32),
                 pltpu.SMEM((1, 2), jnp.int32), pltpu.VMEM(p_side.shape, BF16), pltpu.SemaphoreType.DMA((6,))])
    halo_o = lax.ppermute(msg_o, "gy", outside)
    from_west = lax.ppermute(east, "gx", eastward)
    from_east = lax.ppermute(west, "gx", westward)
    row_n, for_e_n, message_n = call(
        near_kernel, (own, a, sides, halo_o, mine),
        [((near, 3) + bb, F32), ((near, 2) + bb, F32), ((28 * B + 2 * PAD, B), BF16)])
    sent_n = message_n
    message_n = lax.ppermute(message_n, "gy", inside)
    (for_group,) = call(
        border_kernel, (a, sides, from_west, from_east), [((2 * far,) + bb, BF16)], cost=20000000000)
    from_group = lax.ppermute(for_group, "gy", between)
    chosen_n, wanted, joint = call(
        choose_near_kernel, (mine, row_n, for_e_n, message_n, sent_n, halo_o, for_group),
        [((3 * near,) + bb, BF16), ((PAD, B), F32), ((2, 2, 2) + bb, F32)])
    arrived_n = lax.ppermute(chosen_n, "gy", across)
    row_f, for_e_f, for_o_f = call(
        far_kernel, (own, a, sides, from_west, from_east, chosen_n),
        [((far, 3) + bb, F32), ((far, 2) + bb, F32), ((2 * far,) + bb, BF16)], cost=0)
    row_f, message_f = call(
        merge_kernel, (row_f, for_e_f, for_o_f, from_group, chosen_n), [((far, 3) + bb, F32), ((7 * far * B, B), BF16)])
    message_f = lax.all_gather(message_f, "gy", axis_index_groups=cores)
    (chosen_f,) = call(choose_far_kernel, (wanted, row_f, for_e_f, message_f), [((3 * far,) + bb, BF16)])
    arrived_f = lax.ppermute(chosen_f, "gy", across)
    shape = (2, 1, 3, 3) + bb
    out, base = call(
        finish_near_kernel,
        (mine, row_n, for_e_n, message_n, joint, arrived_n, row_f, for_e_f, message_f),
        [(shape, F32), ((far, 3) + bb, F32)], out_specs=[HBM, VMEM],
        scratch=[pltpu.VMEM((near, 3) + bb, F32), pltpu.SemaphoreType.DMA((near,))])
    (out,) = call(
        finish_far_kernel, (mine, base, arrived_f, out), [(shape, F32)],
        in_specs=[VMEM] * 3 + [HBM], out_specs=[HBM], aliases={3: 0},
        scratch=[pltpu.VMEM((far, 3) + bb, F32), pltpu.SemaphoreType.DMA((far,))])
    return out


def solution(mesh):
    return jax.shard_map(
        on_device,
        mesh=mesh,
        in_specs=(
            P("gx", "gy", None, None, None),
            P("gx", "gy", None),
            P("gx", "gy", None, None),
            P("gx", "gy", None, None, None),
            P("gx", "gy", None),
            P("gx", "gy"),
        ),
        out_specs=P("gx", "gy", None, None, None, None),
        check_vma=False,
    )
```
